512 devices in a mesh: seq: 32 (over x, z_lo, core), head: 16 (over y, z_hi).
Axes of the slice: x: 4, y: 4, z: 16 (z_hi: 4, z_lo: 4; z = z_hi * 4 + z_lo), core: 2. Of those that a mesh axis runs over, the one named last changes fastest.
Arguments:
- out_grad: bfloat16 [8192, 4096], P('seq', 'head'), may hold values from -7.2 to 7.2
- x_in: bfloat16 [8192, 4096], P('seq', 'head'), may hold values from -6 to 6
- b_in: bfloat16 [8192, 128], P('seq'), may hold values from -2.5 to 2.5
- c_in: bfloat16 [8192, 128], P('seq'), may hold values from -2.5 to 2.5
- dt_raw: float32 [64, 8192], P('head', 'seq'), may hold values from -5.1 to -0.7
- dt_bias: float32 [64], P('head'), may hold values from -0.5 to 0.5
- a_log: float32 [64], P('head'), may hold values from -7.5 to 2.2
- d_skip: float32 [64], P('head'), may hold values from 0.5 to 1.5
- states: bfloat16 [32, 4096, 128], P('seq', 'head'), may hold values from -6 to 6
- w_out: bfloat16 [4096, 4096], P('head'), may hold values from -0.09375 to 0.09375
- w_in: bfloat16 [4096, 4096], P(None, 'head'), may hold values from -0.125 to 0.125
Outputs:
- in_grad: bfloat16 [4096, 8192], P('head', 'seq')
- bc_grad: bfloat16 [256, 8192], P('head', 'seq')
- dt_grad: float32 [64, 8192], P('head', 'seq')
- param_grad: float32 [3, 64], P(None, 'head')
The draws below stay inside these ranges and needn't reach their ends.
All inputs are finite; a program needn't handle non-finite values.
Results may differ from the reference program's by a relative error of at most 0.015.
Values may be sent and summed in bfloat16 or wider, within the bound.
No kernel may reach another device: no remote copies, remote signals or barrier semaphores. Data moves between devices by JAX's collectives and lax.ppermute only.
A program may use at most 64 MiB of HBM per device.

```python
import jax
import jax.numpy as jnp
from jax import lax

D = 4096
HEADS = 64
HDIM = 64
STATE = 128
SPAN = 256
TOKENS = 8192
INNER = 4096
GROUP_HEADS = 4
N_HEAD = 16


def draw_out_grad(key, part):
    position = jnp.arange(TOKENS, dtype=jnp.float32) / max(TOKENS - 1, 1)
    base_draw = jnp.clip(jax.random.normal(key, (TOKENS, D), jnp.float32), -4.0, 4.0)
    growth = 0.6 * 3.0 ** position
    return (base_draw * growth[:, None]).astype(jnp.bfloat16)


def draw_a_log(key, part):
    key_order, key_slow, key_fast = jax.random.split(jax.random.fold_in(key, 11), 3)
    ranking = jax.random.permutation(key_order, HEADS)
    slow_head = ranking < HEADS // 2
    slow_rate = jax.random.uniform(key_slow, (HEADS,), jnp.float32, 0.3, 1.5) / (TOKENS * 0.06)
    fast_rate = jax.random.uniform(key_fast, (HEADS,), jnp.float32, 0.7, 1.4) * 6.0 / (SPAN * 0.06)
    return jnp.log(jnp.where(slow_head, slow_rate, fast_rate))


def draw_dt_raw(key, part):
    key_jitter, key_block = jax.random.split(jax.random.fold_in(key, 23))
    blocks = TOKENS // SPAN
    offset = jax.random.uniform(key_block, (HEADS, blocks, 1), jnp.float32, -0.7, 0.7)
    jitter = jnp.clip(0.5 * jax.random.normal(key_jitter, (HEADS, blocks, SPAN), jnp.float32), -1.5, 1.5)
    return (-2.9 + offset + jitter).reshape(HEADS, TOKENS)


def strengthened(values, key, source, target, parts, factor):
    def block_of(axis_at):
        return (jnp.arange(values.shape[axis_at]) // (values.shape[axis_at] // parts)).reshape((-1,) + (1,) * (values.ndim - 1 - axis_at))

    near = jax.random.permutation(key, parts)[block_of(target)]
    second = (block_of(target) + parts // 2) % parts
    return jnp.where((block_of(source) == near) | (block_of(source) == second), factor * values, values)


def steps_of(stream_key, extent, cuts, smallest, largest):
    gain, own = 1.0, jax.random.fold_in(stream_key, 6)
    for dim, shards_of in cuts:
        heights = jnp.exp(jax.random.uniform(jax.random.fold_in(own, dim), (shards_of,), jnp.float32, smallest / len(cuts), largest / len(cuts)))
        gain = gain * jnp.repeat(heights, extent[dim] // shards_of).reshape([-1 if axis == dim else 1 for axis in range(len(extent))])
    return gain


def gaussian(stream_key, extent, width, limit, pieces=(), held_as=jnp.bfloat16):
    array = width * jax.random.normal(stream_key, extent, jnp.float32)
    if pieces:
        array = array * steps_of(stream_key, extent, pieces, -0.22, 0.18)
    return jnp.clip(array, -limit, limit).astype(held_as)


def bell_draw_with(stream_key, dims, spread, most, shards, heavy, kind=jnp.bfloat16):
    entries = spread * jax.random.normal(stream_key, dims, jnp.float32)
    if shards:
        entries = entries * steps_of(stream_key, dims, shards, -0.22, 0.18)
    return jnp.clip(strengthened(entries, jax.random.fold_in(stream_key, 3), *heavy), -most, most).astype(kind)


def setup_inputs(seed: int = 0) -> dict:
    key_list = jax.random.split(jax.random.key(seed), 12)
    out_grad = draw_out_grad(jax.random.fold_in(key_list[11], 71), 0)
    x_in = gaussian(key_list[1], (TOKENS, INNER), 1.0, 6.0, ((0, 32), (1, 16)))
    b_in = gaussian(key_list[2], (TOKENS, STATE), 0.3, 2.5, ((0, 32),))
    c_in = gaussian(key_list[3], (TOKENS, STATE), 0.3, 2.5, ((0, 32),))
    dt_raw = draw_dt_raw(jax.random.fold_in(key_list[11], 71), 0)
    dt_bias = jnp.clip(jax.random.uniform(key_list[5], (HEADS,), jnp.float32, -0.5, 0.5) * steps_of(key_list[5], (HEADS,), ((0, 16),), -0.4, 0.0), -0.5, 0.5)
    a_log = draw_a_log(jax.random.fold_in(key_list[11], 71), 0)
    d_skip = jnp.clip(0.5 + 1.0 * jax.random.uniform(key_list[7], (HEADS,), jnp.float32) ** steps_of(key_list[7], (HEADS,), ((0, 16),), -0.2, 0.2), 0.5, 1.5)
    states = gaussian(key_list[8], (TOKENS // SPAN, INNER, STATE), 1.0, 6.0, ((0, 32), (1, 16)))
    w_out = gaussian(key_list[9], (INNER, D), INNER ** -0.5, 0.09375, ((0, 16),))
    w_in = bell_draw_with(key_list[10], (D, INNER), D ** -0.5, 0.125, ((1, 16),), (1, 0, 16, 2.0))
    return dict(out_grad=out_grad, x_in=x_in, b_in=b_in, c_in=c_in, dt_raw=dt_raw, dt_bias=dt_bias, a_log=a_log, d_skip=d_skip, states=states, w_out=w_out, w_in=w_in)


def rounded(values):
    return lax.optimization_barrier(values.astype(jnp.bfloat16)).astype(jnp.float32)


def reference(out_grad, x_in, b_in, c_in, dt_raw, dt_bias, a_log, d_skip, states, w_out, w_in):
    blocks = TOKENS // SPAN
    head_grad = jnp.dot(out_grad, w_out.T, preferred_element_type=jnp.float32).astype(jnp.bfloat16)
    decay_rate = jnp.exp(a_log)
    step_size = jax.nn.softplus(dt_raw + dt_bias[:, None])
    x_blocks = x_in.astype(jnp.float32).reshape(blocks, SPAN, HEADS, HDIM)
    dy_blocks = head_grad.astype(jnp.float32).reshape(blocks, SPAN, HEADS, HDIM)
    b_blocks = b_in.reshape(blocks, SPAN, STATE)
    c_blocks = c_in.reshape(blocks, SPAN, STATE)
    step_blocks = step_size.reshape(HEADS, blocks, SPAN).transpose(1, 0, 2)
    raw_blocks = dt_raw.reshape(HEADS, blocks, SPAN).transpose(1, 0, 2)
    entry_blocks = states.astype(jnp.float32).reshape(blocks, HEADS, HDIM, STATE)
    causal = jnp.arange(SPAN)[:, None] >= jnp.arange(SPAN)[None, :]

    def front(items):
        dy_heads, c_block, step_block = items
        cumlog = jnp.cumsum(-decay_rate[:, None] * step_block, axis=1)
        dy_decay = rounded(dy_heads * jnp.exp(cumlog).T[:, :, None])
        local_state = jnp.einsum('ihp,in->hpn', dy_decay, c_block.astype(jnp.float32))
        return local_state, jnp.exp(cumlog[:, -1])

    local_states, end_totals = lax.map(front, (dy_blocks, c_blocks, step_blocks))

    def carry_step(held_state, items):
        local_state, end_total = items
        return end_total[:, None, None] * held_state + local_state, held_state

    final_state, carried = lax.scan(carry_step, jnp.zeros((HEADS, HDIM, STATE), jnp.float32), (local_states, end_totals), reverse=True)

    def back(items):
        x_heads, dy_heads, b_block, c_block, step_block, raw_block, entry_state, held_state = items
        b_wide = b_block.astype(jnp.float32)
        c_wide = c_block.astype(jnp.float32)
        log_step = -decay_rate[:, None] * step_block
        cumlog = jnp.cumsum(log_step, axis=1)
        log_gaps = cumlog[:, :, None] - cumlog[:, None, :]
        decay_mask = jnp.where(causal[None], jnp.exp(jnp.minimum(log_gaps, 0.0)), 0.0)
        scores = jnp.dot(c_block, b_block.T, preferred_element_type=jnp.float32)
        step_rows = step_block.T
        x_scaled = rounded(x_heads * step_rows[:, :, None])
        pair_dots = jnp.einsum('ihp,jhp->hij', dy_heads, x_scaled)
        kernel = rounded(scores[None] * decay_mask)
        intra_back = jnp.einsum('hij,ihp->jhp', kernel, dy_heads)
        masked_dots = rounded(pair_dots * decay_mask)
        start_decay = jnp.exp(cumlog)
        dy_decay = rounded(dy_heads * start_decay.T[:, :, None])
        carried_bf = rounded(held_state)
        state_back = jnp.einsum('jn,hpn->jhp', b_wide, carried_bf)
        end_decay = jnp.exp(cumlog[:, -1:] - cumlog)
        end_weight = (step_block * end_decay).T
        x_grad = (step_rows[:, :, None] * intra_back + end_weight[:, :, None] * state_back + d_skip[None, :, None] * dy_heads).astype(jnp.bfloat16)
        x_end = rounded(x_heads * end_weight[:, :, None])
        db_heads = jnp.einsum('hij,in->hjn', masked_dots, c_wide) + jnp.einsum('jhp,hpn->hjn', x_end, carried_bf)
        dc_heads = jnp.einsum('hij,jn->hin', masked_dots, b_wide) + jnp.einsum('ihp,hpn->hin', dy_decay, entry_state)
        db_groups = rounded(db_heads.reshape(N_HEAD, GROUP_HEADS, SPAN, STATE).sum(axis=1)).sum(axis=0)
        dc_groups = rounded(dc_heads.reshape(N_HEAD, GROUP_HEADS, SPAN, STATE).sum(axis=1)).sum(axis=0)
        bc_block = jnp.concatenate([db_groups.T, dc_groups.T], axis=0)
        ystate = jnp.einsum('in,hpn->ihp', c_wide, entry_state)
        pair_weight = pair_dots * scores[None] * decay_mask
        state_terms = start_decay * jnp.sum(dy_heads * ystate, axis=2).T
        end_terms = end_weight.T * jnp.sum(x_heads * state_back, axis=2).T
        cum_grad = pair_weight.sum(axis=2) - pair_weight.sum(axis=1) + state_terms - end_terms
        tail_grad = end_terms.sum(axis=1) + jnp.exp(cumlog[:, -1]) * jnp.sum(entry_state * held_state, axis=(1, 2))
        cum_grad = cum_grad.at[:, -1].add(tail_grad)
        step_grad = jnp.cumsum(cum_grad[:, ::-1], axis=1)[:, ::-1]
        dt_sum = -decay_rate[:, None] * step_grad + jnp.sum(x_heads * (intra_back + end_decay.T[:, :, None] * state_back), axis=2).T
        dt_grad = dt_sum * jax.nn.sigmoid(raw_block + dt_bias[:, None])
        param_terms = jnp.stack([jnp.sum(step_grad * log_step, axis=1), jnp.sum(dy_heads * x_heads, axis=(0, 2)), jnp.sum(dt_grad, axis=1)])
        return x_grad, bc_block, dt_grad, param_terms

    x_grads, bc_blocks, dt_blocks, param_blocks = lax.map(back, (x_blocks, dy_blocks, b_blocks, c_blocks, step_blocks, raw_blocks, entry_blocks, carried))
    x_grad = x_grads.reshape(TOKENS, HEADS * HDIM)
    bc_grad = bc_blocks.transpose(1, 0, 2).reshape(2 * STATE, TOKENS).astype(jnp.bfloat16)
    dt_grad = dt_blocks.transpose(1, 0, 2).reshape(HEADS, TOKENS)
    param_grad = param_blocks.sum(axis=0) * (TOKENS * HDIM) ** -0.5
    group_width = GROUP_HEADS * HDIM
    running = jnp.zeros((D, TOKENS), jnp.float32)
    for group_index in range(N_HEAD):
        w_cols = w_in[:, group_index * group_width:(group_index + 1) * group_width]
        x_cols = x_grad[:, group_index * group_width:(group_index + 1) * group_width]
        running = running + rounded(jnp.dot(w_cols, x_cols.T, preferred_element_type=jnp.float32))
    return running.astype(jnp.bfloat16), bc_grad, dt_grad, param_grad
```

```python
import jax
import jax.numpy as jnp
from jax import lax
from jax.experimental import pallas as pl
from jax.experimental.pallas import tpu as pltpu
from jax.sharding import Mesh, PartitionSpec as P

SEQ = ("x", "zl", "core")
HEAD = ("y", "zh")
f32, bf16 = jnp.float32, jnp.bfloat16


def scan_kernel(parts_ref, carried_ref):
    blocks = parts_ref.shape[0]
    held = jnp.zeros(carried_ref.shape[1:], f32)
    for k in range(blocks - 1, -1, -1):
        carried_ref[k] = held
        wide = parts_ref[k].astype(f32)
        total = wide[8:9] + wide[9:10] + wide[10:11]
        held = total * held + wide[:8]


def suffix_scan(parts):
    blocks, _, width = parts.shape
    return pl.pallas_call(
        scan_kernel,
        out_shape=jax.ShapeDtypeStruct((blocks, 8, width), f32),
        cost_estimate=pl.CostEstimate(flops=blocks * 3072, bytes_accessed=blocks * 8192, transcendentals=0),
    )(parts)


def three_parts(values):
    first = values.astype(bf16).astype(f32)
    second = (values - first).astype(bf16).astype(f32)
    return jnp.stack([first, second, values - first - second], axis=-1)


def shards(out_grad, x_in, b_in, c_in, dt_raw, dt_bias, a_log, d_skip, states, w_out, w_in):
    tokens_here, inner_here = x_in.shape
    group_heads = dt_raw.shape[0]
    head_dim = inner_here // group_heads
    state_dim = b_in.shape[1]
    blocks = lax.axis_size(SEQ)
    contract_last = (((1,), (1,)), ((), ()))
    near = lax.all_gather(out_grad, "zh", axis=1, tiled=True)
    whole = lax.all_to_all(jnp.broadcast_to(near[None], (4,) + near.shape), "y", 0, 0)
    head_sum = jnp.zeros((tokens_here, inner_here), f32)
    for y in range(4):
        head_sum = head_sum + lax.dot_general(
            whole[y], w_out[:, y * near.shape[1]:(y + 1) * near.shape[1]], contract_last, preferred_element_type=f32
        )
    dy_heads = head_sum.astype(bf16).reshape(tokens_here, group_heads, head_dim)
    dy_wide = dy_heads.astype(f32)
    x_heads = x_in.reshape(tokens_here, group_heads, head_dim)
    x_wide = x_heads.astype(f32)
    decay_rate = jnp.exp(a_log)
    step_size = jax.nn.softplus(dt_raw + dt_bias[:, None])
    log_step = -decay_rate[:, None] * step_size
    positions = jnp.arange(tokens_here)
    causal = positions[:, None] >= positions[None, :]
    triangle = causal.astype(f32)
    cumlog = jnp.dot(log_step, triangle.T, precision=lax.Precision.HIGHEST)
    log_gaps = cumlog[:, :, None] - cumlog[:, None, :]
    decay_mask = jnp.where(causal[None], jnp.exp(jnp.minimum(log_gaps, 0.0)), 0.0)
    scores = lax.dot_general(c_in, b_in, contract_last, preferred_element_type=f32)
    step_rows = step_size.T
    x_scaled = (x_wide * step_rows[:, :, None]).astype(bf16)
    start_decay = jnp.exp(cumlog)
    dy_decay = (dy_wide * start_decay.T[:, :, None]).astype(bf16)
    local_state = jnp.einsum("ihp,in->hpn", dy_decay, c_in, preferred_element_type=f32)
    end_total = jnp.exp(cumlog[:, -1])
    ends = jnp.pad(three_parts(end_total), ((0, 0), (0, 5)))
    ends = jnp.broadcast_to(ends[:, None, :, None], (group_heads, blocks // group_heads, 8, state_dim))
    sent = jnp.concatenate([local_state.reshape(blocks, 8, state_dim), ends.reshape(blocks, 8, state_dim)], axis=1)
    got = lax.all_to_all(sent.astype(bf16), SEQ, 0, 0)
    carried = lax.all_to_all(suffix_scan(got), SEQ, 0, 0).reshape(group_heads, head_dim, state_dim)

    pair_dots = jnp.einsum("ihp,jhp->hij", dy_heads, x_scaled, preferred_element_type=f32)
    kernel = (scores[None] * decay_mask).astype(bf16)
    intra_back = jnp.einsum("hij,ihp->jhp", kernel, dy_heads, preferred_element_type=f32)
    masked_dots = (pair_dots * decay_mask).astype(bf16)
    entry_state = states.reshape(group_heads, head_dim, state_dim)
    db_intra = jnp.einsum("hij,in->nj", masked_dots, c_in, preferred_element_type=f32)
    dc_intra = jnp.einsum("hij,jn->ni", masked_dots, b_in, preferred_element_type=f32)
    dc_entry = jnp.einsum("ihp,hpn->ni", dy_decay, entry_state, preferred_element_type=f32)
    ystate = jnp.einsum("in,hpn->ihp", c_in, entry_state, preferred_element_type=f32)
    pair_weight = pair_dots * scores[None] * decay_mask
    state_terms = start_decay * jnp.sum(dy_wide * ystate, axis=2).T
    skip_terms = jnp.sum(dy_wide * x_wide, axis=(0, 2))

    carried_bf = carried.astype(bf16)
    state_back = jnp.einsum("jn,hpn->jhp", b_in, carried_bf, preferred_element_type=f32)
    end_decay = jnp.exp(cumlog[:, -1:] - cumlog)
    end_weight = (step_size * end_decay).T
    x_grad = (
        (
            step_rows[:, :, None] * intra_back
            + end_weight[:, :, None] * state_back
            + d_skip[None, :, None] * dy_wide
        )
        .astype(bf16)
        .reshape(tokens_here, inner_here)
    )
    x_end = (x_wide * end_weight[:, :, None]).astype(bf16)
    db_entry = jnp.einsum("jhp,hpn->nj", x_end, carried_bf, preferred_element_type=f32)
    bc_part = jnp.concatenate([db_intra + db_entry, dc_intra + dc_entry], axis=0).astype(bf16)
    in_part = lax.dot_general(w_in, x_grad, contract_last, preferred_element_type=f32).astype(bf16)
    terms = jnp.concatenate(
        [in_part.reshape(4, 4, -1, tokens_here), bc_part.reshape(4, 4, -1, tokens_here)], axis=2
    )
    half = lax.all_to_all(terms, "y", 0, 0).astype(f32).sum(axis=0).astype(bf16)
    both = lax.all_to_all(half, "zh", 0, 0).astype(f32).sum(axis=0).astype(bf16)
    in_rows = in_part.shape[0] // 16

    end_terms = end_weight.T * jnp.sum(x_wide * state_back, axis=2).T
    cum_grad = pair_weight.sum(axis=2) - pair_weight.sum(axis=1) + state_terms - end_terms
    tail_grad = end_terms.sum(axis=1) + end_total * jnp.sum(entry_state.astype(f32) * carried, axis=(1, 2))
    step_grad = jnp.dot(cum_grad, triangle, precision=lax.Precision.HIGHEST) + tail_grad[:, None]
    dt_sum = (
        -decay_rate[:, None] * step_grad
        + jnp.sum(x_wide * (intra_back + end_decay.T[:, :, None] * state_back), axis=2).T
    )
    dt_grad = dt_sum * jax.nn.sigmoid(dt_raw + dt_bias[:, None])
    param_terms = jnp.stack([jnp.sum(step_grad * log_step, axis=1), skip_terms, jnp.sum(dt_grad, axis=1)])
    flat = jnp.pad(param_terms.reshape(1, -1), ((0, 0), (0, 128 - param_terms.size)))
    spread = lax.all_to_all(jnp.broadcast_to(flat[None], (blocks, 1, 128)), SEQ, 0, 0)
    norm_scale = (blocks * tokens_here * head_dim) ** (-0.5)
    param_grad = spread.sum(axis=0)[0, : param_terms.size].reshape(param_terms.shape) * norm_scale
    return (both[:in_rows], both[in_rows:], dt_grad, param_grad)


def solution(mesh):
    fine = Mesh(mesh.devices.reshape(4, 4, 2, 4, 4), ("x", "zl", "core", "y", "zh"))
    return jax.shard_map(
        shards,
        mesh=fine,
        in_specs=(
            P(SEQ, HEAD),
            P(SEQ, HEAD),
            P(SEQ, None),
            P(SEQ, None),
            P(HEAD, SEQ),
            P(HEAD),
            P(HEAD),
            P(HEAD),
            P(SEQ, HEAD, None),
            P(HEAD, None),
            P(None, HEAD),
        ),
        out_specs=(P(HEAD, SEQ), P(HEAD, SEQ), P(HEAD, SEQ), P(None, HEAD)),
        check_vma=False,
    )
```

```python
import jax
import jax.numpy as jnp
from jax import lax
from jax.experimental import pallas as pl
from jax.experimental.pallas import tpu as pltpu
from jax.sharding import Mesh, PartitionSpec as P

SEQ = ("x", "zl", "core")
HEAD = ("y", "zh")
f32, bf16 = jnp.float32, jnp.bfloat16


def scan_kernel(parts_ref, carried_ref):
    blocks = parts_ref.shape[0]
    held = jnp.zeros(carried_ref.shape[1:], f32)
    for k in range(blocks - 1, -1, -1):
        carried_ref[k] = held
        wide = parts_ref[k].astype(f32)
        total = wide[8:9] + wide[9:10] + wide[10:11]
        held = total * held + wide[:8]


def suffix_scan(parts):
    blocks, _, width = parts.shape
    return pl.pallas_call(
        scan_kernel,
        out_shape=jax.ShapeDtypeStruct((blocks, 8, width), f32),
        compiler_params=small(),
        cost_estimate=cost(blocks * 3072, blocks * 8192),
    )(parts)


def three_parts(values):
    first = values.astype(bf16).astype(f32)
    second = (values - first).astype(bf16).astype(f32)
    return jnp.stack([first, second, values - first - second], axis=-1)


def cost(flops, moved):
    return pl.CostEstimate(flops=flops, bytes_accessed=moved, transcendentals=0)


def small():
    return pltpu.CompilerParams(vmem_limit_bytes=16 << 20)


def dot_last(a, b):
    return lax.dot_general(a, b, (((1,), (1,)), ((), ())), preferred_element_type=f32)


def regroup_kernel(w_ref, out_ref):
    out_ref[0] = w_ref[...]


def regrouped(w):
    rows, width = w.shape
    part = width // 4
    return pl.pallas_call(
        regroup_kernel,
        grid=(4,),
        in_specs=[pl.BlockSpec((rows, part), lambda g: (0, g))],
        out_specs=pl.BlockSpec((1, rows, part), lambda g: (g, 0, 0)),
        out_shape=jax.ShapeDtypeStruct((4, rows, part), w.dtype),
        cost_estimate=cost(0, 4 * rows * width),
    )(w)


def partial_kernel(near_ref, w_ref, out_ref):
    out_ref[0] = dot_last(near_ref[...], w_ref[0]).astype(bf16)


def partial_products(near, w_mine):
    groups, inner, depth = w_mine.shape
    tokens = near.shape[0]
    return pl.pallas_call(
        partial_kernel,
        grid=(groups,),
        in_specs=[
            pl.BlockSpec((tokens, depth), lambda g: (0, 0)),
            pl.BlockSpec((1, inner, depth), lambda g: (g, 0, 0)),
        ],
        out_specs=pl.BlockSpec((1, tokens, inner), lambda g: (g, 0, 0)),
        out_shape=jax.ShapeDtypeStruct((groups, tokens, inner), bf16),
        compiler_params=small(),
        cost_estimate=cost(2 * groups * tokens * inner * depth, 4 << 20),
    )(near, w_mine)


def state_kernel(parts_ref, start_ref, c_ref, ends_ref, dy_ref, decayed_ref, sent_ref):
    total = parts_ref[0].astype(f32)
    for y in range(1, parts_ref.shape[0]):
        total = total + parts_ref[y].astype(f32)
    dy = total.astype(bf16)
    dy_ref[...] = dy
    decayed = (dy.astype(f32) * start_ref[...]).astype(bf16)
    decayed_ref[...] = decayed
    state = lax.dot_general(decayed, c_ref[...], (((0,), (0,)), ((), ())), preferred_element_type=f32)
    blocks, rows, width = ends_ref.shape
    state = state.reshape(blocks, rows, width)
    sent_ref[...] = jnp.concatenate([state, ends_ref[...]], axis=1).astype(bf16)


def local_states(parts, start, c_in, ends):
    _, tokens, inner = parts.shape
    blocks, rows, width = ends.shape
    wide = jax.ShapeDtypeStruct((tokens, inner), bf16)
    return pl.pallas_call(
        state_kernel,
        out_shape=(wide, wide, jax.ShapeDtypeStruct((blocks, 2 * rows, width), bf16)),
        compiler_params=small(),
        cost_estimate=cost(2 * tokens * inner * width, 2 << 20),
    )(parts, start, c_in, ends)


def x_grad_kernel(carried_ref, b_ref, base_ref, weight_ref, x_end_ref, bc_ref, sent_ref, back_ref):
    blocks, rows, width = carried_ref.shape
    carried = carried_ref[...].reshape(blocks * rows, width).astype(bf16)
    back = dot_last(b_ref[...], carried)
    back_ref[...] = back
    x_grad = (base_ref[...] + weight_ref[...] * back).astype(bf16)
    entry = jnp.dot(x_end_ref[...], carried, preferred_element_type=f32)
    tokens = entry.shape[0]
    rows = bc_ref.shape[0] // 4
    db = (bc_ref[:width] + entry.T).astype(bf16)
    dc = bc_ref[width:].astype(bf16)
    for y in range(4):
        sent_ref[y, :tokens] = x_grad
        half = db if y < 2 else dc
        sent_ref[y, tokens:] = half[(y % 2) * rows:(y % 2 + 1) * rows]


def x_grads(carried, b_in, base, weight, x_end, bc_base):
    tokens, inner = base.shape
    rows = bc_base.shape[0] // 4
    return pl.pallas_call(
        x_grad_kernel,
        out_shape=(
            jax.ShapeDtypeStruct((4, tokens + rows, inner), bf16),
            jax.ShapeDtypeStruct((tokens, inner), f32),
        ),
        compiler_params=small(),
        cost_estimate=cost(4 * tokens * inner * 128, 2 << 20),
    )(carried, b_in, base, weight, x_end, bc_base)


def in_kernel(y_ref, got_ref, own_ref, *refs):
    *held_refs, out_ref = refs
    tokens = got_ref.shape[2]
    feats = own_ref.shape[0]
    y = y_ref[0]
    total = dot_last(own_ref[...], got_ref[y, :tokens])
    for s, w_ref in enumerate(held_refs):
        total = total + dot_last(w_ref[...], got_ref[lax.rem(y + 3 - s, 4), :tokens])
    out_ref[0, :feats] = total.astype(bf16)
    rows = out_ref.shape[1] - feats
    at = pl.ds(pl.multiple_of(tokens + pl.program_id(0) * rows, rows), rows)
    bc = got_ref[0, at].astype(f32)
    for other in range(1, 4):
        bc = bc + got_ref[other, at].astype(f32)
    out_ref[0, feats:] = bc.astype(bf16)


def in_products(y, got, w_in, held):
    features, inner = w_in.shape
    _, height, tokens = got.shape
    feats, rows = features // 16, (height - tokens) // 4
    return pl.pallas_call(
        in_kernel,
        grid_spec=pltpu.PrefetchScalarGridSpec(
            num_scalar_prefetch=1,
            grid=(4,),
            in_specs=[
                pl.BlockSpec(got.shape, lambda z, y: (0, 0, 0)),
                pl.BlockSpec((feats, inner), lambda z, y: (4 * y[0] + z, 0)),
            ]
            + [pl.BlockSpec((feats, inner), lambda z, y: (z, 0))] * 3,
            out_specs=pl.BlockSpec((1, feats + rows, tokens), lambda z, y: (z, 0, 0)),
        ),
        out_shape=jax.ShapeDtypeStruct((4, feats + rows, tokens), bf16),
        compiler_params=small(),
        cost_estimate=cost(8 * features * inner * tokens // 4, 4 << 20),
    )(y.reshape(1), got, w_in, *held)


def sum_kernel(terms_ref, in_ref, bc_ref):
    feats = in_ref.shape[0]
    total = terms_ref[0].astype(f32)
    for z in range(1, 4):
        total = total + terms_ref[z].astype(f32)
    total = total.astype(bf16)
    in_ref[...] = total[:feats]
    bc_ref[...] = total[feats:]


def final_sums(terms, feats):
    _, height, tokens = terms.shape
    return pl.pallas_call(
        sum_kernel,
        out_shape=(
            jax.ShapeDtypeStruct((feats, tokens), bf16),
            jax.ShapeDtypeStruct((height - feats, tokens), bf16),
        ),
        compiler_params=small(),
        cost_estimate=cost(4 * height * tokens, 1 << 20),
    )(terms)


def shards(out_grad, x_in, b_in, c_in, dt_raw, dt_bias, a_log, d_skip, states, w_out, w_in):
    tokens_here, inner_here = x_in.shape
    group_heads = dt_raw.shape[0]
    head_dim = inner_here // group_heads
    state_dim = b_in.shape[1]
    blocks = lax.axis_size(SEQ)
    contract_last = (((1,), (1,)), ((), ()))
    w_out_y = lax.all_to_all(regrouped(w_out), "y", 0, 0)
    near = lax.all_gather(out_grad, "zh", axis=1, tiled=True)
    head_parts = lax.all_to_all(partial_products(near, w_out_y), "y", 0, 0)
    x_heads = x_in.reshape(tokens_here, group_heads, head_dim)
    x_wide = x_heads.astype(f32)
    decay_rate = jnp.exp(a_log)
    step_size = jax.nn.softplus(dt_raw + dt_bias[:, None])
    log_step = -decay_rate[:, None] * step_size
    positions = jnp.arange(tokens_here)
    causal = positions[:, None] >= positions[None, :]
    triangle = causal.astype(f32)
    cumlog = jnp.dot(log_step, triangle.T, precision=lax.Precision.HIGHEST)
    log_gaps = cumlog[:, :, None] - cumlog[:, None, :]
    decay_mask = jnp.where(causal[None], jnp.exp(jnp.minimum(log_gaps, 0.0)), 0.0)
    scores = lax.dot_general(c_in, b_in, contract_last, preferred_element_type=f32)
    step_rows = step_size.T
    x_scaled = (x_wide * step_rows[:, :, None]).astype(bf16)
    start_decay = jnp.exp(cumlog)
    end_total = jnp.exp(cumlog[:, -1])
    ends = jnp.pad(three_parts(end_total), ((0, 0), (0, 5)))
    ends = jnp.broadcast_to(ends[:, None, :, None], (group_heads, blocks // group_heads, 8, state_dim))
    y = lax.axis_index("y")
    w_in_held, head_parts = lax.optimization_barrier((w_in, head_parts))
    quarter = w_in.shape[0] // 4
    held = []
    for s in range(1, 4):
        piece = lax.dynamic_slice_in_dim(w_in_held, lax.rem(y + s, 4) * quarter, quarter)
        held.append(lax.ppermute(piece, "y", [(i, (i + s) % 4) for i in range(4)]))
    start_wide = jnp.repeat(start_decay.T, head_dim, axis=1)
    dy_flat, decayed_flat, sent = local_states(head_parts, start_wide, c_in, ends.reshape(blocks, 8, state_dim))
    dy_heads = dy_flat.reshape(tokens_here, group_heads, head_dim)
    dy_wide = dy_heads.astype(f32)
    dy_decay = decayed_flat.reshape(tokens_here, group_heads, head_dim)
    got = lax.all_to_all(sent, SEQ, 0, 0)
    carried_rows = lax.all_to_all(suffix_scan(got), SEQ, 0, 0)
    carried = carried_rows.reshape(group_heads, head_dim, state_dim)

    pair_dots = jnp.einsum("ihp,jhp->hij", dy_heads, x_scaled, preferred_element_type=f32)
    kernel = (scores[None] * decay_mask).astype(bf16)
    intra_back = jnp.einsum("hij,ihp->jhp", kernel, dy_heads, preferred_element_type=f32)
    masked_dots = (pair_dots * decay_mask).astype(bf16)
    entry_state = states.reshape(group_heads, head_dim, state_dim)
    db_intra = jnp.einsum("hij,in->nj", masked_dots, c_in, preferred_element_type=f32)
    dc_intra = jnp.einsum("hij,jn->ni", masked_dots, b_in, preferred_element_type=f32)
    dc_entry = jnp.einsum("ihp,hpn->ni", dy_decay, entry_state, preferred_element_type=f32)
    ystate = jnp.einsum("in,hpn->ihp", c_in, entry_state, preferred_element_type=f32)
    pair_weight = pair_dots * scores[None] * decay_mask
    state_terms = start_decay * jnp.sum(dy_wide * ystate, axis=2).T
    skip_terms = jnp.sum(dy_wide * x_wide, axis=(0, 2))

    end_decay = jnp.exp(cumlog[:, -1:] - cumlog)
    end_weight = (step_size * end_decay).T
    flat = (tokens_here, inner_here)
    base = (step_rows[:, :, None] * intra_back + d_skip[None, :, None] * dy_wide).reshape(flat)
    weight_wide = jnp.repeat(end_weight, head_dim, axis=1)
    x_end = (x_in.astype(f32) * weight_wide).astype(bf16)
    bc_base = jnp.concatenate([db_intra, dc_intra + dc_entry], axis=0)
    *held, carried_rows = lax.optimization_barrier((*held, carried_rows))
    sent_y, back_flat = x_grads(carried_rows, b_in, base, weight_wide, x_end, bc_base)
    state_back = back_flat.reshape(tokens_here, group_heads, head_dim)
    terms = in_products(y, lax.all_to_all(sent_y, "y", 0, 0), w_in, held)

    end_terms = end_weight.T * jnp.sum(x_wide * state_back, axis=2).T
    cum_grad = pair_weight.sum(axis=2) - pair_weight.sum(axis=1) + state_terms - end_terms
    tail_grad = end_terms.sum(axis=1) + end_total * jnp.sum(entry_state.astype(f32) * carried, axis=(1, 2))
    step_grad = jnp.dot(cum_grad, triangle, precision=lax.Precision.HIGHEST) + tail_grad[:, None]
    dt_sum = (
        -decay_rate[:, None] * step_grad
        + jnp.sum(x_wide * (intra_back + end_decay.T[:, :, None] * state_back), axis=2).T
    )
    dt_grad = dt_sum * jax.nn.sigmoid(dt_raw + dt_bias[:, None])
    param_terms = jnp.stack([jnp.sum(step_grad * log_step, axis=1), skip_terms, jnp.sum(dt_grad, axis=1)])
    row = jnp.pad(param_terms.reshape(1, -1), ((0, 0), (0, 128 - param_terms.size)))
    row, terms = lax.optimization_barrier((row, terms))
    for axis, flip in (("core", 1), ("zl", 1), ("zl", 2), ("x", 1), ("x", 2)):
        row = row + lax.ppermute(row, axis, [(i, i ^ flip) for i in range(lax.axis_size(axis))])
    in_grad, bc_grad = final_sums(lax.all_to_all(terms, "zh", 0, 0), w_in.shape[0] // 16)
    norm_scale = (blocks * tokens_here * head_dim) ** (-0.5)
    param_grad = row[0, : param_terms.size].reshape(param_terms.shape) * norm_scale
    return (in_grad, bc_grad, dt_grad, param_grad)


def solution(mesh):
    fine = Mesh(mesh.devices.reshape(4, 4, 2, 4, 4), ("x", "zl", "core", "y", "zh"))
    return jax.shard_map(
        shards,
        mesh=fine,
        in_specs=(
            P(SEQ, HEAD),
            P(SEQ, HEAD),
            P(SEQ, None),
            P(SEQ, None),
            P(HEAD, SEQ),
            P(HEAD),
            P(HEAD),
            P(HEAD),
            P(SEQ, HEAD, None),
            P(HEAD, None),
            P(None, HEAD),
        ),
        out_specs=(P(HEAD, SEQ), P(HEAD, SEQ), P(HEAD, SEQ), P(None, HEAD)),
        check_vma=False,
    )
```

```python
import jax
import jax.numpy as jnp
from jax import lax
from jax.experimental import pallas as pl
from jax.experimental.pallas import tpu as pltpu
from jax.sharding import Mesh, PartitionSpec as P

SEQ = ("x", "zl", "core")
HEAD = ("y", "zh")
f32, bf16 = jnp.float32, jnp.bfloat16


def scan_kernel(parts_ref, carried_ref):
    blocks = parts_ref.shape[0]
    held = jnp.zeros(carried_ref.shape[1:], f32)
    for k in range(blocks - 1, -1, -1):
        carried_ref[k] = held
        wide = parts_ref[k].astype(f32)
        total = wide[8:9] + wide[9:10] + wide[10:11]
        held = total * held + wide[:8]


def suffix_scan(parts):
    blocks, _, width = parts.shape
    return pl.pallas_call(
        scan_kernel,
        out_shape=jax.ShapeDtypeStruct((blocks, 8, width), f32),
        compiler_params=small(),
        cost_estimate=cost(blocks * 3072, blocks * 8192),
    )(parts)


def three_parts(values):
    first = values.astype(bf16).astype(f32)
    second = (values - first).astype(bf16).astype(f32)
    return jnp.stack([first, second, values - first - second], axis=-1)


def cost(flops, moved):
    return pl.CostEstimate(flops=flops, bytes_accessed=moved, transcendentals=0)


def small():
    return pltpu.CompilerParams(vmem_limit_bytes=16 << 20)


def dot_last(a, b):
    return lax.dot_general(a, b, (((1,), (1,)), ((), ())), preferred_element_type=f32)


def regroup_kernel(w_ref, out_ref, sems):
    part = out_ref.shape[2]
    copies = [
        pltpu.make_async_copy(w_ref.at[:, pl.ds(g * part, part)], out_ref.at[g], sems.at[g]) for g in range(4)
    ]
    for copy in copies:
        copy.start()
    for copy in copies:
        copy.wait()


def regrouped(w):
    rows, width = w.shape
    return pl.pallas_call(
        regroup_kernel,
        in_specs=[pl.BlockSpec(memory_space=pl.ANY)],
        out_specs=pl.BlockSpec(memory_space=pl.ANY),
        out_shape=jax.ShapeDtypeStruct((4, rows, width // 4), w.dtype),
        scratch_shapes=[pltpu.SemaphoreType.DMA((4,))],
        cost_estimate=cost(0, 4 * rows * width),
    )(w)


def partial_kernel(near_ref, w_ref, out_ref):
    out_ref[0] = dot_last(near_ref[...], w_ref[0]).astype(bf16)


def partial_products(near, w_mine):
    groups, inner, depth = w_mine.shape
    tokens = near.shape[0]
    return pl.pallas_call(
        partial_kernel,
        grid=(groups,),
        in_specs=[
            pl.BlockSpec((tokens, depth), lambda g: (0, 0)),
            pl.BlockSpec((1, inner, depth), lambda g: (g, 0, 0)),
        ],
        out_specs=pl.BlockSpec((1, tokens, inner), lambda g: (g, 0, 0)),
        out_shape=jax.ShapeDtypeStruct((groups, tokens, inner), bf16),
        compiler_params=small(),
        cost_estimate=cost(2 * groups * tokens * inner * depth, 4 << 20),
    )(near, w_mine)


def state_kernel(parts_ref, start_ref, c_ref, ends_ref, dy_ref, decayed_ref, sent_ref):
    total = parts_ref[0].astype(f32)
    for y in range(1, parts_ref.shape[0]):
        total = total + parts_ref[y].astype(f32)
    dy = total.astype(bf16)
    dy_ref[...] = dy
    decayed = (dy.astype(f32) * start_ref[...]).astype(bf16)
    decayed_ref[...] = decayed
    state = lax.dot_general(decayed, c_ref[...], (((0,), (0,)), ((), ())), preferred_element_type=f32)
    blocks, rows, width = ends_ref.shape
    state = state.reshape(blocks, rows, width)
    sent_ref[...] = jnp.concatenate([state, ends_ref[...]], axis=1).astype(bf16)


def local_states(parts, start, c_in, ends):
    _, tokens, inner = parts.shape
    blocks, rows, width = ends.shape
    wide = jax.ShapeDtypeStruct((tokens, inner), bf16)
    return pl.pallas_call(
        state_kernel,
        out_shape=(wide, wide, jax.ShapeDtypeStruct((blocks, 2 * rows, width), bf16)),
        compiler_params=small(),
        cost_estimate=cost(2 * tokens * inner * width, 2 << 20),
    )(parts, start, c_in, ends)


def widened(columns, width):
    tokens, heads = columns.shape
    return jnp.concatenate(
        [jnp.broadcast_to(columns[:, h:h + 1], (tokens, width // heads)) for h in range(heads)], axis=1
    )


def head_sums(values, heads):
    width = values.shape[1] // heads
    return [jnp.sum(values[:, h * width:(h + 1) * width], axis=1, keepdims=True) for h in range(heads)]


def as_rows(columns):
    tokens = columns[0].shape[0]
    lanes = lax.broadcasted_iota(jnp.int32, (tokens, 128), 1)
    spread = jnp.zeros((tokens, 128), f32)
    for k, column in enumerate(columns):
        spread = jnp.where(lanes == k, column, spread)
    return spread.T[:8]


def pre_kernel(rows_ref, x_ref, b_ref, c_ref, states_ref, start_ref, step_ref, weight_ref, scaled_ref, end_ref, scores_ref, y_ref):
    tokens, width = x_ref.shape
    rows = rows_ref[...]
    last = rows[:4, tokens - 1:]
    start = jnp.exp(rows[:4])
    weight = rows[4:] * jnp.exp(last - rows[:4])
    columns = jnp.concatenate([start, weight], axis=0).T
    start_ref[...] = widened(columns[:, :4], width)
    weight_wide = widened(columns[:, 4:], width)
    weight_ref[...] = weight_wide
    step_wide = widened(rows.T[:, 4:], width)
    step_ref[...] = step_wide
    x = x_ref[...].astype(f32)
    scaled_ref[...] = (x * step_wide).astype(bf16)
    end_ref[...] = (x * weight_wide).astype(bf16)
    scores_ref[...] = dot_last(c_ref[...], b_ref[...])
    y_ref[...] = dot_last(c_ref[...], states_ref[...])


def prepared(rows, x_in, b_in, c_in, states):
    tokens, width = x_in.shape
    wide = jax.ShapeDtypeStruct((tokens, width), f32)
    half = jax.ShapeDtypeStruct((tokens, width), bf16)
    square = jax.ShapeDtypeStruct((tokens, tokens), f32)
    return pl.pallas_call(
        pre_kernel,
        out_shape=(wide, wide, wide, half, half, square, wide),
        compiler_params=small(),
        cost_estimate=cost(4 * tokens * width * 128, 2 << 20),
    )(rows, x_in, b_in, c_in, states)


def intra_kernel(
    dy_ref, decayed_ref, x_ref, scaled_ref, b_ref, c_ref, states_ref, rows_ref, skip_ref, start_ref, step_ref, scores_ref, y_ref,
    base_ref, db_ref, dc_ref, part_ref, across_ref,
):
    tokens, width = dy_ref.shape
    head_dim = width // 4
    cum = rows_ref[:4]
    columns = rows_ref[...].T
    scores = scores_ref[...]
    dy = dy_ref[...]
    causal = lax.broadcasted_iota(jnp.int32, (tokens, tokens), 0) >= lax.broadcasted_iota(jnp.int32, (tokens, tokens), 1)
    total = jnp.zeros((tokens, tokens), f32)
    along, down, backs = [], [], []
    for h in range(4):
        mine = slice(h * head_dim, (h + 1) * head_dim)
        dy_h = dy[:, mine]
        gaps = jnp.minimum(columns[:, h:h + 1] - cum[h:h + 1], 0.0)
        mask = jnp.where(causal, jnp.exp(gaps), 0.0)
        weighed = (scores * mask).astype(bf16)
        backs.append(lax.dot_general(weighed, dy_h, (((0,), (0,)), ((), ())), preferred_element_type=f32))
        masked = dot_last(dy_h, scaled_ref[:, mine]) * mask
        total = total + masked
        pairs = masked * scores
        along.append(jnp.sum(pairs, axis=1, keepdims=True))
        down.append(jnp.sum(pairs, axis=0, keepdims=True))
    total = total.astype(bf16)
    db_ref[...] = lax.dot_general(total, c_ref[...], (((0,), (0,)), ((), ())), preferred_element_type=f32)
    dc = jnp.dot(total, b_ref[...], preferred_element_type=f32)
    dc = dc + jnp.dot(decayed_ref[...], states_ref[...], preferred_element_type=f32)
    dc_ref[...] = dc.T.astype(bf16)
    back = jnp.concatenate(backs, axis=1)
    dy = dy.astype(f32)
    x = x_ref[...].astype(f32)
    base_ref[...] = step_ref[...] * back + skip_ref[...] * dy
    entered = head_sums(start_ref[...] * dy * y_ref[...], 4)
    rows = as_rows([a + e for a, e in zip(along, entered)] + head_sums(x * back, 4))
    part_ref[...] = rows - jnp.concatenate(down + [jnp.zeros((4, tokens), f32)], axis=0)
    across_ref[...] = jnp.sum(dy * x, axis=0, keepdims=True)


def intra_terms(dy, decayed, x_in, scaled, b_in, c_in, states, rows, skip, start, step, scores, y_state):
    tokens, width = dy.shape
    state_dim = b_in.shape[1]
    return pl.pallas_call(
        intra_kernel,
        out_shape=(
            jax.ShapeDtypeStruct((tokens, width), f32),
            jax.ShapeDtypeStruct((tokens, state_dim), f32),
            jax.ShapeDtypeStruct((state_dim, tokens), bf16),
            jax.ShapeDtypeStruct((8, tokens), f32),
            jax.ShapeDtypeStruct((1, width), f32),
        ),
        compiler_params=small(),
        cost_estimate=cost(12 * tokens * tokens * width, 4 << 20),
    )(dy, decayed, x_in, scaled, b_in, c_in, states, rows, skip, start, step, scores, y_state)


def dt_kernel(back_ref, x_ref, rows_ref, part_ref, across_ref, carried_ref, states_ref, raw_ref, scal_ref, dt_ref, param_ref):
    tokens, width = x_ref.shape
    head_dim = width // 4
    cum, step = rows_ref[:4], rows_ref[4:]
    last = cum[:, tokens - 1:]
    rate, bias = scal_ref[:, 0:1], scal_ref[:, 1:2]
    dots = as_rows(head_sums(x_ref[...].astype(f32) * back_ref[...], 4))[:4]
    end_decay = jnp.exp(last - cum)
    end_terms = step * end_decay * dots
    carried = carried_ref[...].reshape(4, head_dim, -1)
    held = jnp.sum(carried * states_ref[...].astype(f32).reshape(4, head_dim, -1), axis=1)
    tail = jnp.sum(end_terms, axis=1, keepdims=True) + jnp.exp(last) * jnp.sum(held, axis=1, keepdims=True)
    below = lax.broadcasted_iota(jnp.int32, (tokens, tokens), 0) >= lax.broadcasted_iota(jnp.int32, (tokens, tokens), 1)
    step_grad = tail + jnp.dot(
        part_ref[:4] - end_terms, below.astype(f32), precision=lax.Precision.HIGHEST, preferred_element_type=f32
    )
    dt_sum = part_ref[4:] + end_decay * dots - rate * step_grad
    dt = dt_sum * jax.nn.sigmoid(raw_ref[...] + bias)
    dt_ref[...] = dt
    lanes = lax.broadcasted_iota(jnp.int32, (4, width), 1)
    heads = lax.broadcasted_iota(jnp.int32, (4, width), 0)
    skip = jnp.sum(jnp.where(lanes // head_dim == heads, across_ref[...], 0.0), axis=1, keepdims=True)
    decays = jnp.sum(step_grad * (-rate * step), axis=1, keepdims=True)
    biases = jnp.sum(dt, axis=1, keepdims=True)
    lanes, heads = lanes[:, :128], heads[:, :128]
    placed = jnp.where(lanes == heads, decays, 0.0)
    placed = jnp.where(lanes == heads + 4, skip, placed)
    placed = jnp.where(lanes == heads + 8, biases, placed)
    param_ref[...] = jnp.sum(placed, axis=0, keepdims=True)


def dt_terms(back, x_in, rows, part, across, carried, states, dt_raw, scalars):
    return pl.pallas_call(
        dt_kernel,
        out_shape=(jax.ShapeDtypeStruct(dt_raw.shape, f32), jax.ShapeDtypeStruct((1, 128), f32)),
        compiler_params=small(),
        cost_estimate=cost(1 << 22, 1 << 20),
    )(back, x_in, rows, part, across, carried, states, dt_raw, scalars)


def x_grad_kernel(carried_ref, b_ref, base_ref, weight_ref, x_end_ref, db_ref, dc_ref, sent_ref, back_ref):
    blocks, rows, width = carried_ref.shape
    carried = carried_ref[...].reshape(blocks * rows, width).astype(bf16)
    back = dot_last(b_ref[...], carried)
    back_ref[...] = back
    x_grad = (base_ref[...] + weight_ref[...] * back).astype(bf16)
    entry = jnp.dot(x_end_ref[...], carried, preferred_element_type=f32)
    tokens = entry.shape[0]
    rows = width // 2
    db = (db_ref[...] + entry).T.astype(bf16)
    for y in range(4):
        sent_ref[y, :tokens] = x_grad
        if y < 2:
            sent_ref[y, tokens:] = db[y * rows:(y + 1) * rows]
        else:
            sent_ref[y, tokens:] = dc_ref[(y - 2) * rows:(y - 1) * rows]


def x_grads(carried, b_in, base, weight, x_end, db, dc):
    tokens, inner = base.shape
    rows = db.shape[1] // 2
    return pl.pallas_call(
        x_grad_kernel,
        out_shape=(
            jax.ShapeDtypeStruct((4, tokens + rows, inner), bf16),
            jax.ShapeDtypeStruct((tokens, inner), f32),
        ),
        compiler_params=small(),
        cost_estimate=cost(4 * tokens * inner * 128, 2 << 20),
    )(carried, b_in, base, weight, x_end, db, dc)


def in_kernel(y_ref, got_ref, own_ref, *refs):
    *held_refs, out_ref = refs
    tokens = got_ref.shape[2]
    feats = own_ref.shape[0]
    y = y_ref[0]
    total = dot_last(own_ref[...], got_ref[y, :tokens])
    for s, w_ref in enumerate(held_refs):
        total = total + dot_last(w_ref[...], got_ref[lax.rem(y + 3 - s, 4), :tokens])
    out_ref[0, :feats] = total.astype(bf16)
    rows = out_ref.shape[1] - feats
    at = pl.ds(pl.multiple_of(tokens + pl.program_id(0) * rows, rows), rows)
    bc = got_ref[0, at].astype(f32)
    for other in range(1, 4):
        bc = bc + got_ref[other, at].astype(f32)
    out_ref[0, feats:] = bc.astype(bf16)


def in_products(y, got, w_in, held):
    features, inner = w_in.shape
    _, height, tokens = got.shape
    feats, rows = features // 16, (height - tokens) // 4
    return pl.pallas_call(
        in_kernel,
        grid_spec=pltpu.PrefetchScalarGridSpec(
            num_scalar_prefetch=1,
            grid=(4,),
            in_specs=[
                pl.BlockSpec(got.shape, lambda z, y: (0, 0, 0)),
                pl.BlockSpec((feats, inner), lambda z, y: (4 * y[0] + z, 0)),
            ]
            + [pl.BlockSpec((feats, inner), lambda z, y: (z, 0))] * 3,
            out_specs=pl.BlockSpec((1, feats + rows, tokens), lambda z, y: (z, 0, 0)),
        ),
        out_shape=jax.ShapeDtypeStruct((4, feats + rows, tokens), bf16),
        compiler_params=small(),
        cost_estimate=cost(8 * features * inner * tokens // 4, 4 << 20),
    )(y.reshape(1), got, w_in, *held)


def sum_kernel(terms_ref, in_ref, bc_ref):
    feats = in_ref.shape[0]
    total = terms_ref[0].astype(f32)
    for z in range(1, 4):
        total = total + terms_ref[z].astype(f32)
    total = total.astype(bf16)
    in_ref[...] = total[:feats]
    bc_ref[...] = total[feats:]


def final_sums(terms, feats):
    _, height, tokens = terms.shape
    return pl.pallas_call(
        sum_kernel,
        out_shape=(
            jax.ShapeDtypeStruct((feats, tokens), bf16),
            jax.ShapeDtypeStruct((height - feats, tokens), bf16),
        ),
        compiler_params=small(),
        cost_estimate=cost(4 * height * tokens, 1 << 20),
    )(terms)


def shards(out_grad, x_in, b_in, c_in, dt_raw, dt_bias, a_log, d_skip, states, w_out, w_in):
    tokens_here, inner_here = x_in.shape
    group_heads = dt_raw.shape[0]
    head_dim = inner_here // group_heads
    state_dim = b_in.shape[1]
    blocks = lax.axis_size(SEQ)
    y = lax.axis_index("y")
    entry_state = states[0]

    w_out_y = lax.all_to_all(regrouped(w_out), "y", 0, 0)
    near = lax.all_gather(out_grad, "zh", axis=1, tiled=True)
    head_parts = lax.all_to_all(partial_products(near, w_out_y), "y", 0, 0)

    decay_rate = jnp.exp(a_log)
    step_size = jax.nn.softplus(dt_raw + dt_bias[:, None])
    log_step = -decay_rate[:, None] * step_size
    positions = jnp.arange(tokens_here)
    upto = (positions[:, None] <= positions[None, :]).astype(f32)
    cumlog = jnp.dot(log_step, upto, precision=lax.Precision.HIGHEST)
    rows = jnp.concatenate([cumlog, step_size], axis=0)
    ends = jnp.pad(three_parts(jnp.exp(cumlog[:, -1])), ((0, 0), (0, 5)))
    ends = jnp.broadcast_to(ends[:, None, :, None], (group_heads, blocks // group_heads, 8, state_dim))
    scalars = jnp.pad(jnp.stack([decay_rate, dt_bias], axis=1), ((0, 0), (0, 126)))
    skip = jnp.repeat(d_skip, head_dim)[None]
    start, step, weight, scaled, x_end, scores, y_state = prepared(rows, x_in, b_in, c_in, entry_state)

    w_in_held, head_parts = lax.optimization_barrier((w_in, head_parts))
    quarter = w_in.shape[0] // 4
    pieces = [lax.dynamic_slice_in_dim(w_in_held, lax.rem(y + s, 4) * quarter, quarter) for s in range(1, 4)]
    shift = [[(i, (i + s) % 4) for i in range(4)] for s in range(1, 4)]
    dy, decayed, sent = local_states(head_parts, start, c_in, ends.reshape(blocks, 8, state_dim))
    held = [lax.ppermute(pieces[1], "y", shift[1]), lax.ppermute(pieces[0], "y", shift[0])]
    ahead = suffix_scan(lax.all_to_all(sent, SEQ, 0, 0))
    ahead, dy, piece = lax.optimization_barrier((ahead, dy, pieces[2]))
    held.append(lax.ppermute(piece, "y", shift[2]))
    base, db, dc, part, across = intra_terms(
        dy, decayed, x_in, scaled, b_in, c_in, entry_state, rows, skip, start, step, scores, y_state
    )
    *held, carried, base = lax.optimization_barrier((*held, lax.all_to_all(ahead, SEQ, 0, 0), base))
    sent_y, back = x_grads(carried, b_in, base, weight, x_end, db, dc)
    got = lax.all_to_all(sent_y, "y", 0, 0)
    dt_grad, row = dt_terms(back, x_in, rows, part, across, carried, entry_state, dt_raw, scalars)
    for flip in (1, 2):
        row = row + lax.ppermute(row, "zl", [(i, i ^ flip) for i in range(4)])
    row, got = lax.optimization_barrier((row, got))
    terms = in_products(y, got, w_in, (held[1], held[0], held[2]))
    row, terms = lax.optimization_barrier((row, terms))
    for axis, flip in (("core", 1), ("x", 1), ("x", 2)):
        row = row + lax.ppermute(row, axis, [(i, i ^ flip) for i in range(lax.axis_size(axis))])
    in_grad, bc_grad = final_sums(lax.all_to_all(terms, "zh", 0, 0), w_in.shape[0] // 16)
    norm_scale = (blocks * tokens_here * head_dim) ** (-0.5)
    param_grad = row[0, : 3 * group_heads].reshape(3, group_heads) * norm_scale
    return (in_grad, bc_grad, dt_grad, param_grad)


def solution(mesh):
    fine = Mesh(mesh.devices.reshape(4, 4, 2, 4, 4), ("x", "zl", "core", "y", "zh"))
    return jax.shard_map(
        shards,
        mesh=fine,
        in_specs=(
            P(SEQ, HEAD),
            P(SEQ, HEAD),
            P(SEQ, None),
            P(SEQ, None),
            P(HEAD, SEQ),
            P(HEAD),
            P(HEAD),
            P(HEAD),
            P(SEQ, HEAD, None),
            P(HEAD, None),
            P(None, HEAD),
        ),
        out_specs=(P(HEAD, SEQ), P(HEAD, SEQ), P(HEAD, SEQ), P(None, HEAD)),
        check_vma=False,
    )
```

```python
import jax
import jax.numpy as jnp
from jax import lax
from jax.experimental import pallas as pl
from jax.experimental.pallas import tpu as pltpu
from jax.sharding import Mesh, PartitionSpec as P

SEQ = ("x", "zl", "core")
HEAD = ("y", "zh")
f32, bf16 = jnp.float32, jnp.bfloat16


def scan_kernel(parts_ref, carried_ref):
    blocks = parts_ref.shape[0]
    held = jnp.zeros(carried_ref.shape[1:], f32)
    for k in range(blocks - 1, -1, -1):
        carried_ref[k] = held
        wide = parts_ref[k].astype(f32)
        total = wide[8:9] + wide[9:10] + wide[10:11]
        held = total * held + wide[:8]


def suffix_scan(parts):
    blocks, _, width = parts.shape
    return pl.pallas_call(
        scan_kernel,
        out_shape=jax.ShapeDtypeStruct((blocks, 8, width), f32),
        compiler_params=small(),
        cost_estimate=cost(blocks * 3072, blocks * 8192),
    )(parts)


def three_parts(values):
    first = values.astype(bf16).astype(f32)
    second = (values - first).astype(bf16).astype(f32)
    return jnp.stack([first, second, values - first - second], axis=-1)


def cost(flops, moved):
    return pl.CostEstimate(flops=flops, bytes_accessed=moved, transcendentals=0)


def small(mib=16):
    return pltpu.CompilerParams(vmem_limit_bytes=mib << 20)


def dot_last(a, b):
    return lax.dot_general(a, b, (((1,), (1,)), ((), ())), preferred_element_type=f32)


def regroup_kernel(w_ref, out_ref, stage_ref, in_sems, out_sems):
    _, pieces, rows, part = stage_ref.shape
    steps = [(g, r) for g in range(4) for r in range(pieces)]

    def copy_in(g, r):
        source = w_ref.at[pl.ds(r * rows, rows), pl.ds(g * part, part)]
        return pltpu.make_async_copy(source, stage_ref.at[g, r], in_sems.at[g, r])

    def copy_out(g, r):
        return pltpu.make_async_copy(stage_ref.at[g, r], out_ref.at[g, pl.ds(r * rows, rows)], out_sems.at[g, r])

    for step in steps:
        copy_in(*step).start()
    for step in steps:
        copy_in(*step).wait()
        copy_out(*step).start()
    for step in steps:
        copy_out(*step).wait()


def regrouped(w):
    rows, width = w.shape
    pieces = 4
    return pl.pallas_call(
        regroup_kernel,
        in_specs=[pl.BlockSpec(memory_space=pl.ANY)],
        out_specs=pl.BlockSpec(memory_space=pl.ANY),
        out_shape=jax.ShapeDtypeStruct((4, rows, width // 4), w.dtype),
        scratch_shapes=[
            pltpu.VMEM((4, pieces, rows // pieces, width // 4), w.dtype),
            pltpu.SemaphoreType.DMA((4, pieces)),
            pltpu.SemaphoreType.DMA((4, pieces)),
        ],
        cost_estimate=cost(0, 4 * rows * width),
    )(w)


def partial_kernel(near_ref, w_ref, out_ref):
    out_ref[0] = dot_last(w_ref[0], near_ref[...]).astype(bf16)


def partial_products(near, w_mine):
    groups, inner, depth = w_mine.shape
    tokens = near.shape[0]
    return pl.pallas_call(
        partial_kernel,
        grid=(groups,),
        in_specs=[
            pl.BlockSpec((tokens, depth), lambda g: (0, 0)),
            pl.BlockSpec((1, inner, depth), lambda g: (g, 0, 0)),
        ],
        out_specs=pl.BlockSpec((1, inner, tokens), lambda g: (g, 0, 0)),
        out_shape=jax.ShapeDtypeStruct((groups, inner, tokens), bf16),
        compiler_params=small(),
        cost_estimate=cost(2 * groups * tokens * inner * depth, 4 << 20),
    )(near, w_mine)


def over_channels(rows, height):
    heads, tokens = rows.shape
    return jnp.concatenate(
        [jnp.broadcast_to(rows[h:h + 1], (height // heads, tokens)) for h in range(heads)], axis=0
    )


def state_kernel(parts_ref, rows_ref, c_ref, ends_ref, dy_ref, sent_ref):
    total = parts_ref[0].astype(f32)
    for y in range(1, parts_ref.shape[0]):
        total = total + parts_ref[y].astype(f32)
    dy = total.astype(bf16)
    dy_ref[...] = dy
    start = over_channels(jnp.exp(rows_ref[:4]), dy.shape[0])
    decayed = (dy.astype(f32) * start).astype(bf16)
    state = jnp.dot(decayed, c_ref[...], preferred_element_type=f32)
    blocks, rows, width = ends_ref.shape
    state = state.reshape(blocks, rows, width)
    sent_ref[...] = jnp.concatenate([state, ends_ref[...]], axis=1).astype(bf16)


def local_states(parts, rows, c_in, ends):
    _, inner, tokens = parts.shape
    blocks, height, width = ends.shape
    return pl.pallas_call(
        state_kernel,
        out_shape=(pltpu.HBM((inner, tokens), bf16), pltpu.HBM((blocks, 2 * height, width), bf16)),
        compiler_params=small(),
        cost_estimate=cost(2 * tokens * inner * width, 2 << 20),
    )(parts, rows, c_in, ends)


def widened(columns, width):
    tokens, heads = columns.shape
    return jnp.concatenate(
        [jnp.broadcast_to(columns[:, h:h + 1], (tokens, width // heads)) for h in range(heads)], axis=1
    )


def head_sums(values, heads):
    width = values.shape[1] // heads
    return [jnp.sum(values[:, h * width:(h + 1) * width], axis=1, keepdims=True) for h in range(heads)]


def as_rows(columns):
    tokens = columns[0].shape[0]
    lanes = lax.broadcasted_iota(jnp.int32, (tokens, 128), 1)
    spread = jnp.zeros((tokens, 128), f32)
    for k, column in enumerate(columns):
        spread = jnp.where(lanes == k, column, spread)
    return spread.T[:8]


def intra_kernel(dy_ref, x_ref, b_ref, c_ref, states_ref, rows_ref, skip_ref, wide_ref, half_ref, part_ref):
    width, tokens = dy_ref.shape
    head_dim = width // 4
    cum = rows_ref[:4]
    columns = rows_ref[...].T
    step = widened(columns[:, 4:], width)
    start = widened(jnp.exp(columns[:, :4]), width)
    b, c, states = b_ref[...], c_ref[...], states_ref[...]
    scores = dot_last(c, b)
    entered = dot_last(c, states)
    dy_wide = dy_ref[...].astype(f32).T
    dy = dy_wide.astype(bf16)
    x = x_ref[...].astype(f32)
    scaled = (x * step).astype(bf16)
    causal = lax.broadcasted_iota(jnp.int32, (tokens, tokens), 0) >= lax.broadcasted_iota(jnp.int32, (tokens, tokens), 1)
    total = jnp.zeros((tokens, tokens), f32)
    along, down, backs = [], [], []
    for h in range(4):
        mine = slice(h * head_dim, (h + 1) * head_dim)
        dy_h = dy[:, mine]
        gaps = jnp.minimum(columns[:, h:h + 1] - cum[h:h + 1], 0.0)
        mask = jnp.where(causal, jnp.exp(gaps), 0.0)
        weighed = (scores * mask).astype(bf16)
        backs.append(lax.dot_general(weighed, dy_h, (((0,), (0,)), ((), ())), preferred_element_type=f32))
        masked = dot_last(dy_h, scaled[:, mine]) * mask
        total = total + masked
        pairs = masked * scores
        along.append(jnp.sum(pairs, axis=1, keepdims=True))
        down.append(jnp.sum(pairs, axis=0, keepdims=True))
    total = total.astype(bf16)
    db = lax.dot_general(total, c, (((0,), (0,)), ((), ())), preferred_element_type=f32)
    dc = jnp.dot(total, b, preferred_element_type=f32)
    dc = dc + jnp.dot((dy_wide * start).astype(bf16), states, preferred_element_type=f32)
    back = jnp.concatenate(backs, axis=1)
    wide_ref[:width] = (step * back + skip_ref[...] * dy_wide).T
    wide_ref[width:] = db.T
    half_ref[:width] = x.T.astype(bf16)
    half_ref[width:] = dc.T.astype(bf16)
    entered = head_sums(start * dy_wide * entered, 4)
    rows = as_rows([a + e for a, e in zip(along, entered)] + head_sums(x * back, 4))
    part_ref[:8] = rows - jnp.concatenate(down + [jnp.zeros((4, tokens), f32)], axis=0)
    part_ref[8:] = jnp.broadcast_to(jnp.sum(dy_wide * x, axis=0, keepdims=True), (8, width))


def intra_terms(dy, x_in, b_in, c_in, states, rows, skip):
    width, tokens = dy.shape
    height = width + b_in.shape[1]
    return pl.pallas_call(
        intra_kernel,
        out_shape=(pltpu.HBM((height, tokens), f32), pltpu.HBM((height, tokens), bf16), pltpu.HBM((16, tokens), f32)),
        cost_estimate=cost(14 * tokens * tokens * width, 2 << 20),
    )(dy, x_in, b_in, c_in, states, rows, skip)


def dt_kernel(back_ref, half_ref, rows_ref, part_ref, carried_ref, states_ref, raw_ref, scal_ref, dt_ref, param_ref):
    width, tokens = back_ref.shape
    head_dim = width // 4
    cum, step = rows_ref[:4], rows_ref[4:]
    last = cum[:, tokens - 1:]
    rate, bias = scal_ref[:, 0:1], scal_ref[:, 1:2]
    dots = jnp.sum((half_ref[:width].astype(f32) * back_ref[...]).reshape(4, head_dim, tokens), axis=1)
    end_decay = jnp.exp(last - cum)
    end_terms = step * end_decay * dots
    carried = carried_ref[...].reshape(4, head_dim, -1)
    held = jnp.sum(carried * states_ref[...].astype(f32).reshape(4, head_dim, -1), axis=1)
    tail = jnp.sum(end_terms, axis=1, keepdims=True) + jnp.exp(last) * jnp.sum(held, axis=1, keepdims=True)
    below = lax.broadcasted_iota(jnp.int32, (tokens, tokens), 0) >= lax.broadcasted_iota(jnp.int32, (tokens, tokens), 1)
    step_grad = tail + jnp.dot(
        part_ref[:4] - end_terms, below.astype(f32), precision=lax.Precision.HIGHEST, preferred_element_type=f32
    )
    dt_sum = part_ref[4:8] + end_decay * dots - rate * step_grad
    dt = dt_sum * jax.nn.sigmoid(raw_ref[...] + bias)
    dt_ref[...] = dt
    lanes = lax.broadcasted_iota(jnp.int32, (4, width), 1)
    heads = lax.broadcasted_iota(jnp.int32, (4, width), 0)
    skip = jnp.sum(jnp.where(lanes // head_dim == heads, part_ref[8:9], 0.0), axis=1, keepdims=True)
    decays = jnp.sum(step_grad * (-rate * step), axis=1, keepdims=True)
    biases = jnp.sum(dt, axis=1, keepdims=True)
    lanes, heads = lanes[:, :128], heads[:, :128]
    placed = jnp.where(lanes == heads, decays, 0.0)
    placed = jnp.where(lanes == heads + 4, skip, placed)
    placed = jnp.where(lanes == heads + 8, biases, placed)
    param_ref[...] = jnp.sum(placed, axis=0, keepdims=True)


def dt_terms(back, half, rows, part, carried, states, dt_raw, scalars):
    return pl.pallas_call(
        dt_kernel,
        out_shape=(jax.ShapeDtypeStruct(dt_raw.shape, f32), jax.ShapeDtypeStruct((1, 128), f32)),
        compiler_params=small(),
        cost_estimate=cost(1 << 22, 1 << 20),
    )(back, half, rows, part, carried, states, dt_raw, scalars)


def x_grad_kernel(carried_ref, b_ref, wide_hbm, half_hbm, rows_ref, sent_ref, back_ref, wide_ref, half_ref, sems):
    fetches = [
        pltpu.make_async_copy(wide_hbm, wide_ref, sems.at[0]),
        pltpu.make_async_copy(half_hbm, half_ref, sems.at[1]),
    ]
    for fetch in fetches:
        fetch.start()
    blocks, height, state_dim = carried_ref.shape
    width = blocks * height
    tokens = b_ref.shape[0]
    carried = carried_ref[...].reshape(width, state_dim).astype(bf16)
    back = dot_last(carried, b_ref[...])
    back_ref[...] = back
    cum = rows_ref[:4]
    weight = over_channels(rows_ref[4:] * jnp.exp(cum[:, tokens - 1:] - cum), width)
    for fetch in fetches:
        fetch.wait()
    x_grad = (wide_ref[:width] + weight * back).astype(bf16)
    x_end = (half_ref[:width].astype(f32) * weight).astype(bf16)
    entry = lax.dot_general(carried, x_end, (((0,), (0,)), ((), ())), preferred_element_type=f32)
    db = (wide_ref[width:] + entry).astype(bf16)
    rows = state_dim // 2
    for y in range(4):
        sent_ref[y, :width] = x_grad
        if y < 2:
            sent_ref[y, width:] = db[y * rows:(y + 1) * rows]
        else:
            sent_ref[y, width:] = half_ref[width + (y - 2) * rows:width + (y - 1) * rows]


def x_grads(carried, b_in, wide, half, rows):
    tokens, state_dim = b_in.shape
    inner = wide.shape[0] - state_dim
    at_vmem, at_hbm = pl.BlockSpec(memory_space=pltpu.VMEM), pl.BlockSpec(memory_space=pltpu.HBM)
    return pl.pallas_call(
        x_grad_kernel,
        in_specs=[at_vmem, at_vmem, at_hbm, at_hbm, at_vmem],
        scratch_shapes=[
            pltpu.VMEM(wide.shape, wide.dtype),
            pltpu.VMEM(half.shape, half.dtype),
            pltpu.SemaphoreType.DMA((2,)),
        ],
        out_shape=(pltpu.HBM((4, inner + state_dim // 2, tokens), bf16), pltpu.HBM((inner, tokens), f32)),
        cost_estimate=cost(4 * tokens * inner * 128, 2 << 20),
    )(carried, b_in, wide, half, rows)


def in_kernel(y_ref, got_ref, own_hbm, *refs):
    *held_hbm, out_hbm, w_ref, out_ref, w_sems, out_sems = refs
    _, _, feats, inner = w_ref.shape
    rows = out_ref.shape[1] - feats
    y = y_ref[0]

    def fetch(z, s):
        at = pl.multiple_of((4 * y + z) * feats, feats) if s == 0 else z * feats
        source = own_hbm if s == 0 else held_hbm[s - 1]
        return pltpu.make_async_copy(source.at[pl.ds(at, feats)], w_ref.at[z, s], w_sems.at[z, s])

    def store(z):
        return pltpu.make_async_copy(out_ref.at[z], out_hbm.at[z], out_sems.at[z])

    for z in range(4):
        for s in range(4):
            fetch(z, s).start()
    for z in range(4):
        at = slice(inner + z * rows, inner + (z + 1) * rows)
        bc = got_ref[0, at].astype(f32)
        for other in range(1, 4):
            bc = bc + got_ref[other, at].astype(f32)
        out_ref[z, feats:] = bc.astype(bf16)
        total = jnp.zeros((feats, got_ref.shape[2]), f32)
        for s in range(4):
            fetch(z, s).wait()
            total = total + jnp.dot(w_ref[z, s], got_ref[lax.rem(y + 4 - s, 4), :inner], preferred_element_type=f32)
        out_ref[z, :feats] = total.astype(bf16)
        store(z).start()
    for z in range(4):
        store(z).wait()


def in_products(y, got, w_in, held):
    features, inner = w_in.shape
    _, height, tokens = got.shape
    feats, rows = features // 16, (height - inner) // 4
    out = (4, feats + rows, tokens)
    return pl.pallas_call(
        in_kernel,
        in_specs=[pl.BlockSpec(memory_space=pltpu.SMEM), pl.BlockSpec(memory_space=pltpu.VMEM)]
        + [pl.BlockSpec(memory_space=pltpu.HBM)] * 4,
        out_specs=pl.BlockSpec(memory_space=pltpu.HBM),
        out_shape=jax.ShapeDtypeStruct(out, bf16),
        scratch_shapes=[
            pltpu.VMEM((4, 4, feats, inner), w_in.dtype),
            pltpu.VMEM(out, bf16),
            pltpu.SemaphoreType.DMA((4, 4)),
            pltpu.SemaphoreType.DMA((4,)),
        ],
        cost_estimate=cost(8 * features * inner * tokens // 4, 4 << 20),
    )(y.reshape(1), got, w_in, *held)


def sum_kernel(terms_ref, in_ref, bc_ref):
    feats = in_ref.shape[0]
    total = terms_ref[0].astype(f32)
    for z in range(1, 4):
        total = total + terms_ref[z].astype(f32)
    total = total.astype(bf16)
    in_ref[...] = total[:feats]
    bc_ref[...] = total[feats:]


def final_sums(terms, feats):
    _, height, tokens = terms.shape
    return pl.pallas_call(
        sum_kernel,
        out_shape=(
            jax.ShapeDtypeStruct((feats, tokens), bf16),
            jax.ShapeDtypeStruct((height - feats, tokens), bf16),
        ),
        compiler_params=small(),
        cost_estimate=cost(4 * height * tokens, 1 << 20),
    )(terms)


def shards(out_grad, x_in, b_in, c_in, dt_raw, dt_bias, a_log, d_skip, states, w_out, w_in):
    tokens_here, inner_here = x_in.shape
    group_heads = dt_raw.shape[0]
    head_dim = inner_here // group_heads
    state_dim = b_in.shape[1]
    blocks = lax.axis_size(SEQ)
    y = lax.axis_index("y")
    entry_state = states[0]

    w_out_y = lax.all_to_all(regrouped(w_out), "y", 0, 0)
    near = lax.all_gather(out_grad, "zh", axis=1, tiled=True)
    head_parts = lax.all_to_all(partial_products(near, w_out_y), "y", 0, 0)

    decay_rate = jnp.exp(a_log)
    step_size = jax.nn.softplus(dt_raw + dt_bias[:, None])
    log_step = -decay_rate[:, None] * step_size
    positions = jnp.arange(tokens_here)
    upto = (positions[:, None] <= positions[None, :]).astype(f32)
    cumlog = jnp.dot(log_step, upto, precision=lax.Precision.HIGHEST)
    rows = jnp.concatenate([cumlog, step_size], axis=0)
    ends = jnp.pad(three_parts(jnp.exp(cumlog[:, -1])), ((0, 0), (0, 5)))
    ends = jnp.broadcast_to(ends[:, None, :, None], (group_heads, blocks // group_heads, 8, state_dim))
    scalars = jnp.pad(jnp.stack([decay_rate, dt_bias], axis=1), ((0, 0), (0, 126)))
    skip = jnp.repeat(d_skip, head_dim)[None]
    w_in_held, head_parts = lax.optimization_barrier((w_in, head_parts))
    quarter = w_in.shape[0] // 4
    pieces = [lax.dynamic_slice_in_dim(w_in_held, lax.rem(y + s, 4) * quarter, quarter) for s in range(1, 4)]
    shift = [[(i, (i + s) % 4) for i in range(4)] for s in range(1, 4)]
    dy, sent = local_states(head_parts, rows, c_in, ends.reshape(blocks, 8, state_dim))
    held = [lax.ppermute(pieces[1], "y", shift[1]), lax.ppermute(pieces[0], "y", shift[0])]
    ahead = suffix_scan(lax.all_to_all(sent, SEQ, 0, 0))
    ahead, dy, piece = lax.optimization_barrier((ahead, dy, pieces[2]))
    held.append(lax.ppermute(piece, "y", shift[2]))
    wide, half, part = intra_terms(dy, x_in, b_in, c_in, entry_state, rows, skip)
    *held, carried, wide = lax.optimization_barrier((*held, lax.all_to_all(ahead, SEQ, 0, 0), wide))
    sent_y, back = x_grads(carried, b_in, wide, half, rows)
    got = lax.all_to_all(sent_y, "y", 0, 0)
    dt_grad, row = dt_terms(back, half, rows, part, carried, entry_state, dt_raw, scalars)
    for flip in (1, 2):
        row = row + lax.ppermute(row, "zl", [(i, i ^ flip) for i in range(4)])
    row, got = lax.optimization_barrier((row, got))
    terms = in_products(y, got, w_in, (held[1], held[0], held[2]))
    row, terms = lax.optimization_barrier((row, terms))
    for axis, flip in (("core", 1), ("x", 1), ("x", 2)):
        row = row + lax.ppermute(row, axis, [(i, i ^ flip) for i in range(lax.axis_size(axis))])
    in_grad, bc_grad = final_sums(lax.all_to_all(terms, "zh", 0, 0), w_in.shape[0] // 16)
    norm_scale = (blocks * tokens_here * head_dim) ** (-0.5)
    param_grad = row[0, : 3 * group_heads].reshape(3, group_heads) * norm_scale
    return (in_grad, bc_grad, dt_grad, param_grad)


def solution(mesh):
    fine = Mesh(mesh.devices.reshape(4, 4, 2, 4, 4), ("x", "zl", "core", "y", "zh"))
    return jax.shard_map(
        shards,
        mesh=fine,
        in_specs=(
            P(SEQ, HEAD),
            P(SEQ, HEAD),
            P(SEQ, None),
            P(SEQ, None),
            P(HEAD, SEQ),
            P(HEAD),
            P(HEAD),
            P(HEAD),
            P(SEQ, HEAD, None),
            P(HEAD, None),
            P(None, HEAD),
        ),
        out_specs=(P(HEAD, SEQ), P(HEAD, SEQ), P(HEAD, SEQ), P(None, HEAD)),
        check_vma=False,
    )
```

```python
import jax
import jax.numpy as jnp
from jax import lax
from jax.experimental import pallas as pl
from jax.experimental.pallas import tpu as pltpu
from jax.sharding import Mesh, PartitionSpec as P

SEQ = ("x", "zl", "core")
HEAD = ("y", "zh")
f32, bf16 = jnp.float32, jnp.bfloat16


def scan_kernel(parts_ref, carried_ref):
    blocks = parts_ref.shape[0]
    held = jnp.zeros(carried_ref.shape[1:], f32)
    for k in range(blocks - 1, -1, -1):
        carried_ref[k] = held
        wide = parts_ref[k].astype(f32)
        total = wide[8:9] + wide[9:10] + wide[10:11]
        held = total * held + wide[:8]


def suffix_scan(parts):
    blocks, _, width = parts.shape
    return pl.pallas_call(
        scan_kernel,
        out_shape=jax.ShapeDtypeStruct((blocks, 8, width), f32),
        compiler_params=small(),
        cost_estimate=cost(blocks * 3072, blocks * 8192),
    )(parts)


def three_parts(values):
    first = values.astype(bf16).astype(f32)
    second = (values - first).astype(bf16).astype(f32)
    return jnp.stack([first, second, values - first - second], axis=-1)


def cost(flops, moved):
    return pl.CostEstimate(flops=flops, bytes_accessed=moved, transcendentals=0)


def small(mib=16):
    return pltpu.CompilerParams(vmem_limit_bytes=mib << 20)


def dot_last(a, b):
    return lax.dot_general(a, b, (((1,), (1,)), ((), ())), preferred_element_type=f32)


def regroup_kernel(w_ref, out_ref, stage_ref, in_sems, out_sems):
    _, pieces, rows, part = stage_ref.shape
    steps = [(g, r) for g in range(4) for r in range(pieces)]

    def copy_in(g, r):
        source = w_ref.at[pl.ds(r * rows, rows), pl.ds(g * part, part)]
        return pltpu.make_async_copy(source, stage_ref.at[g, r], in_sems.at[g, r])

    def copy_out(g, r):
        return pltpu.make_async_copy(stage_ref.at[g, r], out_ref.at[g, pl.ds(r * rows, rows)], out_sems.at[g, r])

    for step in steps:
        copy_in(*step).start()
    for step in steps:
        copy_in(*step).wait()
        copy_out(*step).start()
    for step in steps:
        copy_out(*step).wait()


def regrouped(w):
    rows, width = w.shape
    pieces = 4
    return pl.pallas_call(
        regroup_kernel,
        in_specs=[pl.BlockSpec(memory_space=pl.ANY)],
        out_specs=pl.BlockSpec(memory_space=pl.ANY),
        out_shape=jax.ShapeDtypeStruct((4, rows, width // 4), w.dtype),
        scratch_shapes=[
            pltpu.VMEM((4, pieces, rows // pieces, width // 4), w.dtype),
            pltpu.SemaphoreType.DMA((4, pieces)),
            pltpu.SemaphoreType.DMA((4, pieces)),
        ],
        cost_estimate=cost(0, 4 * rows * width),
    )(w)


def partial_kernel(near_ref, w_ref, out_ref):
    out_ref[0] = dot_last(w_ref[0], near_ref[...]).astype(bf16)


def partial_products(near, w_mine):
    groups, inner, depth = w_mine.shape
    tokens = near.shape[0]
    return pl.pallas_call(
        partial_kernel,
        grid=(groups,),
        in_specs=[
            pl.BlockSpec((tokens, depth), lambda g: (0, 0)),
            pl.BlockSpec((1, inner, depth), lambda g: (g, 0, 0)),
        ],
        out_specs=pl.BlockSpec((1, inner, tokens), lambda g: (g, 0, 0)),
        out_shape=jax.ShapeDtypeStruct((groups, inner, tokens), bf16),
        compiler_params=small(),
        cost_estimate=cost(2 * groups * tokens * inner * depth, 4 << 20),
    )(near, w_mine)


def over_channels(rows, height):
    heads, tokens = rows.shape
    return jnp.concatenate(
        [jnp.broadcast_to(rows[h:h + 1], (height // heads, tokens)) for h in range(heads)], axis=0
    )


def state_kernel(parts_ref, rows_ref, c_ref, ends_ref, dy_ref, sent_ref):
    total = parts_ref[0].astype(f32)
    for y in range(1, parts_ref.shape[0]):
        total = total + parts_ref[y].astype(f32)
    dy = total.astype(bf16)
    dy_ref[...] = dy
    start = over_channels(jnp.exp(rows_ref[:4]), dy.shape[0])
    decayed = (dy.astype(f32) * start).astype(bf16)
    state = jnp.dot(decayed, c_ref[...], preferred_element_type=f32)
    blocks, rows, width = ends_ref.shape
    state = state.reshape(blocks, rows, width)
    sent_ref[...] = jnp.concatenate([state, ends_ref[...]], axis=1).astype(bf16)


def local_states(parts, rows, c_in, ends):
    _, inner, tokens = parts.shape
    blocks, height, width = ends.shape
    return pl.pallas_call(
        state_kernel,
        out_shape=(pltpu.HBM((inner, tokens), bf16), pltpu.HBM((blocks, 2 * height, width), bf16)),
        compiler_params=small(),
        cost_estimate=cost(2 * tokens * inner * width, 2 << 20),
    )(parts, rows, c_in, ends)


def widened(columns, width):
    tokens, heads = columns.shape
    return jnp.concatenate(
        [jnp.broadcast_to(columns[:, h:h + 1], (tokens, width // heads)) for h in range(heads)], axis=1
    )


def head_sums(values, heads):
    width = values.shape[1] // heads
    return [jnp.sum(values[:, h * width:(h + 1) * width], axis=1, keepdims=True) for h in range(heads)]


def as_rows(columns):
    tokens = columns[0].shape[0]
    lanes = lax.broadcasted_iota(jnp.int32, (tokens, 128), 1)
    spread = jnp.zeros((tokens, 128), f32)
    for k, column in enumerate(columns):
        spread = jnp.where(lanes == k, column, spread)
    return spread.T[:8]


def intra_kernel(dy_ref, x_ref, b_ref, c_ref, states_ref, rows_ref, skip_ref, wide_ref, half_ref, part_ref):
    width, tokens = dy_ref.shape
    head_dim = width // 4
    cum = rows_ref[:4]
    columns = rows_ref[...].T
    step = widened(columns[:, 4:], width)
    start = widened(jnp.exp(columns[:, :4]), width)
    b, c, states = b_ref[...], c_ref[...], states_ref[...]
    scores = dot_last(c, b)
    entered = dot_last(c, states)
    dy_wide = dy_ref[...].astype(f32).T
    dy = dy_wide.astype(bf16)
    x = x_ref[...].astype(f32)
    scaled = (x * step).astype(bf16)
    causal = lax.broadcasted_iota(jnp.int32, (tokens, tokens), 0) >= lax.broadcasted_iota(jnp.int32, (tokens, tokens), 1)
    total = jnp.zeros((tokens, tokens), f32)
    along, down, backs = [], [], []
    for h in range(4):
        mine = slice(h * head_dim, (h + 1) * head_dim)
        dy_h = dy[:, mine]
        gaps = jnp.minimum(columns[:, h:h + 1] - cum[h:h + 1], 0.0)
        mask = jnp.where(causal, jnp.exp(gaps), 0.0)
        weighed = (scores * mask).astype(bf16)
        backs.append(lax.dot_general(weighed, dy_h, (((0,), (0,)), ((), ())), preferred_element_type=f32))
        masked = dot_last(dy_h, scaled[:, mine]) * mask
        total = total + masked
        pairs = masked * scores
        along.append(jnp.sum(pairs, axis=1, keepdims=True))
        down.append(jnp.sum(pairs, axis=0, keepdims=True))
    total = total.astype(bf16)
    db = lax.dot_general(total, c, (((0,), (0,)), ((), ())), preferred_element_type=f32)
    dc = jnp.dot(total, b, preferred_element_type=f32)
    dc = dc + jnp.dot((dy_wide * start).astype(bf16), states, preferred_element_type=f32)
    back = jnp.concatenate(backs, axis=1)
    wide_ref[:width] = (step * back + skip_ref[...] * dy_wide).T
    wide_ref[width:] = db.T
    half_ref[:width] = x.T.astype(bf16)
    half_ref[width:] = dc.T.astype(bf16)
    entered = head_sums(start * dy_wide * entered, 4)
    rows = as_rows([a + e for a, e in zip(along, entered)] + head_sums(x * back, 4))
    part_ref[:8] = rows - jnp.concatenate(down + [jnp.zeros((4, tokens), f32)], axis=0)
    part_ref[8:] = jnp.broadcast_to(jnp.sum(dy_wide * x, axis=0, keepdims=True), (8, width))


def intra_terms(dy, x_in, b_in, c_in, states, rows, skip):
    width, tokens = dy.shape
    height = width + b_in.shape[1]
    return pl.pallas_call(
        intra_kernel,
        out_shape=(pltpu.HBM((height, tokens), f32), pltpu.HBM((height, tokens), bf16), pltpu.HBM((16, tokens), f32)),
        cost_estimate=cost(14 * tokens * tokens * width, 2 << 20),
    )(dy, x_in, b_in, c_in, states, rows, skip)


def dt_kernel(back_ref, half_ref, rows_ref, part_ref, carried_ref, states_ref, raw_ref, scal_ref, dt_ref, param_ref):
    width, tokens = back_ref.shape
    head_dim = width // 4
    cum, step = rows_ref[:4], rows_ref[4:]
    last = cum[:, tokens - 1:]
    rate, bias = scal_ref[:, 0:1], scal_ref[:, 1:2]
    dots = jnp.sum((half_ref[:width].astype(f32) * back_ref[...]).reshape(4, head_dim, tokens), axis=1)
    end_decay = jnp.exp(last - cum)
    end_terms = step * end_decay * dots
    carried = carried_ref[...].reshape(4, head_dim, -1)
    held = jnp.sum(carried * states_ref[...].astype(f32).reshape(4, head_dim, -1), axis=1)
    tail = jnp.sum(end_terms, axis=1, keepdims=True) + jnp.exp(last) * jnp.sum(held, axis=1, keepdims=True)
    below = lax.broadcasted_iota(jnp.int32, (tokens, tokens), 0) >= lax.broadcasted_iota(jnp.int32, (tokens, tokens), 1)
    step_grad = tail + jnp.dot(
        part_ref[:4] - end_terms, below.astype(f32), precision=lax.Precision.HIGHEST, preferred_element_type=f32
    )
    dt_sum = part_ref[4:8] + end_decay * dots - rate * step_grad
    dt = dt_sum * jax.nn.sigmoid(raw_ref[...] + bias)
    dt_ref[...] = dt
    lanes = lax.broadcasted_iota(jnp.int32, (4, width), 1)
    heads = lax.broadcasted_iota(jnp.int32, (4, width), 0)
    skip = jnp.sum(jnp.where(lanes // head_dim == heads, part_ref[8:9], 0.0), axis=1, keepdims=True)
    decays = jnp.sum(step_grad * (-rate * step), axis=1, keepdims=True)
    biases = jnp.sum(dt, axis=1, keepdims=True)
    lanes, heads = lanes[:, :128], heads[:, :128]
    placed = jnp.where(lanes == heads, decays, 0.0)
    placed = jnp.where(lanes == heads + 4, skip, placed)
    placed = jnp.where(lanes == heads + 8, biases, placed)
    param_ref[...] = jnp.sum(placed, axis=0, keepdims=True)


def dt_terms(back, half, rows, part, carried, states, dt_raw, scalars):
    return pl.pallas_call(
        dt_kernel,
        out_shape=(jax.ShapeDtypeStruct(dt_raw.shape, f32), jax.ShapeDtypeStruct((1, 128), f32)),
        cost_estimate=cost(1 << 22, 1 << 20),
    )(back, half, rows, part, carried, states, dt_raw, scalars)


def x_grad_kernel(carried_ref, b_ref, wide_hbm, half_hbm, rows_ref, sent_ref, back_ref, wide_ref, half_ref, sems):
    fetches = [
        pltpu.make_async_copy(wide_hbm, wide_ref, sems.at[0]),
        pltpu.make_async_copy(half_hbm, half_ref, sems.at[1]),
    ]
    for fetch in fetches:
        fetch.start()
    blocks, height, state_dim = carried_ref.shape
    width = blocks * height
    tokens = b_ref.shape[0]
    carried = carried_ref[...].reshape(width, state_dim).astype(bf16)
    back = dot_last(carried, b_ref[...])
    back_ref[...] = back
    cum = rows_ref[:4]
    weight = over_channels(rows_ref[4:] * jnp.exp(cum[:, tokens - 1:] - cum), width)
    for fetch in fetches:
        fetch.wait()
    x_grad = (wide_ref[:width] + weight * back).astype(bf16)
    x_end = (half_ref[:width].astype(f32) * weight).astype(bf16)
    entry = lax.dot_general(carried, x_end, (((0,), (0,)), ((), ())), preferred_element_type=f32)
    db = (wide_ref[width:] + entry).astype(bf16)
    rows = state_dim // 2
    for y in range(4):
        sent_ref[y, :width] = x_grad
        if y < 2:
            sent_ref[y, width:] = db[y * rows:(y + 1) * rows]
        else:
            sent_ref[y, width:] = half_ref[width + (y - 2) * rows:width + (y - 1) * rows]


def x_grads(carried, b_in, wide, half, rows):
    tokens, state_dim = b_in.shape
    inner = wide.shape[0] - state_dim
    at_vmem, at_hbm = pl.BlockSpec(memory_space=pltpu.VMEM), pl.BlockSpec(memory_space=pltpu.HBM)
    return pl.pallas_call(
        x_grad_kernel,
        in_specs=[at_vmem, at_vmem, at_hbm, at_hbm, at_vmem],
        scratch_shapes=[
            pltpu.VMEM(wide.shape, wide.dtype),
            pltpu.VMEM(half.shape, half.dtype),
            pltpu.SemaphoreType.DMA((2,)),
        ],
        out_shape=(pltpu.HBM((4, inner + state_dim // 2, tokens), bf16), pltpu.HBM((inner, tokens), f32)),
        cost_estimate=cost(4 * tokens * inner * 128, 2 << 20),
    )(carried, b_in, wide, half, rows)


def in_kernel(y_ref, got_ref, *refs):
    *w_refs, out_ref = refs
    quarter, inner = w_refs[0].shape
    feats = quarter // 4
    rows = out_ref.shape[1] - feats
    y = y_ref[0]
    x_grad = jnp.concatenate([got_ref[lax.rem(y + 4 - s, 4), :inner] for s in range(4)], axis=0)
    for z in range(4):
        at = slice(inner + z * rows, inner + (z + 1) * rows)
        bc = got_ref[0, at].astype(f32)
        for other in range(1, 4):
            bc = bc + got_ref[other, at].astype(f32)
        out_ref[z, feats:] = bc.astype(bf16)
        w = jnp.concatenate([w_ref[z * feats:(z + 1) * feats] for w_ref in w_refs], axis=1)
        out_ref[z, :feats] = jnp.dot(w, x_grad, preferred_element_type=f32).astype(bf16)


def in_products(y, got, pieces):
    quarter, inner = pieces[0].shape
    _, height, tokens = got.shape
    feats, rows = quarter // 4, (height - inner) // 4
    return pl.pallas_call(
        in_kernel,
        in_specs=[pl.BlockSpec(memory_space=pltpu.SMEM)] + [pl.BlockSpec(memory_space=pltpu.VMEM)] * 5,
        out_shape=pltpu.HBM((4, feats + rows, tokens), bf16),
        compiler_params=small(),
        cost_estimate=cost(8 * quarter * inner * tokens, 4 << 20),
    )(y.reshape(1), got, *pieces)


def sum_kernel(terms_ref, in_ref, bc_ref):
    feats = in_ref.shape[0]
    total = terms_ref[0].astype(f32)
    for z in range(1, 4):
        total = total + terms_ref[z].astype(f32)
    total = total.astype(bf16)
    in_ref[...] = total[:feats]
    bc_ref[...] = total[feats:]


def final_sums(terms, feats):
    _, height, tokens = terms.shape
    return pl.pallas_call(
        sum_kernel,
        out_shape=(
            jax.ShapeDtypeStruct((feats, tokens), bf16),
            jax.ShapeDtypeStruct((height - feats, tokens), bf16),
        ),
        compiler_params=small(),
        cost_estimate=cost(4 * height * tokens, 1 << 20),
    )(terms)


def shards(out_grad, x_in, b_in, c_in, dt_raw, dt_bias, a_log, d_skip, states, w_out, w_in):
    tokens_here, inner_here = x_in.shape
    group_heads = dt_raw.shape[0]
    head_dim = inner_here // group_heads
    state_dim = b_in.shape[1]
    blocks = lax.axis_size(SEQ)
    y = lax.axis_index("y")
    entry_state = states[0]

    w_out_y = lax.all_to_all(regrouped(w_out), "y", 0, 0)
    near = lax.all_gather(out_grad, "zh", axis=1, tiled=True)
    products = partial_products(near, w_out_y)
    w_in_held, products = lax.optimization_barrier((w_in, products))
    quarter = w_in.shape[0] // 4
    pieces = [lax.dynamic_slice_in_dim(w_in_held, lax.rem(y + s, 4) * quarter, quarter) for s in range(4)]
    held = [pieces[0]] + [lax.ppermute(pieces[s], "y", [(i, (i + s) % 4) for i in range(4)]) for s in range(1, 4)]
    head_parts = lax.all_to_all(products, "y", 0, 0)

    decay_rate = jnp.exp(a_log)
    step_size = jax.nn.softplus(dt_raw + dt_bias[:, None])
    log_step = -decay_rate[:, None] * step_size
    positions = jnp.arange(tokens_here)
    upto = (positions[:, None] <= positions[None, :]).astype(f32)
    cumlog = jnp.dot(log_step, upto, precision=lax.Precision.HIGHEST)
    rows = jnp.concatenate([cumlog, step_size], axis=0)
    ends = jnp.pad(three_parts(jnp.exp(cumlog[:, -1])), ((0, 0), (0, 5)))
    ends = jnp.broadcast_to(ends[:, None, :, None], (group_heads, blocks // group_heads, 8, state_dim))
    scalars = jnp.pad(jnp.stack([decay_rate, dt_bias], axis=1), ((0, 0), (0, 126)))
    skip = jnp.repeat(d_skip, head_dim)[None]
    dy, sent = local_states(head_parts, rows, c_in, ends.reshape(blocks, 8, state_dim))
    ahead = suffix_scan(lax.all_to_all(sent, SEQ, 0, 0))
    ahead, dy, held[2] = lax.optimization_barrier((ahead, dy, held[2]))
    wide, half, part = intra_terms(dy, x_in, b_in, c_in, entry_state, rows, skip)
    *held, carried, wide = lax.optimization_barrier((*held, lax.all_to_all(ahead, SEQ, 0, 0), wide))
    sent_y, back = x_grads(carried, b_in, wide, half, rows)
    got = lax.all_to_all(sent_y, "y", 0, 0)
    dt_grad, row = dt_terms(back, half, rows, part, carried, entry_state, dt_raw, scalars)
    row = row + lax.ppermute(row, "zl", [(i, i ^ 1) for i in range(4)])
    row, got = lax.optimization_barrier((row, got))
    terms = in_products(y, got, held)
    row, terms = lax.optimization_barrier((row, terms))
    for axis, flip in (("zl", 2), ("x", 1), ("x", 2), ("core", 1)):
        row = row + lax.ppermute(row, axis, [(i, i ^ flip) for i in range(lax.axis_size(axis))])
    in_grad, bc_grad = final_sums(lax.all_to_all(terms, "zh", 0, 0), w_in.shape[0] // 16)
    norm_scale = (blocks * tokens_here * head_dim) ** (-0.5)
    param_grad = row[0, : 3 * group_heads].reshape(3, group_heads) * norm_scale
    return (in_grad, bc_grad, dt_grad, param_grad)


def solution(mesh):
    fine = Mesh(mesh.devices.reshape(4, 4, 2, 4, 4), ("x", "zl", "core", "y", "zh"))
    return jax.shard_map(
        shards,
        mesh=fine,
        in_specs=(
            P(SEQ, HEAD),
            P(SEQ, HEAD),
            P(SEQ, None),
            P(SEQ, None),
            P(HEAD, SEQ),
            P(HEAD),
            P(HEAD),
            P(HEAD),
            P(SEQ, HEAD, None),
            P(HEAD, None),
            P(None, HEAD),
        ),
        out_specs=(P(HEAD, SEQ), P(HEAD, SEQ), P(HEAD, SEQ), P(None, HEAD)),
        check_vma=False,
    )
```

```python
import jax
import jax.numpy as jnp
from jax import lax
from jax.experimental import pallas as pl
from jax.experimental.pallas import tpu as pltpu
from jax.sharding import Mesh, PartitionSpec as P

SEQ = ("x", "zl", "core")
HEAD = ("y", "zh")
f32, bf16 = jnp.float32, jnp.bfloat16


def scan_kernel(parts_ref, carried_ref):
    blocks = parts_ref.shape[0]
    held = jnp.zeros(carried_ref.shape[1:], f32)
    for k in range(blocks - 1, -1, -1):
        carried_ref[k] = held
        wide = parts_ref[k].astype(f32)
        total = wide[8:9] + wide[9:10] + wide[10:11]
        held = total * held + wide[:8]


def suffix_scan(parts):
    blocks, _, width = parts.shape
    return pl.pallas_call(
        scan_kernel,
        out_shape=jax.ShapeDtypeStruct((blocks, 8, width), f32),
        compiler_params=small(),
        cost_estimate=cost(blocks * 3072, blocks * 8192),
    )(parts)


def three_parts(values):
    first = values.astype(bf16).astype(f32)
    second = (values - first).astype(bf16).astype(f32)
    return jnp.stack([first, second, values - first - second], axis=-1)


def cost(flops, moved):
    return pl.CostEstimate(flops=flops, bytes_accessed=moved, transcendentals=0)


def small(mib=16):
    return pltpu.CompilerParams(vmem_limit_bytes=mib << 20)


def dot_last(a, b):
    return lax.dot_general(a, b, (((1,), (1,)), ((), ())), preferred_element_type=f32)


def regroup_kernel(w_ref, out_ref, stage_ref, in_sems, out_sems):
    _, pieces, rows, part = stage_ref.shape
    steps = [(g, r) for g in range(4) for r in range(pieces)]

    def copy_in(g, r):
        source = w_ref.at[pl.ds(r * rows, rows), pl.ds(g * part, part)]
        return pltpu.make_async_copy(source, stage_ref.at[g, r], in_sems.at[g, r])

    def copy_out(g, r):
        return pltpu.make_async_copy(stage_ref.at[g, r], out_ref.at[g, pl.ds(r * rows, rows)], out_sems.at[g, r])

    for step in steps:
        copy_in(*step).start()
    for step in steps:
        copy_in(*step).wait()
        copy_out(*step).start()
    for step in steps:
        copy_out(*step).wait()


def regrouped(w):
    rows, width = w.shape
    pieces = 4
    return pl.pallas_call(
        regroup_kernel,
        in_specs=[pl.BlockSpec(memory_space=pl.ANY)],
        out_specs=pl.BlockSpec(memory_space=pl.ANY),
        out_shape=jax.ShapeDtypeStruct((4, rows, width // 4), w.dtype),
        scratch_shapes=[
            pltpu.VMEM((4, pieces, rows // pieces, width // 4), w.dtype),
            pltpu.SemaphoreType.DMA((4, pieces)),
            pltpu.SemaphoreType.DMA((4, pieces)),
        ],
        cost_estimate=cost(0, 4 * rows * width),
    )(w)


def partial_kernel(near_ref, w_ref, out_ref):
    groups, inner, depth = w_ref.shape
    out = dot_last(w_ref[...].reshape(groups * inner, depth), near_ref[...]).astype(bf16)
    out_ref[...] = out.reshape(out_ref.shape)


def partial_products(near, w_mine):
    groups, inner, depth = w_mine.shape
    tokens = near.shape[0]
    return pl.pallas_call(
        partial_kernel,
        out_shape=pltpu.HBM((groups, inner, tokens), bf16),
        compiler_params=small(),
        cost_estimate=cost(2 * groups * tokens * inner * depth, 4 << 20),
    )(near, w_mine)


def over_channels(rows, height):
    heads, tokens = rows.shape
    return jnp.concatenate(
        [jnp.broadcast_to(rows[h:h + 1], (height // heads, tokens)) for h in range(heads)], axis=0
    )


def state_kernel(parts_ref, rows_ref, c_ref, ends_ref, dy_ref, sent_ref):
    total = parts_ref[0].astype(f32)
    for y in range(1, parts_ref.shape[0]):
        total = total + parts_ref[y].astype(f32)
    dy = total.astype(bf16)
    dy_ref[...] = dy
    start = over_channels(jnp.exp(rows_ref[:4]), dy.shape[0])
    decayed = (dy.astype(f32) * start).astype(bf16)
    state = jnp.dot(decayed, c_ref[...], preferred_element_type=f32)
    blocks, rows, width = ends_ref.shape
    state = state.reshape(blocks, rows, width)
    sent_ref[...] = jnp.concatenate([state, ends_ref[...]], axis=1).astype(bf16)


def local_states(parts, rows, c_in, ends):
    _, inner, tokens = parts.shape
    blocks, height, width = ends.shape
    return pl.pallas_call(
        state_kernel,
        out_shape=(pltpu.HBM((inner, tokens), bf16), pltpu.HBM((blocks, 2 * height, width), bf16)),
        compiler_params=small(),
        cost_estimate=cost(2 * tokens * inner * width, 2 << 20),
    )(parts, rows, c_in, ends)


def widened(columns, width):
    tokens, heads = columns.shape
    return jnp.concatenate(
        [jnp.broadcast_to(columns[:, h:h + 1], (tokens, width // heads)) for h in range(heads)], axis=1
    )


def head_sums(values, heads):
    width = values.shape[1] // heads
    return [jnp.sum(values[:, h * width:(h + 1) * width], axis=1, keepdims=True) for h in range(heads)]


def as_rows(columns):
    tokens = columns[0].shape[0]
    lanes = lax.broadcasted_iota(jnp.int32, (tokens, 128), 1)
    spread = jnp.zeros((tokens, 128), f32)
    for k, column in enumerate(columns):
        spread = jnp.where(lanes == k, column, spread)
    return spread.T[:8]


def intra_kernel(dy_ref, x_ref, b_ref, c_ref, states_ref, rows_ref, skip_ref, wide_ref, half_ref, part_ref):
    width, tokens = dy_ref.shape
    head_dim = width // 4
    cum = rows_ref[:4]
    columns = rows_ref[:8].T
    step = widened(columns[:, 4:], width)
    start = widened(jnp.exp(columns[:, :4]), width)
    b, c, states = b_ref[...], c_ref[...], states_ref[...]
    scores = dot_last(c, b)
    entered = dot_last(c, states)
    dy_wide = dy_ref[...].astype(f32).T
    dy = dy_wide.astype(bf16)
    x = x_ref[...].astype(f32)
    scaled = (x * step).astype(bf16)
    causal = lax.broadcasted_iota(jnp.int32, (tokens, tokens), 0) >= lax.broadcasted_iota(jnp.int32, (tokens, tokens), 1)
    total = jnp.zeros((tokens, tokens), f32)
    along, down, backs = [], [], []
    for h in range(4):
        mine = slice(h * head_dim, (h + 1) * head_dim)
        dy_h = dy[:, mine]
        gaps = jnp.minimum(columns[:, h:h + 1] - cum[h:h + 1], 0.0)
        mask = jnp.where(causal, jnp.exp(gaps), 0.0)
        weighed = (scores * mask).astype(bf16)
        backs.append(lax.dot_general(weighed, dy_h, (((0,), (0,)), ((), ())), preferred_element_type=f32))
        masked = dot_last(dy_h, scaled[:, mine]) * mask
        total = total + masked
        pairs = masked * scores
        along.append(jnp.sum(pairs, axis=1, keepdims=True))
        down.append(jnp.sum(pairs, axis=0, keepdims=True))
    total = total.astype(bf16)
    db = lax.dot_general(total, c, (((0,), (0,)), ((), ())), preferred_element_type=f32)
    dc = jnp.dot(total, b, preferred_element_type=f32)
    dc = dc + jnp.dot((dy_wide * start).astype(bf16), states, preferred_element_type=f32)
    back = jnp.concatenate(backs, axis=1)
    wide_ref[:width] = (step * back + skip_ref[...] * dy_wide).T
    wide_ref[width:] = db.T
    half_ref[:width] = x.T.astype(bf16)
    half_ref[width:] = dc.T.astype(bf16)
    entered = head_sums(start * dy_wide * entered, 4)
    rows = as_rows([a + e for a, e in zip(along, entered)] + head_sums(x * back, 4))
    part_ref[:8] = rows - jnp.concatenate(down + [jnp.zeros((4, tokens), f32)], axis=0)
    part_ref[8:] = jnp.broadcast_to(jnp.sum(dy_wide * x, axis=0, keepdims=True), (8, width))


def intra_terms(dy, x_in, b_in, c_in, states, rows, skip):
    width, tokens = dy.shape
    height = width + b_in.shape[1]
    return pl.pallas_call(
        intra_kernel,
        out_shape=(jax.ShapeDtypeStruct((height, tokens), f32), jax.ShapeDtypeStruct((height, tokens), bf16), jax.ShapeDtypeStruct((16, tokens), f32)),
        compiler_params=small(),
        cost_estimate=cost(14 * tokens * tokens * width, 2 << 20),
    )(dy, x_in, b_in, c_in, states, rows, skip)


def dt_kernel(back_ref, half_ref, rows_ref, part_ref, carried_ref, states_ref, raw_ref, dt_ref, param_ref):
    width, tokens = back_ref.shape
    head_dim = width // 4
    cum, step = rows_ref[:4], rows_ref[4:8]
    last = cum[:, tokens - 1:]
    rate, bias = rows_ref[8:12], rows_ref[12:]
    dots = jnp.sum((half_ref[:width].astype(f32) * back_ref[...]).reshape(4, head_dim, tokens), axis=1)
    end_decay = jnp.exp(last - cum)
    end_terms = step * end_decay * dots
    carried = carried_ref[...].reshape(4, head_dim, -1)
    held = jnp.sum(carried * states_ref[...].astype(f32).reshape(4, head_dim, -1), axis=1)
    tail = jnp.sum(end_terms, axis=1, keepdims=True) + jnp.exp(last) * jnp.sum(held, axis=1, keepdims=True)
    below = lax.broadcasted_iota(jnp.int32, (tokens, tokens), 0) >= lax.broadcasted_iota(jnp.int32, (tokens, tokens), 1)
    step_grad = tail + jnp.dot(
        part_ref[:4] - end_terms, below.astype(f32), precision=lax.Precision.HIGHEST, preferred_element_type=f32
    )
    dt_sum = part_ref[4:8] + end_decay * dots - rate * step_grad
    dt = dt_sum * jax.nn.sigmoid(raw_ref[...] + bias)
    dt_ref[...] = dt
    lanes = lax.broadcasted_iota(jnp.int32, (4, width), 1)
    heads = lax.broadcasted_iota(jnp.int32, (4, width), 0)
    skip = jnp.sum(jnp.where(lanes // head_dim == heads, part_ref[8:9], 0.0), axis=1, keepdims=True)
    decays = jnp.sum(step_grad * (-rate * step), axis=1, keepdims=True)
    biases = jnp.sum(dt, axis=1, keepdims=True)
    lanes, heads = lanes[:, :128], heads[:, :128]
    placed = jnp.where(lanes == heads, decays, 0.0)
    placed = jnp.where(lanes == heads + 4, skip, placed)
    placed = jnp.where(lanes == heads + 8, biases, placed)
    param_ref[...] = jnp.sum(placed, axis=0, keepdims=True)


def dt_terms(back, half, rows, part, carried, states, dt_raw):
    return pl.pallas_call(
        dt_kernel,
        out_shape=(jax.ShapeDtypeStruct(dt_raw.shape, f32), jax.ShapeDtypeStruct((1, 128), f32)),
        cost_estimate=cost(1 << 22, 1 << 20),
    )(back, half, rows, part, carried, states, dt_raw)


def x_grad_kernel(carried_ref, b_ref, wide_ref, half_ref, rows_ref, sent_ref, back_ref):
    blocks, height, state_dim = carried_ref.shape
    width = blocks * height
    tokens = b_ref.shape[0]
    carried = carried_ref[...].reshape(width, state_dim).astype(bf16)
    back = dot_last(carried, b_ref[...])
    back_ref[...] = back
    cum = rows_ref[:4]
    weight = over_channels(rows_ref[4:8] * jnp.exp(cum[:, tokens - 1:] - cum), width)
    x_grad = (wide_ref[:width] + weight * back).astype(bf16)
    x_end = (half_ref[:width].astype(f32) * weight).astype(bf16)
    entry = lax.dot_general(carried, x_end, (((0,), (0,)), ((), ())), preferred_element_type=f32)
    db = (wide_ref[width:] + entry).astype(bf16)
    rows = state_dim // 2
    for y in range(4):
        sent_ref[y, :width] = x_grad
        if y < 2:
            sent_ref[y, width:] = db[y * rows:(y + 1) * rows]
        else:
            sent_ref[y, width:] = half_ref[width + (y - 2) * rows:width + (y - 1) * rows]


def x_grads(carried, b_in, wide, half, rows):
    tokens, state_dim = b_in.shape
    inner = wide.shape[0] - state_dim
    return pl.pallas_call(
        x_grad_kernel,
        out_shape=(pltpu.HBM((4, inner + state_dim // 2, tokens), bf16), pltpu.HBM((inner, tokens), f32)),
        compiler_params=small(),
        cost_estimate=cost(4 * tokens * inner * 128, 2 << 20),
    )(carried, b_in, wide, half, rows)


def in_kernel(y_ref, got_ref, *refs):
    *w_refs, out_ref = refs
    quarter, inner = w_refs[0].shape
    feats = quarter // 4
    rows = out_ref.shape[1] - feats
    y = y_ref[0]
    x_grad = jnp.concatenate([got_ref[lax.rem(y + 4 - s, 4), :inner] for s in range(4)], axis=0)
    for z in range(4):
        at = slice(inner + z * rows, inner + (z + 1) * rows)
        bc = got_ref[0, at].astype(f32)
        for other in range(1, 4):
            bc = bc + got_ref[other, at].astype(f32)
        out_ref[z, feats:] = bc.astype(bf16)
        w = jnp.concatenate([w_ref[z * feats:(z + 1) * feats] for w_ref in w_refs], axis=1)
        out_ref[z, :feats] = jnp.dot(w, x_grad, preferred_element_type=f32).astype(bf16)


def in_products(y, got, pieces):
    quarter, inner = pieces[0].shape
    _, height, tokens = got.shape
    feats, rows = quarter // 4, (height - inner) // 4
    return pl.pallas_call(
        in_kernel,
        in_specs=[pl.BlockSpec(memory_space=pltpu.SMEM)] + [pl.BlockSpec(memory_space=pltpu.VMEM)] * 5,
        out_shape=pltpu.HBM((4, feats + rows, tokens), bf16),
        compiler_params=small(),
        cost_estimate=cost(8 * quarter * inner * tokens, 4 << 20),
    )(y.reshape(1), got, *pieces)


def sum_kernel(terms_ref, in_ref, bc_ref):
    feats = in_ref.shape[0]
    total = terms_ref[0].astype(f32)
    for z in range(1, 4):
        total = total + terms_ref[z].astype(f32)
    total = total.astype(bf16)
    in_ref[...] = total[:feats]
    bc_ref[...] = total[feats:]


def final_sums(terms, feats):
    _, height, tokens = terms.shape
    return pl.pallas_call(
        sum_kernel,
        out_shape=(
            jax.ShapeDtypeStruct((feats, tokens), bf16),
            jax.ShapeDtypeStruct((height - feats, tokens), bf16),
        ),
        compiler_params=small(),
        cost_estimate=cost(4 * height * tokens, 1 << 20),
    )(terms)


def summed_over(row, axis):
    first, second, third = (lax.ppermute(row, axis, [(i, (i + s) % 4) for i in range(4)]) for s in (1, 2, 3))
    return (row + second) + (first + third)


def shards(out_grad, x_in, b_in, c_in, dt_raw, dt_bias, a_log, d_skip, states, w_out, w_in):
    tokens_here, inner_here = x_in.shape
    group_heads = dt_raw.shape[0]
    head_dim = inner_here // group_heads
    state_dim = b_in.shape[1]
    blocks = lax.axis_size(SEQ)
    y = lax.axis_index("y")
    entry_state = states[0]

    w_out_y = lax.all_to_all(regrouped(w_out), "y", 0, 0)
    near = lax.all_gather(out_grad, "zh", axis=1, tiled=True)
    products = partial_products(near, w_out_y)
    w_in_held, products = lax.optimization_barrier((w_in, products))
    quarter = w_in.shape[0] // 4
    pieces = [lax.dynamic_slice_in_dim(w_in_held, lax.rem(y + s, 4) * quarter, quarter) for s in range(4)]
    held = [pieces[0]] + [lax.ppermute(pieces[s], "y", [(i, (i + s) % 4) for i in range(4)]) for s in range(1, 4)]
    head_parts = lax.all_to_all(products, "y", 0, 0)

    decay_rate = jnp.exp(a_log)
    step_size = jax.nn.softplus(dt_raw + dt_bias[:, None])
    log_step = -decay_rate[:, None] * step_size
    positions = jnp.arange(tokens_here)
    upto = (positions[:, None] <= positions[None, :]).astype(f32)
    cumlog = jnp.dot(log_step, upto, precision=lax.Precision.HIGHEST)
    wide_scalars = jnp.broadcast_to(jnp.concatenate([decay_rate, dt_bias])[:, None], (2 * group_heads, tokens_here))
    rows = jnp.concatenate([cumlog, step_size, wide_scalars], axis=0)
    ends = jnp.pad(three_parts(jnp.exp(cumlog[:, -1])), ((0, 0), (0, 5)))
    ends = jnp.broadcast_to(ends[:, None, :, None], (group_heads, blocks // group_heads, 8, state_dim))
    skip = jnp.repeat(d_skip, head_dim)[None]
    dy, sent = local_states(head_parts, rows, c_in, ends.reshape(blocks, 8, state_dim))
    ahead = suffix_scan(lax.all_to_all(sent, SEQ, 0, 0))
    ahead, dy, held[2] = lax.optimization_barrier((ahead, dy, held[2]))
    wide, half, part = intra_terms(dy, x_in, b_in, c_in, entry_state, rows, skip)
    *held, carried = lax.optimization_barrier((*held, lax.all_to_all(ahead, SEQ, 0, 0)))
    sent_y, back = x_grads(carried, b_in, wide, half, rows)
    got = lax.all_to_all(sent_y, "y", 0, 0)
    dt_grad, row = dt_terms(back, half, rows, part, carried, entry_state, dt_raw)
    row = summed_over(row, "zl")
    row, got = lax.optimization_barrier((row, got))
    terms = in_products(y, got, held)
    row, terms = lax.optimization_barrier((row, terms))
    row = summed_over(row, "x")
    row = row + lax.ppermute(row, "core", [(0, 1), (1, 0)])
    in_grad, bc_grad = final_sums(lax.all_to_all(terms, "zh", 0, 0), w_in.shape[0] // 16)
    norm_scale = (blocks * tokens_here * head_dim) ** (-0.5)
    param_grad = row[0, : 3 * group_heads].reshape(3, group_heads) * norm_scale
    return (in_grad, bc_grad, dt_grad, param_grad)


def solution(mesh):
    fine = Mesh(mesh.devices.reshape(4, 4, 2, 4, 4), ("x", "zl", "core", "y", "zh"))
    return jax.shard_map(
        shards,
        mesh=fine,
        in_specs=(
            P(SEQ, HEAD),
            P(SEQ, HEAD),
            P(SEQ, None),
            P(SEQ, None),
            P(HEAD, SEQ),
            P(HEAD),
            P(HEAD),
            P(HEAD),
            P(SEQ, HEAD, None),
            P(HEAD, None),
            P(None, HEAD),
        ),
        out_specs=(P(HEAD, SEQ), P(HEAD, SEQ), P(HEAD, SEQ), P(None, HEAD)),
        check_vma=False,
    )
```

```python
import jax
import jax.numpy as jnp
from jax import lax
from jax.experimental import pallas as pl
from jax.experimental.pallas import tpu as pltpu
from jax.sharding import Mesh, PartitionSpec as P

SEQ = ("x", "zl", "core")
HEAD = ("y", "zh")
f32, bf16 = jnp.float32, jnp.bfloat16


def scan_kernel(parts_ref, carried_ref):
    blocks = parts_ref.shape[0]
    held = jnp.zeros(carried_ref.shape[1:], f32)
    for k in range(blocks - 1, -1, -1):
        carried_ref[k] = held
        wide = parts_ref[k].astype(f32)
        total = wide[8:9] + wide[9:10] + wide[10:11]
        held = total * held + wide[:8]


def suffix_scan(parts):
    blocks, _, width = parts.shape
    return pl.pallas_call(
        scan_kernel,
        out_shape=jax.ShapeDtypeStruct((blocks, 8, width), f32),
        compiler_params=small(),
        cost_estimate=cost(blocks * 3072, blocks * 8192),
    )(parts)


def three_parts(values):
    first = values.astype(bf16).astype(f32)
    second = (values - first).astype(bf16).astype(f32)
    return jnp.stack([first, second, values - first - second], axis=-1)


def cost(flops, moved):
    return pl.CostEstimate(flops=flops, bytes_accessed=moved, transcendentals=0)


def small(mib=16):
    return pltpu.CompilerParams(vmem_limit_bytes=mib << 20)


def dot_last(a, b):
    return lax.dot_general(a, b, (((1,), (1,)), ((), ())), preferred_element_type=f32)


def regroup_kernel(w_ref, out_ref, stage_ref, in_sems, out_sems):
    _, pieces, rows, part = stage_ref.shape
    steps = [(g, r) for g in range(4) for r in range(pieces)]

    def copy_in(g, r):
        source = w_ref.at[pl.ds(r * rows, rows), pl.ds(g * part, part)]
        return pltpu.make_async_copy(source, stage_ref.at[g, r], in_sems.at[g, r])

    def copy_out(g, r):
        return pltpu.make_async_copy(stage_ref.at[g, r], out_ref.at[g, pl.ds(r * rows, rows)], out_sems.at[g, r])

    for step in steps:
        copy_in(*step).start()
    for step in steps:
        copy_in(*step).wait()
        copy_out(*step).start()
    for step in steps:
        copy_out(*step).wait()


def regrouped(w):
    rows, width = w.shape
    pieces = 4
    return pl.pallas_call(
        regroup_kernel,
        in_specs=[pl.BlockSpec(memory_space=pl.ANY)],
        out_specs=pl.BlockSpec(memory_space=pl.ANY),
        out_shape=jax.ShapeDtypeStruct((4, rows, width // 4), w.dtype),
        scratch_shapes=[
            pltpu.VMEM((4, pieces, rows // pieces, width // 4), w.dtype),
            pltpu.SemaphoreType.DMA((4, pieces)),
            pltpu.SemaphoreType.DMA((4, pieces)),
        ],
        cost_estimate=cost(0, 4 * rows * width),
    )(w)


def partial_kernel(near_ref, w_ref, out_ref):
    groups, inner, depth = w_ref.shape
    out = dot_last(w_ref[...].reshape(groups * inner, depth), near_ref[...]).astype(bf16)
    out_ref[...] = out.reshape(out_ref.shape)


def partial_products(near, w_mine):
    groups, inner, depth = w_mine.shape
    tokens = near.shape[0]
    return pl.pallas_call(
        partial_kernel,
        out_shape=pltpu.HBM((groups, inner, tokens), bf16),
        compiler_params=small(),
        cost_estimate=cost(2 * groups * tokens * inner * depth, 4 << 20),
    )(near, w_mine)


def over_channels(rows, height):
    heads, tokens = rows.shape
    return jnp.concatenate(
        [jnp.broadcast_to(rows[h:h + 1], (height // heads, tokens)) for h in range(heads)], axis=0
    )


def state_kernel(parts_ref, rows_ref, c_ref, ends_ref, dy_ref, sent_ref):
    total = parts_ref[0].astype(f32)
    for y in range(1, parts_ref.shape[0]):
        total = total + parts_ref[y].astype(f32)
    dy = total.astype(bf16)
    dy_ref[...] = dy
    start = over_channels(jnp.exp(rows_ref[:4]), dy.shape[0])
    decayed = (dy.astype(f32) * start).astype(bf16)
    state = jnp.dot(decayed, c_ref[...], preferred_element_type=f32)
    blocks, rows, width = ends_ref.shape
    state = state.reshape(blocks, rows, width)
    sent_ref[...] = jnp.concatenate([state, ends_ref[...]], axis=1).astype(bf16)


def local_states(parts, rows, c_in, ends):
    _, inner, tokens = parts.shape
    blocks, height, width = ends.shape
    return pl.pallas_call(
        state_kernel,
        out_shape=(pltpu.HBM((inner, tokens), bf16), pltpu.HBM((blocks, 2 * height, width), bf16)),
        compiler_params=small(),
        cost_estimate=cost(2 * tokens * inner * width, 2 << 20),
    )(parts, rows, c_in, ends)


def widened(columns, width):
    tokens, heads = columns.shape
    return jnp.concatenate(
        [jnp.broadcast_to(columns[:, h:h + 1], (tokens, width // heads)) for h in range(heads)], axis=1
    )


def head_sums(values, heads):
    width = values.shape[1] // heads
    return [jnp.sum(values[:, h * width:(h + 1) * width], axis=1, keepdims=True) for h in range(heads)]


def as_rows(columns):
    tokens = columns[0].shape[0]
    lanes = lax.broadcasted_iota(jnp.int32, (tokens, 128), 1)
    spread = jnp.zeros((tokens, 128), f32)
    for k, column in enumerate(columns):
        spread = jnp.where(lanes == k, column, spread)
    return spread.T[:8]


def intra_kernel(dy_ref, x_ref, b_ref, c_ref, states_ref, rows_ref, skip_ref, wide_ref, half_ref, part_ref):
    width, tokens = dy_ref.shape
    head_dim = width // 4
    cum = rows_ref[:4]
    columns = rows_ref[:8].T
    step = widened(columns[:, 4:], width)
    start = widened(jnp.exp(columns[:, :4]), width)
    b, c, states = b_ref[...], c_ref[...], states_ref[...]
    scores = dot_last(c, b)
    entered = dot_last(c, states)
    dy_wide = dy_ref[...].astype(f32).T
    dy = dy_wide.astype(bf16)
    x = x_ref[...].astype(f32)
    scaled = (x * step).astype(bf16)
    causal = lax.broadcasted_iota(jnp.int32, (tokens, tokens), 0) >= lax.broadcasted_iota(jnp.int32, (tokens, tokens), 1)
    total = jnp.zeros((tokens, tokens), f32)
    along, down, backs = [], [], []
    for h in range(4):
        mine = slice(h * head_dim, (h + 1) * head_dim)
        dy_h = dy[:, mine]
        gaps = jnp.minimum(columns[:, h:h + 1] - cum[h:h + 1], 0.0)
        mask = jnp.where(causal, jnp.exp(gaps), 0.0)
        weighed = (scores * mask).astype(bf16)
        backs.append(lax.dot_general(weighed, dy_h, (((0,), (0,)), ((), ())), preferred_element_type=f32))
        masked = dot_last(dy_h, scaled[:, mine]) * mask
        total = total + masked
        pairs = masked * scores
        along.append(jnp.sum(pairs, axis=1, keepdims=True))
        down.append(jnp.sum(pairs, axis=0, keepdims=True))
    total = total.astype(bf16)
    db = lax.dot_general(total, c, (((0,), (0,)), ((), ())), preferred_element_type=f32)
    dc = jnp.dot(total, b, preferred_element_type=f32)
    dc = dc + jnp.dot((dy_wide * start).astype(bf16), states, preferred_element_type=f32)
    back = jnp.concatenate(backs, axis=1)
    wide_ref[:width] = (step * back + skip_ref[...] * dy_wide).T
    wide_ref[width:] = db.T
    half_ref[:width] = x.T.astype(bf16)
    half_ref[width:] = dc.T.astype(bf16)
    entered = head_sums(start * dy_wide * entered, 4)
    rows = as_rows([a + e for a, e in zip(along, entered)] + head_sums(x * back, 4))
    part_ref[:8] = rows - jnp.concatenate(down + [jnp.zeros((4, tokens), f32)], axis=0)
    part_ref[8:] = jnp.broadcast_to(jnp.sum(dy_wide * x, axis=0, keepdims=True), (8, width))


def intra_terms(dy, x_in, b_in, c_in, states, rows, skip):
    width, tokens = dy.shape
    height = width + b_in.shape[1]
    return pl.pallas_call(
        intra_kernel,
        out_shape=(jax.ShapeDtypeStruct((height, tokens), f32), jax.ShapeDtypeStruct((height, tokens), bf16), jax.ShapeDtypeStruct((16, tokens), f32)),
        compiler_params=small(),
        cost_estimate=cost(14 * tokens * tokens * width, 2 << 20),
    )(dy, x_in, b_in, c_in, states, rows, skip)


def dt_kernel(back_ref, half_ref, rows_ref, part_ref, carried_ref, states_ref, raw_ref, dt_ref, param_ref):
    width, tokens = back_ref.shape
    head_dim = width // 4
    cum, step = rows_ref[:4], rows_ref[4:8]
    last = cum[:, tokens - 1:]
    rate, bias = rows_ref[8:12], rows_ref[12:]
    dots = jnp.sum((half_ref[:width].astype(f32) * back_ref[...]).reshape(4, head_dim, tokens), axis=1)
    end_decay = jnp.exp(last - cum)
    end_terms = step * end_decay * dots
    carried = carried_ref[...].reshape(4, head_dim, -1)
    held = jnp.sum(carried * states_ref[...].astype(f32).reshape(4, head_dim, -1), axis=1)
    tail = jnp.sum(end_terms, axis=1, keepdims=True) + jnp.exp(last) * jnp.sum(held, axis=1, keepdims=True)
    below = lax.broadcasted_iota(jnp.int32, (tokens, tokens), 0) >= lax.broadcasted_iota(jnp.int32, (tokens, tokens), 1)
    step_grad = tail + jnp.dot(
        part_ref[:4] - end_terms, below.astype(f32), precision=lax.Precision.HIGHEST, preferred_element_type=f32
    )
    dt_sum = part_ref[4:8] + end_decay * dots - rate * step_grad
    dt = dt_sum * jax.nn.sigmoid(raw_ref[...] + bias)
    dt_ref[...] = dt
    lanes = lax.broadcasted_iota(jnp.int32, (4, width), 1)
    heads = lax.broadcasted_iota(jnp.int32, (4, width), 0)
    skip = jnp.sum(jnp.where(lanes // head_dim == heads, part_ref[8:9], 0.0), axis=1, keepdims=True)
    decays = jnp.sum(step_grad * (-rate * step), axis=1, keepdims=True)
    biases = jnp.sum(dt, axis=1, keepdims=True)
    lanes, heads = lanes[:, :128], heads[:, :128]
    placed = jnp.where(lanes == heads, decays, 0.0)
    placed = jnp.where(lanes == heads + 4, skip, placed)
    placed = jnp.where(lanes == heads + 8, biases, placed)
    param_ref[...] = jnp.sum(placed, axis=0, keepdims=True)


def dt_terms(back, half, rows, part, carried, states, dt_raw):
    return pl.pallas_call(
        dt_kernel,
        out_shape=(jax.ShapeDtypeStruct(dt_raw.shape, f32), jax.ShapeDtypeStruct((1, 128), f32)),
        cost_estimate=cost(1 << 22, 1 << 20),
    )(back, half, rows, part, carried, states, dt_raw)


def x_grad_kernel(carried_ref, b_ref, wide_ref, half_ref, rows_ref, sent_ref, back_ref):
    blocks, height, state_dim = carried_ref.shape
    width = blocks * height
    tokens = b_ref.shape[0]
    carried = carried_ref[...].reshape(width, state_dim).astype(bf16)
    back = dot_last(carried, b_ref[...])
    back_ref[...] = back
    cum = rows_ref[:4]
    weight = over_channels(rows_ref[4:8] * jnp.exp(cum[:, tokens - 1:] - cum), width)
    x_grad = (wide_ref[:width] + weight * back).astype(bf16)
    x_end = (half_ref[:width].astype(f32) * weight).astype(bf16)
    entry = lax.dot_general(carried, x_end, (((0,), (0,)), ((), ())), preferred_element_type=f32)
    db = (wide_ref[width:] + entry).astype(bf16)
    rows = state_dim // 2
    for y in range(4):
        sent_ref[y, :width] = x_grad
        if y < 2:
            sent_ref[y, width:] = db[y * rows:(y + 1) * rows]
        else:
            sent_ref[y, width:] = half_ref[width + (y - 2) * rows:width + (y - 1) * rows]


def x_grads(carried, b_in, wide, half, rows):
    tokens, state_dim = b_in.shape
    inner = wide.shape[0] - state_dim
    return pl.pallas_call(
        x_grad_kernel,
        out_shape=(pltpu.HBM((4, inner + state_dim // 2, tokens), bf16), pltpu.HBM((inner, tokens), f32)),
        compiler_params=small(),
        cost_estimate=cost(4 * tokens * inner * 128, 2 << 20),
    )(carried, b_in, wide, half, rows)


def in_kernel(y_ref, got_ref, *refs):
    *w_refs, out_ref = refs
    quarter, inner = w_refs[0].shape
    feats = quarter // 4
    rows = out_ref.shape[1] - feats
    y = y_ref[0]
    x_grad = jnp.concatenate([got_ref[lax.rem(y + 4 - s, 4), :inner] for s in range(4)], axis=0)
    for z in range(4):
        at = slice(inner + z * rows, inner + (z + 1) * rows)
        bc = got_ref[0, at].astype(f32)
        for other in range(1, 4):
            bc = bc + got_ref[other, at].astype(f32)
        out_ref[z, feats:] = bc.astype(bf16)
        w = jnp.concatenate([w_ref[z * feats:(z + 1) * feats] for w_ref in w_refs], axis=1)
        out_ref[z, :feats] = jnp.dot(w, x_grad, preferred_element_type=f32).astype(bf16)


def in_products(y, got, pieces):
    quarter, inner = pieces[0].shape
    _, height, tokens = got.shape
    feats, rows = quarter // 4, (height - inner) // 4
    return pl.pallas_call(
        in_kernel,
        in_specs=[pl.BlockSpec(memory_space=pltpu.SMEM)] + [pl.BlockSpec(memory_space=pltpu.VMEM)] * 5,
        out_shape=pltpu.HBM((4, feats + rows, tokens), bf16),
        compiler_params=small(),
        cost_estimate=cost(8 * quarter * inner * tokens, 4 << 20),
    )(y.reshape(1), got, *pieces)


def sum_kernel(terms_ref, in_ref, bc_ref):
    feats = in_ref.shape[0]
    total = terms_ref[0].astype(f32)
    for z in range(1, 4):
        total = total + terms_ref[z].astype(f32)
    total = total.astype(bf16)
    in_ref[...] = total[:feats]
    bc_ref[...] = total[feats:]


def final_sums(terms, feats):
    _, height, tokens = terms.shape
    return pl.pallas_call(
        sum_kernel,
        out_shape=(
            jax.ShapeDtypeStruct((feats, tokens), bf16),
            jax.ShapeDtypeStruct((height - feats, tokens), bf16),
        ),
        compiler_params=small(),
        cost_estimate=cost(4 * height * tokens, 1 << 20),
    )(terms)


def shifted(row, axis):
    return [lax.ppermute(row, axis, [(i, (i + s) % 4) for i in range(4)]) for s in (1, 2, 3)]


def paired(row, rounds):
    first, second, third = rounds
    return (row + second) + (first + third)


def shards(out_grad, x_in, b_in, c_in, dt_raw, dt_bias, a_log, d_skip, states, w_out, w_in):
    tokens_here, inner_here = x_in.shape
    group_heads = dt_raw.shape[0]
    head_dim = inner_here // group_heads
    state_dim = b_in.shape[1]
    blocks = lax.axis_size(SEQ)
    y = lax.axis_index("y")
    entry_state = states[0]

    w_out_y = lax.all_to_all(regrouped(w_out), "y", 0, 0)
    near = lax.all_gather(out_grad, "zh", axis=1, tiled=True)
    products = partial_products(near, w_out_y)
    w_in_held, products = lax.optimization_barrier((w_in, products))
    quarter = w_in.shape[0] // 4

    def exchanged(source, s):
        piece = lax.dynamic_slice_in_dim(source, lax.rem(y + s, 4) * quarter, quarter)
        return lax.ppermute(piece, "y", [(i, (i + s) % 4) for i in range(4)])

    head_parts = lax.all_to_all(products, "y", 0, 0)

    decay_rate = jnp.exp(a_log)
    step_size = jax.nn.softplus(dt_raw + dt_bias[:, None])
    log_step = -decay_rate[:, None] * step_size
    positions = jnp.arange(tokens_here)
    upto = (positions[:, None] <= positions[None, :]).astype(f32)
    cumlog = jnp.dot(log_step, upto, precision=lax.Precision.HIGHEST)
    wide_scalars = jnp.broadcast_to(jnp.concatenate([decay_rate, dt_bias])[:, None], (2 * group_heads, tokens_here))
    rows = jnp.concatenate([cumlog, step_size, wide_scalars], axis=0)
    ends = jnp.pad(three_parts(jnp.exp(cumlog[:, -1])), ((0, 0), (0, 5)))
    ends = jnp.broadcast_to(ends[:, None, :, None], (group_heads, blocks // group_heads, 8, state_dim))
    skip = jnp.repeat(d_skip, head_dim)[None]
    dy, sent = local_states(head_parts, rows, c_in, ends.reshape(blocks, 8, state_dim))
    ahead = suffix_scan(lax.all_to_all(sent, SEQ, 0, 0))
    held = [None, None, exchanged(w_in_held, 2), exchanged(w_in_held, 3)]
    ahead, dy, w_in_late = lax.optimization_barrier((ahead, dy, w_in_held))
    held[0] = lax.dynamic_slice_in_dim(w_in_late, y * quarter, quarter)
    held[1] = exchanged(w_in_late, 1)
    wide, half, part = intra_terms(dy, x_in, b_in, c_in, entry_state, rows, skip)
    held[2], held[3], carried = lax.optimization_barrier((held[2], held[3], lax.all_to_all(ahead, SEQ, 0, 0)))
    sent_y, back = x_grads(carried, b_in, wide, half, rows)
    got = lax.all_to_all(sent_y, "y", 0, 0)
    dt_grad, row = dt_terms(back, half, rows, part, carried, entry_state, dt_raw)
    *rounds, got = lax.optimization_barrier((*shifted(row, "zl"), got))
    terms = in_products(y, got, held)
    *rounds, terms = lax.optimization_barrier((*rounds, terms))
    row = paired(row, rounds)
    row = paired(row, shifted(row, "x"))
    row = row + lax.ppermute(row, "core", [(0, 1), (1, 0)])
    in_grad, bc_grad = final_sums(lax.all_to_all(terms, "zh", 0, 0), w_in.shape[0] // 16)
    norm_scale = (blocks * tokens_here * head_dim) ** (-0.5)
    param_grad = row[0, : 3 * group_heads].reshape(3, group_heads) * norm_scale
    return (in_grad, bc_grad, dt_grad, param_grad)


def solution(mesh):
    fine = Mesh(mesh.devices.reshape(4, 4, 2, 4, 4), ("x", "zl", "core", "y", "zh"))
    return jax.shard_map(
        shards,
        mesh=fine,
        in_specs=(
            P(SEQ, HEAD),
            P(SEQ, HEAD),
            P(SEQ, None),
            P(SEQ, None),
            P(HEAD, SEQ),
            P(HEAD),
            P(HEAD),
            P(HEAD),
            P(SEQ, HEAD, None),
            P(HEAD, None),
            P(None, HEAD),
        ),
        out_specs=(P(HEAD, SEQ), P(HEAD, SEQ), P(HEAD, SEQ), P(None, HEAD)),
        check_vma=False,
    )
```

```python
import jax
import jax.numpy as jnp
from jax import lax
from jax.experimental import pallas as pl
from jax.experimental.pallas import tpu as pltpu
from jax.sharding import Mesh, PartitionSpec as P

SEQ = ("x", "zl", "core")
HEAD = ("y", "zh")
f32, bf16 = jnp.float32, jnp.bfloat16


def scan_kernel(parts_ref, carried_ref):
    blocks = parts_ref.shape[0]
    held = jnp.zeros(carried_ref.shape[1:], f32)
    for k in range(blocks - 1, -1, -1):
        carried_ref[k] = held
        wide = parts_ref[k].astype(f32)
        total = wide[8:9] + wide[9:10] + wide[10:11]
        held = total * held + wide[:8]


def suffix_scan(parts):
    blocks, _, width = parts.shape
    return pl.pallas_call(
        scan_kernel,
        out_shape=jax.ShapeDtypeStruct((blocks, 8, width), f32),
        compiler_params=small(),
        cost_estimate=cost(blocks * 3072, blocks * 8192),
    )(parts)


def three_parts(values):
    first = values.astype(bf16).astype(f32)
    second = (values - first).astype(bf16).astype(f32)
    return jnp.stack([first, second, values - first - second], axis=-1)


def cost(flops, moved):
    return pl.CostEstimate(flops=flops, bytes_accessed=moved, transcendentals=0)


def small(mib=16):
    return pltpu.CompilerParams(vmem_limit_bytes=mib << 20)


def dot_last(a, b):
    return lax.dot_general(a, b, (((1,), (1,)), ((), ())), preferred_element_type=f32)


def regroup_kernel(w_ref, out_ref, stage_ref, in_sems, out_sems):
    _, pieces, rows, part = stage_ref.shape
    steps = [(g, r) for g in range(4) for r in range(pieces)]

    def copy_in(g, r):
        source = w_ref.at[pl.ds(r * rows, rows), pl.ds(g * part, part)]
        return pltpu.make_async_copy(source, stage_ref.at[g, r], in_sems.at[g, r])

    def copy_out(g, r):
        return pltpu.make_async_copy(stage_ref.at[g, r], out_ref.at[g, pl.ds(r * rows, rows)], out_sems.at[g, r])

    for step in steps:
        copy_in(*step).start()
    for step in steps:
        copy_in(*step).wait()
        copy_out(*step).start()
    for step in steps:
        copy_out(*step).wait()


def regrouped(w):
    rows, width = w.shape
    pieces = 4
    return pl.pallas_call(
        regroup_kernel,
        in_specs=[pl.BlockSpec(memory_space=pl.ANY)],
        out_specs=pl.BlockSpec(memory_space=pl.ANY),
        out_shape=jax.ShapeDtypeStruct((4, rows, width // 4), w.dtype),
        scratch_shapes=[
            pltpu.VMEM((4, pieces, rows // pieces, width // 4), w.dtype),
            pltpu.SemaphoreType.DMA((4, pieces)),
            pltpu.SemaphoreType.DMA((4, pieces)),
        ],
        cost_estimate=cost(0, 4 * rows * width),
    )(w)


def partial_kernel(near_ref, w_ref, out_ref):
    groups, inner, depth = w_ref.shape
    out = dot_last(w_ref[...].reshape(groups * inner, depth), near_ref[...]).astype(bf16)
    out_ref[...] = out.reshape(out_ref.shape)


def partial_products(near, w_mine):
    groups, inner, depth = w_mine.shape
    tokens = near.shape[0]
    return pl.pallas_call(
        partial_kernel,
        out_shape=pltpu.HBM((groups, inner, tokens), bf16),
        compiler_params=small(),
        cost_estimate=cost(2 * groups * tokens * inner * depth, 4 << 20),
    )(near, w_mine)


def over_channels(rows, height):
    heads, tokens = rows.shape
    return jnp.concatenate(
        [jnp.broadcast_to(rows[h:h + 1], (height // heads, tokens)) for h in range(heads)], axis=0
    )


def state_kernel(parts_ref, rows_ref, c_ref, ends_ref, dy_ref, sent_ref):
    total = parts_ref[0].astype(f32)
    for y in range(1, parts_ref.shape[0]):
        total = total + parts_ref[y].astype(f32)
    dy = total.astype(bf16)
    dy_ref[...] = dy
    start = over_channels(jnp.exp(rows_ref[:4]), dy.shape[0])
    decayed = (dy.astype(f32) * start).astype(bf16)
    state = jnp.dot(decayed, c_ref[...], preferred_element_type=f32)
    blocks, rows, width = ends_ref.shape
    state = state.reshape(blocks, rows, width)
    sent_ref[...] = jnp.concatenate([state, ends_ref[...]], axis=1).astype(bf16)


def local_states(parts, rows, c_in, ends):
    _, inner, tokens = parts.shape
    blocks, height, width = ends.shape
    return pl.pallas_call(
        state_kernel,
        out_shape=(pltpu.HBM((inner, tokens), bf16), pltpu.HBM((blocks, 2 * height, width), bf16)),
        compiler_params=small(),
        cost_estimate=cost(2 * tokens * inner * width, 2 << 20),
    )(parts, rows, c_in, ends)


def widened(columns, width):
    tokens, heads = columns.shape
    return jnp.concatenate(
        [jnp.broadcast_to(columns[:, h:h + 1], (tokens, width // heads)) for h in range(heads)], axis=1
    )


def head_sums(values, heads):
    width = values.shape[1] // heads
    return [jnp.sum(values[:, h * width:(h + 1) * width], axis=1, keepdims=True) for h in range(heads)]


def as_rows(columns):
    tokens = columns[0].shape[0]
    lanes = lax.broadcasted_iota(jnp.int32, (tokens, 128), 1)
    spread = jnp.zeros((tokens, 128), f32)
    for k, column in enumerate(columns):
        spread = jnp.where(lanes == k, column, spread)
    return spread.T[:8]


def intra_kernel(dy_ref, x_ref, b_ref, c_ref, states_ref, rows_ref, skip_ref, wide_ref, half_ref, part_ref):
    width, tokens = dy_ref.shape
    head_dim = width // 4
    cum = rows_ref[:4]
    columns = rows_ref[:8].T
    step = widened(columns[:, 4:], width)
    start = widened(jnp.exp(columns[:, :4]), width)
    b, c, states = b_ref[...], c_ref[...], states_ref[...]
    scores = dot_last(c, b)
    entered = dot_last(c, states)
    dy_wide = dy_ref[...].astype(f32).T
    dy = dy_wide.astype(bf16)
    x = x_ref[...].astype(f32)
    scaled = (x * step).astype(bf16)
    causal = lax.broadcasted_iota(jnp.int32, (tokens, tokens), 0) >= lax.broadcasted_iota(jnp.int32, (tokens, tokens), 1)
    total = jnp.zeros((tokens, tokens), f32)
    along, down, backs = [], [], []
    for h in range(4):
        mine = slice(h * head_dim, (h + 1) * head_dim)
        dy_h = dy[:, mine]
        gaps = jnp.minimum(columns[:, h:h + 1] - cum[h:h + 1], 0.0)
        mask = jnp.where(causal, jnp.exp(gaps), 0.0)
        weighed = (scores * mask).astype(bf16)
        backs.append(lax.dot_general(weighed, dy_h, (((0,), (0,)), ((), ())), preferred_element_type=f32))
        masked = dot_last(dy_h, scaled[:, mine]) * mask
        total = total + masked
        pairs = masked * scores
        along.append(jnp.sum(pairs, axis=1, keepdims=True))
        down.append(jnp.sum(pairs, axis=0, keepdims=True))
    total = total.astype(bf16)
    db = lax.dot_general(total, c, (((0,), (0,)), ((), ())), preferred_element_type=f32)
    dc = jnp.dot(total, b, preferred_element_type=f32)
    dc = dc + jnp.dot((dy_wide * start).astype(bf16), states, preferred_element_type=f32)
    back = jnp.concatenate(backs, axis=1)
    wide_ref[:width] = (step * back + skip_ref[...] * dy_wide).T
    wide_ref[width:] = db.T
    half_ref[:width] = x.T.astype(bf16)
    half_ref[width:] = dc.T.astype(bf16)
    entered = head_sums(start * dy_wide * entered, 4)
    rows = as_rows([a + e for a, e in zip(along, entered)] + head_sums(x * back, 4))
    part_ref[:8] = rows - jnp.concatenate(down + [jnp.zeros((4, tokens), f32)], axis=0)
    part_ref[8:] = jnp.broadcast_to(jnp.sum(dy_wide * x, axis=0, keepdims=True), (8, width))


def intra_terms(dy, x_in, b_in, c_in, states, rows, skip):
    width, tokens = dy.shape
    height = width + b_in.shape[1]
    return pl.pallas_call(
        intra_kernel,
        out_shape=(jax.ShapeDtypeStruct((height, tokens), f32), jax.ShapeDtypeStruct((height, tokens), bf16), jax.ShapeDtypeStruct((16, tokens), f32)),
        compiler_params=small(),
        cost_estimate=cost(14 * tokens * tokens * width, 2 << 20),
    )(dy, x_in, b_in, c_in, states, rows, skip)


def dt_rows(back, carried, half_ref, rows_ref, part_ref, states_ref, raw_ref, dt_ref, param_ref):
    width, tokens = back.shape
    head_dim = width // 4
    cum, step = rows_ref[:4], rows_ref[4:8]
    last = cum[:, tokens - 1:]
    rate, bias = rows_ref[8:12], rows_ref[12:]
    dots = jnp.sum((half_ref[:width].astype(f32) * back).reshape(4, head_dim, tokens), axis=1)
    end_decay = jnp.exp(last - cum)
    end_terms = step * end_decay * dots
    carried = carried.reshape(4, head_dim, -1)
    held = jnp.sum(carried * states_ref[...].astype(f32).reshape(4, head_dim, -1), axis=1)
    tail = jnp.sum(end_terms, axis=1, keepdims=True) + jnp.exp(last) * jnp.sum(held, axis=1, keepdims=True)
    below = lax.broadcasted_iota(jnp.int32, (tokens, tokens), 0) >= lax.broadcasted_iota(jnp.int32, (tokens, tokens), 1)
    step_grad = tail + jnp.dot(
        part_ref[:4] - end_terms, below.astype(f32), precision=lax.Precision.HIGHEST, preferred_element_type=f32
    )
    dt_sum = part_ref[4:8] + end_decay * dots - rate * step_grad
    dt = dt_sum * jax.nn.sigmoid(raw_ref[...] + bias)
    dt_ref[...] = dt
    lanes = lax.broadcasted_iota(jnp.int32, (4, width), 1)
    heads = lax.broadcasted_iota(jnp.int32, (4, width), 0)
    skip = jnp.sum(jnp.where(lanes // head_dim == heads, part_ref[8:9], 0.0), axis=1, keepdims=True)
    decays = jnp.sum(step_grad * (-rate * step), axis=1, keepdims=True)
    biases = jnp.sum(dt, axis=1, keepdims=True)
    lanes, heads = lanes[:, :128], heads[:, :128]
    placed = jnp.where(lanes == heads, decays, 0.0)
    placed = jnp.where(lanes == heads + 4, skip, placed)
    placed = jnp.where(lanes == heads + 8, biases, placed)
    param_ref[...] = jnp.sum(placed, axis=0, keepdims=True)


def x_grad_kernel(
    carried_ref, b_ref, wide_ref, half_ref, rows_ref, part_ref, states_ref, raw_ref, sent_ref, dt_ref, param_ref
):
    blocks, height, state_dim = carried_ref.shape
    width = blocks * height
    tokens = b_ref.shape[0]
    carried_wide = carried_ref[...].reshape(width, state_dim)
    carried = carried_wide.astype(bf16)
    back = dot_last(carried, b_ref[...])
    cum = rows_ref[:4]
    weight = over_channels(rows_ref[4:8] * jnp.exp(cum[:, tokens - 1:] - cum), width)
    x_grad = (wide_ref[:width] + weight * back).astype(bf16)
    x_end = (half_ref[:width].astype(f32) * weight).astype(bf16)
    entry = lax.dot_general(carried, x_end, (((0,), (0,)), ((), ())), preferred_element_type=f32)
    db = (wide_ref[width:] + entry).astype(bf16)
    rows = state_dim // 2
    for y in range(4):
        sent_ref[y, :width] = x_grad
        if y < 2:
            sent_ref[y, width:] = db[y * rows:(y + 1) * rows]
        else:
            sent_ref[y, width:] = half_ref[width + (y - 2) * rows:width + (y - 1) * rows]
    dt_rows(back, carried_wide, half_ref, rows_ref, part_ref, states_ref, raw_ref, dt_ref, param_ref)


def x_grads(carried, b_in, wide, half, rows, part, states, dt_raw):
    tokens, state_dim = b_in.shape
    inner = wide.shape[0] - state_dim
    return pl.pallas_call(
        x_grad_kernel,
        out_shape=(
            pltpu.HBM((4, inner + state_dim // 2, tokens), bf16),
            jax.ShapeDtypeStruct(dt_raw.shape, f32),
            jax.ShapeDtypeStruct((1, 128), f32),
        ),
        compiler_params=small(),
        cost_estimate=cost(4 * tokens * inner * 128, 2 << 20),
    )(carried, b_in, wide, half, rows, part, states, dt_raw)


def in_kernel(place_ref, got_ref, own_ref, near_ref, other_ref, half_ref, rest_ref, out_ref):
    quarter, inner = own_ref.shape
    feats = quarter // 4
    rows = out_ref.shape[1] - feats
    y, core = place_ref[0], place_ref[1]
    sources = [y, lax.rem(y + 3 + 2 * core, 4), lax.rem(y + 5 - 2 * core, 4), lax.rem(y + 2, 4)]
    x_grad = jnp.concatenate([got_ref[source, :inner] for source in sources], axis=0)
    for z in range(4):
        at = slice(inner + z * rows, inner + (z + 1) * rows)
        bc = got_ref[0, at].astype(f32)
        for other in range(1, 4):
            bc = bc + got_ref[other, at].astype(f32)
        out_ref[z, feats:] = bc.astype(bf16)
        mine = slice(z * feats, (z + 1) * feats)
        part = slice((z % 2) * feats, (z % 2 + 1) * feats)
        far = jnp.where(core == z // 2, half_ref[part], rest_ref[part])
        w = jnp.concatenate([own_ref[mine], near_ref[mine], other_ref[mine], far], axis=1)
        out_ref[z, :feats] = jnp.dot(w, x_grad, preferred_element_type=f32).astype(bf16)


def in_products(place, got, pieces):
    quarter, inner = pieces[0].shape
    _, height, tokens = got.shape
    feats, rows = quarter // 4, (height - inner) // 4
    return pl.pallas_call(
        in_kernel,
        in_specs=[pl.BlockSpec(memory_space=pltpu.SMEM)] + [pl.BlockSpec(memory_space=pltpu.VMEM)] * 6,
        out_shape=pltpu.HBM((4, feats + rows, tokens), bf16),
        compiler_params=small(),
        cost_estimate=cost(8 * quarter * inner * tokens, 4 << 20),
    )(place, got, *pieces)


def sum_kernel(terms_ref, in_ref, bc_ref):
    feats = in_ref.shape[0]
    total = terms_ref[0].astype(f32)
    for z in range(1, 4):
        total = total + terms_ref[z].astype(f32)
    total = total.astype(bf16)
    in_ref[...] = total[:feats]
    bc_ref[...] = total[feats:]


def final_sums(terms, feats):
    _, height, tokens = terms.shape
    return pl.pallas_call(
        sum_kernel,
        out_shape=(
            jax.ShapeDtypeStruct((feats, tokens), bf16),
            jax.ShapeDtypeStruct((height - feats, tokens), bf16),
        ),
        compiler_params=small(),
        cost_estimate=cost(4 * height * tokens, 1 << 20),
    )(terms)


def shifted(row, axis):
    return [lax.ppermute(row, axis, [(i, (i + s) % 4) for i in range(4)]) for s in (1, 2, 3)]


def paired(row, rounds):
    first, second, third = rounds
    return (row + second) + (first + third)


def shards(out_grad, x_in, b_in, c_in, dt_raw, dt_bias, a_log, d_skip, states, w_out, w_in):
    tokens_here, inner_here = x_in.shape
    group_heads = dt_raw.shape[0]
    head_dim = inner_here // group_heads
    state_dim = b_in.shape[1]
    blocks = lax.axis_size(SEQ)
    y = lax.axis_index("y")
    entry_state = states[0]

    w_out_y = lax.all_to_all(regrouped(w_out), "y", 0, 0)
    near = lax.all_gather(out_grad, "zh", axis=1, tiled=True)
    products = partial_products(near, w_out_y)
    w_in_held, products = lax.optimization_barrier((w_in, products))
    quarter = w_in.shape[0] // 4
    core = lax.axis_index("core")
    own = lax.dynamic_slice_in_dim(w_in_held, y * quarter, quarter)
    near_piece = lax.dynamic_slice_in_dim(w_in_held, lax.rem(y + 1 + 2 * core, 4) * quarter, quarter)
    far_at = lax.rem(y + 2, 4) * quarter + core * (quarter // 2)
    far_half = lax.dynamic_slice_in_dim(w_in_held, far_at, quarter // 2)
    head_parts = lax.all_to_all(products, "y", 0, 0)

    decay_rate = jnp.exp(a_log)
    step_size = jax.nn.softplus(dt_raw + dt_bias[:, None])
    log_step = -decay_rate[:, None] * step_size
    positions = jnp.arange(tokens_here)
    upto = (positions[:, None] <= positions[None, :]).astype(f32)
    cumlog = jnp.dot(log_step, upto, precision=lax.Precision.HIGHEST)
    wide_scalars = jnp.broadcast_to(jnp.concatenate([decay_rate, dt_bias])[:, None], (2 * group_heads, tokens_here))
    rows = jnp.concatenate([cumlog, step_size, wide_scalars], axis=0)
    ends = jnp.pad(three_parts(jnp.exp(cumlog[:, -1])), ((0, 0), (0, 5)))
    ends = jnp.broadcast_to(ends[:, None, :, None], (group_heads, blocks // group_heads, 8, state_dim))
    skip = jnp.repeat(d_skip, head_dim)[None]
    own, far_half, head_parts = lax.optimization_barrier((own, far_half, head_parts))
    one_step = [((c, i), (c, (i + 1 + 2 * c) % 4)) for c in range(2) for i in range(4)]
    near_piece = lax.ppermute(near_piece, ("core", "y"), [(4 * a[0] + a[1], 4 * b[0] + b[1]) for a, b in one_step])
    far_half = lax.ppermute(far_half, "y", [(i, (i + 2) % 4) for i in range(4)])
    swap = [(0, 1), (1, 0)]
    held = [own, near_piece, lax.ppermute(near_piece, "core", swap), far_half, lax.ppermute(far_half, "core", swap)]
    dy, sent = local_states(head_parts, rows, c_in, ends.reshape(blocks, 8, state_dim))
    ahead = suffix_scan(lax.all_to_all(sent, SEQ, 0, 0))
    ahead, dy = lax.optimization_barrier((ahead, dy))
    wide, half, part = intra_terms(dy, x_in, b_in, c_in, entry_state, rows, skip)
    *held, carried = lax.optimization_barrier((*held, lax.all_to_all(ahead, SEQ, 0, 0)))
    sent_y, dt_grad, row = x_grads(carried, b_in, wide, half, rows, part, entry_state, dt_raw)
    got = lax.all_to_all(sent_y, "y", 0, 0)
    *rounds, got = lax.optimization_barrier((*shifted(row, "zl"), got))
    terms = in_products(jnp.stack([y, core]), got, held)
    *rounds, terms = lax.optimization_barrier((*rounds, terms))
    row = paired(row, rounds)
    row = paired(row, shifted(row, "x"))
    row = row + lax.ppermute(row, "core", [(0, 1), (1, 0)])
    in_grad, bc_grad = final_sums(lax.all_to_all(terms, "zh", 0, 0), w_in.shape[0] // 16)
    norm_scale = (blocks * tokens_here * head_dim) ** (-0.5)
    param_grad = row[0, : 3 * group_heads].reshape(3, group_heads) * norm_scale
    return (in_grad, bc_grad, dt_grad, param_grad)


def solution(mesh):
    fine = Mesh(mesh.devices.reshape(4, 4, 2, 4, 4), ("x", "zl", "core", "y", "zh"))
    return jax.shard_map(
        shards,
        mesh=fine,
        in_specs=(
            P(SEQ, HEAD),
            P(SEQ, HEAD),
            P(SEQ, None),
            P(SEQ, None),
            P(HEAD, SEQ),
            P(HEAD),
            P(HEAD),
            P(HEAD),
            P(SEQ, HEAD, None),
            P(HEAD, None),
            P(None, HEAD),
        ),
        out_specs=(P(HEAD, SEQ), P(HEAD, SEQ), P(HEAD, SEQ), P(None, HEAD)),
        check_vma=False,
    )
```

```python
import jax
import jax.numpy as jnp
from jax import lax
from jax.experimental import pallas as pl
from jax.experimental.pallas import tpu as pltpu
from jax.sharding import Mesh, PartitionSpec as P

SEQ = ("x", "zl", "core")
HEAD = ("y", "zh")
f32, bf16 = jnp.float32, jnp.bfloat16


def scan_kernel(parts_ref, carried_ref):
    blocks = parts_ref.shape[0]
    held = jnp.zeros(carried_ref.shape[1:], f32)
    for k in range(blocks - 1, -1, -1):
        carried_ref[k] = held
        wide = parts_ref[k].astype(f32)
        total = wide[8:9] + wide[9:10] + wide[10:11]
        held = total * held + wide[:8]


def suffix_scan(parts):
    blocks, _, width = parts.shape
    return pl.pallas_call(
        scan_kernel,
        out_shape=jax.ShapeDtypeStruct((blocks, 8, width), f32),
        compiler_params=small(),
        cost_estimate=cost(blocks * 3072, blocks * 8192),
    )(parts)


def three_parts(values):
    first = values.astype(bf16).astype(f32)
    second = (values - first).astype(bf16).astype(f32)
    return jnp.stack([first, second, values - first - second], axis=-1)


def cost(flops, moved):
    return pl.CostEstimate(flops=flops, bytes_accessed=moved, transcendentals=0)


def small(mib=16):
    return pltpu.CompilerParams(vmem_limit_bytes=mib << 20)


def dot_last(a, b):
    return lax.dot_general(a, b, (((1,), (1,)), ((), ())), preferred_element_type=f32)


def regroup_kernel(w_ref, out_ref, stage_ref, in_sems, out_sems):
    _, pieces, rows, part = stage_ref.shape
    steps = [(g, r) for g in range(4) for r in range(pieces)]

    def copy_in(g, r):
        source = w_ref.at[pl.ds(r * rows, rows), pl.ds(g * part, part)]
        return pltpu.make_async_copy(source, stage_ref.at[g, r], in_sems.at[g, r])

    def copy_out(g, r):
        return pltpu.make_async_copy(stage_ref.at[g, r], out_ref.at[g, pl.ds(r * rows, rows)], out_sems.at[g, r])

    for step in steps:
        copy_in(*step).start()
    for step in steps:
        copy_in(*step).wait()
        copy_out(*step).start()
    for step in steps:
        copy_out(*step).wait()


def regrouped(w):
    rows, width = w.shape
    pieces = 4
    return pl.pallas_call(
        regroup_kernel,
        in_specs=[pl.BlockSpec(memory_space=pl.ANY)],
        out_specs=pl.BlockSpec(memory_space=pl.ANY),
        out_shape=jax.ShapeDtypeStruct((4, rows, width // 4), w.dtype),
        scratch_shapes=[
            pltpu.VMEM((4, pieces, rows // pieces, width // 4), w.dtype),
            pltpu.SemaphoreType.DMA((4, pieces)),
            pltpu.SemaphoreType.DMA((4, pieces)),
        ],
        cost_estimate=cost(0, 4 * rows * width),
    )(w)


def partial_kernel(near_ref, w_ref, out_ref):
    groups, inner, depth = w_ref.shape
    out = dot_last(w_ref[...].reshape(groups * inner, depth), near_ref[...]).astype(bf16)
    out_ref[...] = out.reshape(out_ref.shape)


def partial_products(near, w_mine):
    groups, inner, depth = w_mine.shape
    tokens = near.shape[0]
    return pl.pallas_call(
        partial_kernel,
        out_shape=pltpu.HBM((groups, inner, tokens), bf16),
        compiler_params=small(),
        cost_estimate=cost(2 * groups * tokens * inner * depth, 4 << 20),
    )(near, w_mine)


def over_channels(rows, height):
    heads, tokens = rows.shape
    return jnp.concatenate(
        [jnp.broadcast_to(rows[h:h + 1], (height // heads, tokens)) for h in range(heads)], axis=0
    )


def state_kernel(parts_ref, rows_ref, c_ref, ends_ref, dy_ref, sent_ref):
    total = parts_ref[0].astype(f32)
    for y in range(1, parts_ref.shape[0]):
        total = total + parts_ref[y].astype(f32)
    dy = total.astype(bf16)
    dy_ref[...] = dy
    start = over_channels(jnp.exp(rows_ref[:4]), dy.shape[0])
    decayed = (dy.astype(f32) * start).astype(bf16)
    state = jnp.dot(decayed, c_ref[...], preferred_element_type=f32)
    blocks, rows, width = ends_ref.shape
    state = state.reshape(blocks, rows, width)
    sent_ref[...] = jnp.concatenate([state, ends_ref[...]], axis=1).astype(bf16)


def local_states(parts, rows, c_in, ends):
    _, inner, tokens = parts.shape
    blocks, height, width = ends.shape
    return pl.pallas_call(
        state_kernel,
        out_shape=(pltpu.HBM((inner, tokens), bf16), pltpu.HBM((blocks, 2 * height, width), bf16)),
        compiler_params=small(),
        cost_estimate=cost(2 * tokens * inner * width, 2 << 20),
    )(parts, rows, c_in, ends)


def widened(columns, width):
    tokens, heads = columns.shape
    return jnp.concatenate(
        [jnp.broadcast_to(columns[:, h:h + 1], (tokens, width // heads)) for h in range(heads)], axis=1
    )


def head_sums(values, heads):
    width = values.shape[1] // heads
    return [jnp.sum(values[:, h * width:(h + 1) * width], axis=1, keepdims=True) for h in range(heads)]


def as_rows(columns):
    tokens = columns[0].shape[0]
    lanes = lax.broadcasted_iota(jnp.int32, (tokens, 128), 1)
    spread = jnp.zeros((tokens, 128), f32)
    for k, column in enumerate(columns):
        spread = jnp.where(lanes == k, column, spread)
    return spread.T[:8]


def intra_kernel(dy_ref, x_ref, b_ref, c_ref, states_ref, rows_ref, skip_ref, wide_ref, half_ref, part_ref):
    width, tokens = dy_ref.shape
    head_dim = width // 4
    cum = rows_ref[:4]
    columns = rows_ref[:8].T
    step = widened(columns[:, 4:], width)
    start = widened(jnp.exp(columns[:, :4]), width)
    b, c, states = b_ref[...], c_ref[...], states_ref[...]
    scores = dot_last(c, b)
    entered = dot_last(c, states)
    dy_wide = dy_ref[...].astype(f32).T
    dy = dy_wide.astype(bf16)
    x = x_ref[...].astype(f32)
    scaled = (x * step).astype(bf16)
    causal = lax.broadcasted_iota(jnp.int32, (tokens, tokens), 0) >= lax.broadcasted_iota(jnp.int32, (tokens, tokens), 1)
    total = jnp.zeros((tokens, tokens), f32)
    along, down, backs = [], [], []
    for h in range(4):
        mine = slice(h * head_dim, (h + 1) * head_dim)
        dy_h = dy[:, mine]
        gaps = jnp.minimum(columns[:, h:h + 1] - cum[h:h + 1], 0.0)
        mask = jnp.where(causal, jnp.exp(gaps), 0.0)
        weighed = (scores * mask).astype(bf16)
        backs.append(lax.dot_general(weighed, dy_h, (((0,), (0,)), ((), ())), preferred_element_type=f32))
        masked = dot_last(dy_h, scaled[:, mine]) * mask
        total = total + masked
        pairs = masked * scores
        along.append(jnp.sum(pairs, axis=1, keepdims=True))
        down.append(jnp.sum(pairs, axis=0, keepdims=True))
    total = total.astype(bf16)
    db = lax.dot_general(total, c, (((0,), (0,)), ((), ())), preferred_element_type=f32)
    dc = jnp.dot(total, b, preferred_element_type=f32)
    dc = dc + jnp.dot((dy_wide * start).astype(bf16), states, preferred_element_type=f32)
    back = jnp.concatenate(backs, axis=1)
    wide_ref[:width] = (step * back + skip_ref[...] * dy_wide).T
    wide_ref[width:] = db.T
    half_ref[:width] = x.T.astype(bf16)
    half_ref[width:] = dc.T.astype(bf16)
    entered = head_sums(start * dy_wide * entered, 4)
    rows = as_rows([a + e for a, e in zip(along, entered)] + head_sums(x * back, 4))
    part_ref[:8] = rows - jnp.concatenate(down + [jnp.zeros((4, tokens), f32)], axis=0)
    part_ref[8:] = jnp.broadcast_to(jnp.sum(dy_wide * x, axis=0, keepdims=True), (8, width))


def intra_terms(dy, x_in, b_in, c_in, states, rows, skip):
    width, tokens = dy.shape
    height = width + b_in.shape[1]
    return pl.pallas_call(
        intra_kernel,
        out_shape=(jax.ShapeDtypeStruct((height, tokens), f32), jax.ShapeDtypeStruct((height, tokens), bf16), jax.ShapeDtypeStruct((16, tokens), f32)),
        compiler_params=small(),
        cost_estimate=cost(14 * tokens * tokens * width, 2 << 20),
    )(dy, x_in, b_in, c_in, states, rows, skip)


def dt_rows(back, carried, half_ref, rows_ref, part_ref, states_ref, raw_ref, dt_ref, param_ref):
    width, tokens = back.shape
    head_dim = width // 4
    cum, step = rows_ref[:4], rows_ref[4:8]
    last = cum[:, tokens - 1:]
    rate, bias = rows_ref[8:12], rows_ref[12:]
    dots = jnp.sum((half_ref[:width].astype(f32) * back).reshape(4, head_dim, tokens), axis=1)
    end_decay = jnp.exp(last - cum)
    end_terms = step * end_decay * dots
    carried = carried.reshape(4, head_dim, -1)
    held = jnp.sum(carried * states_ref[...].astype(f32).reshape(4, head_dim, -1), axis=1)
    tail = jnp.sum(end_terms, axis=1, keepdims=True) + jnp.exp(last) * jnp.sum(held, axis=1, keepdims=True)
    below = lax.broadcasted_iota(jnp.int32, (tokens, tokens), 0) >= lax.broadcasted_iota(jnp.int32, (tokens, tokens), 1)
    step_grad = tail + jnp.dot(
        part_ref[:4] - end_terms, below.astype(f32), precision=lax.Precision.HIGHEST, preferred_element_type=f32
    )
    dt_sum = part_ref[4:8] + end_decay * dots - rate * step_grad
    dt = dt_sum * jax.nn.sigmoid(raw_ref[...] + bias)
    dt_ref[...] = dt
    lanes = lax.broadcasted_iota(jnp.int32, (4, width), 1)
    heads = lax.broadcasted_iota(jnp.int32, (4, width), 0)
    skip = jnp.sum(jnp.where(lanes // head_dim == heads, part_ref[8:9], 0.0), axis=1, keepdims=True)
    decays = jnp.sum(step_grad * (-rate * step), axis=1, keepdims=True)
    biases = jnp.sum(dt, axis=1, keepdims=True)
    lanes, heads = lanes[:, :128], heads[:, :128]
    placed = jnp.where(lanes == heads, decays, 0.0)
    placed = jnp.where(lanes == heads + 4, skip, placed)
    placed = jnp.where(lanes == heads + 8, biases, placed)
    param_ref[...] = jnp.sum(placed, axis=0, keepdims=True)


def x_grad_kernel(
    carried_ref, b_ref, wide_ref, half_ref, rows_ref, part_ref, states_ref, raw_ref, sent_ref, dt_ref, param_ref
):
    blocks, height, state_dim = carried_ref.shape
    width = blocks * height
    tokens = b_ref.shape[0]
    carried_wide = carried_ref[...].reshape(width, state_dim)
    carried = carried_wide.astype(bf16)
    back = dot_last(carried, b_ref[...])
    cum = rows_ref[:4]
    weight = over_channels(rows_ref[4:8] * jnp.exp(cum[:, tokens - 1:] - cum), width)
    x_grad = (wide_ref[:width] + weight * back).astype(bf16)
    x_end = (half_ref[:width].astype(f32) * weight).astype(bf16)
    entry = lax.dot_general(carried, x_end, (((0,), (0,)), ((), ())), preferred_element_type=f32)
    db = (wide_ref[width:] + entry).astype(bf16)
    rows = state_dim // 2
    for y in range(4):
        sent_ref[y, :width] = x_grad
        if y < 2:
            sent_ref[y, width:] = db[y * rows:(y + 1) * rows]
        else:
            sent_ref[y, width:] = half_ref[width + (y - 2) * rows:width + (y - 1) * rows]
    dt_rows(back, carried_wide, half_ref, rows_ref, part_ref, states_ref, raw_ref, dt_ref, param_ref)


def x_grads(carried, b_in, wide, half, rows, part, states, dt_raw):
    tokens, state_dim = b_in.shape
    inner = wide.shape[0] - state_dim
    return pl.pallas_call(
        x_grad_kernel,
        out_shape=(
            pltpu.HBM((4, inner + state_dim // 2, tokens), bf16),
            jax.ShapeDtypeStruct(dt_raw.shape, f32),
            jax.ShapeDtypeStruct((1, 128), f32),
        ),
        compiler_params=small(),
        cost_estimate=cost(4 * tokens * inner * 128, 2 << 20),
    )(carried, b_in, wide, half, rows, part, states, dt_raw)


def in_kernel(place_ref, got_ref, own_ref, near_ref, other_ref, half_ref, rest_ref, *out_refs):
    quarter, inner = own_ref.shape
    feats = quarter // 4
    rows = out_refs[0].shape[0] - feats
    y, core, zh = place_ref[0], place_ref[1], place_ref[2]
    sources = [y, lax.rem(y + 3 + 2 * core, 4), lax.rem(y + 5 - 2 * core, 4), lax.rem(y + 2, 4)]
    x_grad = jnp.concatenate([got_ref[source, :inner] for source in sources], axis=0)
    targets = [zh, lax.rem(zh + 1 + 2 * core, 4), lax.rem(zh + 2, 4), lax.rem(zh + 3 + 2 * core, 4)]
    for z, out_ref in zip(targets, out_refs):
        at = pl.ds(pl.multiple_of(inner + z * rows, rows), rows)
        bc = got_ref[0, at].astype(f32)
        for other in range(1, 4):
            bc = bc + got_ref[other, at].astype(f32)
        out_ref[feats:] = bc.astype(bf16)
        mine = pl.ds(pl.multiple_of(z * feats, feats), feats)
        part = pl.ds(pl.multiple_of(lax.rem(z, 2) * feats, feats), feats)
        far = jnp.where(core == z // 2, half_ref[part], rest_ref[part])
        w = jnp.concatenate([own_ref[mine], near_ref[mine], other_ref[mine], far], axis=1)
        out_ref[:feats] = jnp.dot(w, x_grad, preferred_element_type=f32).astype(bf16)


def in_products(place, got, pieces):
    quarter, inner = pieces[0].shape
    _, height, tokens = got.shape
    feats, rows = quarter // 4, (height - inner) // 4
    return pl.pallas_call(
        in_kernel,
        in_specs=[pl.BlockSpec(memory_space=pltpu.SMEM)] + [pl.BlockSpec(memory_space=pltpu.VMEM)] * 6,
        out_shape=[jax.ShapeDtypeStruct((feats + rows, tokens), bf16)] * 4,
        compiler_params=small(),
        cost_estimate=cost(8 * quarter * inner * tokens, 4 << 20),
    )(place, got, *pieces)


def sum_kernel(own_ref, chain_ref, direct_ref, in_ref, bc_ref):
    feats = in_ref.shape[0]
    total = own_ref[...].astype(f32) + chain_ref[...].astype(f32) + direct_ref[...].astype(f32)
    total = total.astype(bf16)
    in_ref[...] = total[:feats]
    bc_ref[...] = total[feats:]


def final_sums(own, chain, direct, feats):
    height, tokens = own.shape
    return pl.pallas_call(
        sum_kernel,
        out_shape=(
            jax.ShapeDtypeStruct((feats, tokens), bf16),
            jax.ShapeDtypeStruct((height - feats, tokens), bf16),
        ),
        compiler_params=small(),
        cost_estimate=cost(4 * height * tokens, 1 << 20),
    )(own, chain, direct)


def ring_step(value, axis, way):
    pairs = [(c, i, (i + (way if c == 0 else -way)) % 4) for c in range(2) for i in range(4)]
    return lax.ppermute(value, ("core", axis), [(4 * c + i, 4 * c + j) for c, i, j in pairs])


def shifted(row, axis):
    return [lax.ppermute(row, axis, [(i, (i + s) % 4) for i in range(4)]) for s in (1, 2, 3)]


def paired(row, rounds):
    first, second, third = rounds
    return (row + second) + (first + third)


def shards(out_grad, x_in, b_in, c_in, dt_raw, dt_bias, a_log, d_skip, states, w_out, w_in):
    tokens_here, inner_here = x_in.shape
    group_heads = dt_raw.shape[0]
    head_dim = inner_here // group_heads
    state_dim = b_in.shape[1]
    blocks = lax.axis_size(SEQ)
    y = lax.axis_index("y")
    entry_state = states[0]

    w_out_y = lax.all_to_all(regrouped(w_out), "y", 0, 0)
    near = lax.all_gather(out_grad, "zh", axis=1, tiled=True)
    products = partial_products(near, w_out_y)
    w_in_held, products = lax.optimization_barrier((w_in, products))
    quarter = w_in.shape[0] // 4
    core = lax.axis_index("core")
    own = lax.dynamic_slice_in_dim(w_in_held, y * quarter, quarter)
    near_piece = lax.dynamic_slice_in_dim(w_in_held, lax.rem(y + 1 + 2 * core, 4) * quarter, quarter)
    far_at = lax.rem(y + 2, 4) * quarter + core * (quarter // 2)
    far_half = lax.dynamic_slice_in_dim(w_in_held, far_at, quarter // 2)
    head_parts = lax.all_to_all(products, "y", 0, 0)

    decay_rate = jnp.exp(a_log)
    step_size = jax.nn.softplus(dt_raw + dt_bias[:, None])
    log_step = -decay_rate[:, None] * step_size
    positions = jnp.arange(tokens_here)
    upto = (positions[:, None] <= positions[None, :]).astype(f32)
    cumlog = jnp.dot(log_step, upto, precision=lax.Precision.HIGHEST)
    wide_scalars = jnp.broadcast_to(jnp.concatenate([decay_rate, dt_bias])[:, None], (2 * group_heads, tokens_here))
    rows = jnp.concatenate([cumlog, step_size, wide_scalars], axis=0)
    ends = jnp.pad(three_parts(jnp.exp(cumlog[:, -1])), ((0, 0), (0, 5)))
    ends = jnp.broadcast_to(ends[:, None, :, None], (group_heads, blocks // group_heads, 8, state_dim))
    skip = jnp.repeat(d_skip, head_dim)[None]
    own, far_half, head_parts = lax.optimization_barrier((own, far_half, head_parts))
    one_step = [((c, i), (c, (i + 1 + 2 * c) % 4)) for c in range(2) for i in range(4)]
    near_piece = lax.ppermute(near_piece, ("core", "y"), [(4 * a[0] + a[1], 4 * b[0] + b[1]) for a, b in one_step])
    far_half = lax.ppermute(far_half, "y", [(i, (i + 2) % 4) for i in range(4)])
    swap = [(0, 1), (1, 0)]
    held = [own, near_piece, lax.ppermute(near_piece, "core", swap), far_half, lax.ppermute(far_half, "core", swap)]
    dy, sent = local_states(head_parts, rows, c_in, ends.reshape(blocks, 8, state_dim))
    ahead = suffix_scan(lax.all_to_all(sent, SEQ, 0, 0))
    ahead, dy = lax.optimization_barrier((ahead, dy))
    wide, half, part = intra_terms(dy, x_in, b_in, c_in, entry_state, rows, skip)
    *held, carried = lax.optimization_barrier((*held, lax.all_to_all(ahead, SEQ, 0, 0)))
    sent_y, dt_grad, row = x_grads(carried, b_in, wide, half, rows, part, entry_state, dt_raw)
    got = lax.all_to_all(sent_y, "y", 0, 0)
    *rounds, got = lax.optimization_barrier((*shifted(row, "zl"), got))
    place = jnp.stack([y, core, lax.axis_index("zh")])
    mine, near_terms, far_terms, direct_terms = in_products(place, got, held)
    relayed = ring_step(far_terms, "zh", 1)
    direct = ring_step(direct_terms, "zh", -1)
    row = paired(row, rounds)
    relayed, direct, *rounds = lax.optimization_barrier((relayed, direct, *shifted(row, "x")))
    onward = (near_terms.astype(f32) + relayed.astype(f32)).astype(bf16)
    *rounds, onward = lax.optimization_barrier((*rounds, onward))
    chain = ring_step(onward, "zh", 1)
    row = paired(row, rounds)
    row = row + lax.ppermute(row, "core", [(0, 1), (1, 0)])
    in_grad, bc_grad = final_sums(mine, chain, direct, w_in.shape[0] // 16)
    norm_scale = (blocks * tokens_here * head_dim) ** (-0.5)
    param_grad = row[0, : 3 * group_heads].reshape(3, group_heads) * norm_scale
    return (in_grad, bc_grad, dt_grad, param_grad)


def solution(mesh):
    fine = Mesh(mesh.devices.reshape(4, 4, 2, 4, 4), ("x", "zl", "core", "y", "zh"))
    return jax.shard_map(
        shards,
        mesh=fine,
        in_specs=(
            P(SEQ, HEAD),
            P(SEQ, HEAD),
            P(SEQ, None),
            P(SEQ, None),
            P(HEAD, SEQ),
            P(HEAD),
            P(HEAD),
            P(HEAD),
            P(SEQ, HEAD, None),
            P(HEAD, None),
            P(None, HEAD),
        ),
        out_specs=(P(HEAD, SEQ), P(HEAD, SEQ), P(HEAD, SEQ), P(None, HEAD)),
        check_vma=False,
    )
```

```python
import jax
import jax.numpy as jnp
from jax import lax
from jax.experimental import pallas as pl
from jax.experimental.pallas import tpu as pltpu
from jax.sharding import Mesh, PartitionSpec as P

SEQ = ("x", "zl", "core")
HEAD = ("y", "zh")
f32, bf16 = jnp.float32, jnp.bfloat16


def scan_kernel(parts_ref, carried_ref):
    blocks = parts_ref.shape[0]
    held = jnp.zeros(carried_ref.shape[1:], f32)
    for k in range(blocks - 1, -1, -1):
        carried_ref[k] = held
        wide = parts_ref[k].astype(f32)
        total = wide[8:9] + wide[9:10] + wide[10:11]
        held = total * held + wide[:8]


def suffix_scan(parts):
    blocks, _, width = parts.shape
    return pl.pallas_call(
        scan_kernel,
        out_shape=jax.ShapeDtypeStruct((blocks, 8, width), f32),
        compiler_params=small(),
        cost_estimate=cost(blocks * 3072, blocks * 8192),
    )(parts)


def three_parts(values):
    first = values.astype(bf16).astype(f32)
    second = (values - first).astype(bf16).astype(f32)
    return jnp.stack([first, second, values - first - second], axis=-1)


def cost(flops, moved):
    return pl.CostEstimate(flops=flops, bytes_accessed=moved, transcendentals=0)


def small(mib=16):
    return pltpu.CompilerParams(vmem_limit_bytes=mib << 20)


def dot_last(a, b):
    return lax.dot_general(a, b, (((1,), (1,)), ((), ())), preferred_element_type=f32)


def regroup_kernel(w_ref, out_ref, stage_ref, in_sems, out_sems):
    _, pieces, rows, part = stage_ref.shape
    steps = [(g, r) for g in range(4) for r in range(pieces)]

    def copy_in(g, r):
        source = w_ref.at[pl.ds(r * rows, rows), pl.ds(g * part, part)]
        return pltpu.make_async_copy(source, stage_ref.at[g, r], in_sems.at[g, r])

    def copy_out(g, r):
        return pltpu.make_async_copy(stage_ref.at[g, r], out_ref.at[g, pl.ds(r * rows, rows)], out_sems.at[g, r])

    for step in steps:
        copy_in(*step).start()
    for step in steps:
        copy_in(*step).wait()
        copy_out(*step).start()
    for step in steps:
        copy_out(*step).wait()


def regrouped(w):
    rows, width = w.shape
    pieces = 4
    return pl.pallas_call(
        regroup_kernel,
        in_specs=[pl.BlockSpec(memory_space=pl.ANY)],
        out_specs=pl.BlockSpec(memory_space=pl.ANY),
        out_shape=jax.ShapeDtypeStruct((4, rows, width // 4), w.dtype),
        scratch_shapes=[
            pltpu.VMEM((4, pieces, rows // pieces, width // 4), w.dtype),
            pltpu.SemaphoreType.DMA((4, pieces)),
            pltpu.SemaphoreType.DMA((4, pieces)),
        ],
        cost_estimate=cost(0, 4 * rows * width),
    )(w)


def partial_kernel(near_ref, w_ref, out_ref):
    groups, inner, depth = w_ref.shape
    out = dot_last(w_ref[...].reshape(groups * inner, depth), near_ref[...]).astype(bf16)
    out_ref[...] = out.reshape(out_ref.shape)


def partial_products(near, w_mine):
    groups, inner, depth = w_mine.shape
    tokens = near.shape[0]
    return pl.pallas_call(
        partial_kernel,
        out_shape=pltpu.HBM((groups, inner, tokens), bf16),
        compiler_params=small(),
        cost_estimate=cost(2 * groups * tokens * inner * depth, 4 << 20),
    )(near, w_mine)


def over_channels(rows, height):
    heads, tokens = rows.shape
    return jnp.concatenate(
        [jnp.broadcast_to(rows[h:h + 1], (height // heads, tokens)) for h in range(heads)], axis=0
    )


def state_kernel(parts_ref, rows_ref, c_ref, ends_ref, dy_ref, sent_ref):
    total = parts_ref[0].astype(f32)
    for y in range(1, parts_ref.shape[0]):
        total = total + parts_ref[y].astype(f32)
    dy = total.astype(bf16)
    dy_ref[...] = dy
    start = over_channels(jnp.exp(rows_ref[:4]), dy.shape[0])
    decayed = (dy.astype(f32) * start).astype(bf16)
    state = jnp.dot(decayed, c_ref[...], preferred_element_type=f32)
    blocks, rows, width = ends_ref.shape
    state = state.reshape(blocks, rows, width)
    sent_ref[...] = jnp.concatenate([state, ends_ref[...]], axis=1).astype(bf16)


def local_states(parts, rows, c_in, ends):
    _, inner, tokens = parts.shape
    blocks, height, width = ends.shape
    return pl.pallas_call(
        state_kernel,
        out_shape=(pltpu.HBM((inner, tokens), bf16), pltpu.HBM((blocks, 2 * height, width), bf16)),
        compiler_params=small(),
        cost_estimate=cost(2 * tokens * inner * width, 2 << 20),
    )(parts, rows, c_in, ends)


def widened(columns, width):
    tokens, heads = columns.shape
    return jnp.concatenate(
        [jnp.broadcast_to(columns[:, h:h + 1], (tokens, width // heads)) for h in range(heads)], axis=1
    )


def head_sums(values, heads):
    width = values.shape[1] // heads
    return [jnp.sum(values[:, h * width:(h + 1) * width], axis=1, keepdims=True) for h in range(heads)]


def as_rows(columns):
    tokens = columns[0].shape[0]
    lanes = lax.broadcasted_iota(jnp.int32, (tokens, 128), 1)
    spread = jnp.zeros((tokens, 128), f32)
    for k, column in enumerate(columns):
        spread = jnp.where(lanes == k, column, spread)
    return spread.T[:8]


def intra_kernel(dy_ref, x_ref, b_ref, c_ref, states_ref, rows_ref, skip_ref, wide_ref, half_ref, part_ref):
    width, tokens = dy_ref.shape
    head_dim = width // 4
    cum = rows_ref[:4]
    columns = rows_ref[:8].T
    step = widened(columns[:, 4:], width)
    start = widened(jnp.exp(columns[:, :4]), width)
    b, c, states = b_ref[...], c_ref[...], states_ref[...]
    scores = dot_last(c, b)
    entered = dot_last(c, states)
    dy_wide = dy_ref[...].astype(f32).T
    dy = dy_wide.astype(bf16)
    x = x_ref[...].astype(f32)
    scaled = (x * step).astype(bf16)
    causal = lax.broadcasted_iota(jnp.int32, (tokens, tokens), 0) >= lax.broadcasted_iota(jnp.int32, (tokens, tokens), 1)
    total = jnp.zeros((tokens, tokens), f32)
    along, down, backs = [], [], []
    for h in range(4):
        mine = slice(h * head_dim, (h + 1) * head_dim)
        dy_h = dy[:, mine]
        gaps = jnp.minimum(columns[:, h:h + 1] - cum[h:h + 1], 0.0)
        mask = jnp.where(causal, jnp.exp(gaps), 0.0)
        weighed = (scores * mask).astype(bf16)
        backs.append(lax.dot_general(weighed, dy_h, (((0,), (0,)), ((), ())), preferred_element_type=f32))
        masked = dot_last(dy_h, scaled[:, mine]) * mask
        total = total + masked
        pairs = masked * scores
        along.append(jnp.sum(pairs, axis=1, keepdims=True))
        down.append(jnp.sum(pairs, axis=0, keepdims=True))
    total = total.astype(bf16)
    db = lax.dot_general(total, c, (((0,), (0,)), ((), ())), preferred_element_type=f32)
    dc = jnp.dot(total, b, preferred_element_type=f32)
    dc = dc + jnp.dot((dy_wide * start).astype(bf16), states, preferred_element_type=f32)
    back = jnp.concatenate(backs, axis=1)
    wide_ref[:width] = (step * back + skip_ref[...] * dy_wide).T
    wide_ref[width:] = db.T
    half_ref[:width] = x.T.astype(bf16)
    half_ref[width:] = dc.T.astype(bf16)
    entered = head_sums(start * dy_wide * entered, 4)
    rows = as_rows([a + e for a, e in zip(along, entered)] + head_sums(x * back, 4))
    part_ref[:8] = rows - jnp.concatenate(down + [jnp.zeros((4, tokens), f32)], axis=0)
    part_ref[8:] = jnp.broadcast_to(jnp.sum(dy_wide * x, axis=0, keepdims=True), (8, width))


def intra_terms(dy, x_in, b_in, c_in, states, rows, skip):
    width, tokens = dy.shape
    height = width + b_in.shape[1]
    return pl.pallas_call(
        intra_kernel,
        out_shape=(jax.ShapeDtypeStruct((height, tokens), f32), jax.ShapeDtypeStruct((height, tokens), bf16), jax.ShapeDtypeStruct((16, tokens), f32)),
        compiler_params=small(),
        cost_estimate=cost(14 * tokens * tokens * width, 2 << 20),
    )(dy, x_in, b_in, c_in, states, rows, skip)


def dt_rows(back, carried, half_ref, rows_ref, part_ref, states_ref, raw_ref, dt_ref, param_ref):
    width, tokens = back.shape
    head_dim = width // 4
    cum, step = rows_ref[:4], rows_ref[4:8]
    last = cum[:, tokens - 1:]
    rate, bias = rows_ref[8:12], rows_ref[12:]
    dots = jnp.sum((half_ref[:width].astype(f32) * back).reshape(4, head_dim, tokens), axis=1)
    end_decay = jnp.exp(last - cum)
    end_terms = step * end_decay * dots
    carried = carried.reshape(4, head_dim, -1)
    held = jnp.sum(carried * states_ref[...].astype(f32).reshape(4, head_dim, -1), axis=1)
    tail = jnp.sum(end_terms, axis=1, keepdims=True) + jnp.exp(last) * jnp.sum(held, axis=1, keepdims=True)
    below = lax.broadcasted_iota(jnp.int32, (tokens, tokens), 0) >= lax.broadcasted_iota(jnp.int32, (tokens, tokens), 1)
    step_grad = tail + jnp.dot(
        part_ref[:4] - end_terms, below.astype(f32), precision=lax.Precision.HIGHEST, preferred_element_type=f32
    )
    dt_sum = part_ref[4:8] + end_decay * dots - rate * step_grad
    dt = dt_sum * jax.nn.sigmoid(raw_ref[...] + bias)
    dt_ref[...] = dt
    lanes = lax.broadcasted_iota(jnp.int32, (4, width), 1)
    heads = lax.broadcasted_iota(jnp.int32, (4, width), 0)
    skip = jnp.sum(jnp.where(lanes // head_dim == heads, part_ref[8:9], 0.0), axis=1, keepdims=True)
    decays = jnp.sum(step_grad * (-rate * step), axis=1, keepdims=True)
    biases = jnp.sum(dt, axis=1, keepdims=True)
    lanes, heads = lanes[:, :128], heads[:, :128]
    placed = jnp.where(lanes == heads, decays, 0.0)
    placed = jnp.where(lanes == heads + 4, skip, placed)
    placed = jnp.where(lanes == heads + 8, biases, placed)
    param_ref[...] = jnp.sum(placed, axis=0, keepdims=True)


def x_grad_kernel(
    carried_ref, b_ref, wide_ref, half_ref, rows_ref, part_ref, states_ref, raw_ref, sent_ref, dt_ref, param_ref
):
    blocks, height, state_dim = carried_ref.shape
    width = blocks * height
    tokens = b_ref.shape[0]
    carried_wide = carried_ref[...].reshape(width, state_dim)
    carried = carried_wide.astype(bf16)
    back = dot_last(carried, b_ref[...])
    cum = rows_ref[:4]
    weight = over_channels(rows_ref[4:8] * jnp.exp(cum[:, tokens - 1:] - cum), width)
    x_grad = (wide_ref[:width] + weight * back).astype(bf16)
    x_end = (half_ref[:width].astype(f32) * weight).astype(bf16)
    entry = lax.dot_general(carried, x_end, (((0,), (0,)), ((), ())), preferred_element_type=f32)
    db = (wide_ref[width:] + entry).astype(bf16)
    rows = state_dim // 2
    for y in range(4):
        sent_ref[y, :width] = x_grad
        if y < 2:
            sent_ref[y, width:] = db[y * rows:(y + 1) * rows]
        else:
            sent_ref[y, width:] = half_ref[width + (y - 2) * rows:width + (y - 1) * rows]
    dt_rows(back, carried_wide, half_ref, rows_ref, part_ref, states_ref, raw_ref, dt_ref, param_ref)


def x_grads(carried, b_in, wide, half, rows, part, states, dt_raw):
    tokens, state_dim = b_in.shape
    inner = wide.shape[0] - state_dim
    return pl.pallas_call(
        x_grad_kernel,
        out_shape=(
            pltpu.HBM((4, inner + state_dim // 2, tokens), bf16),
            jax.ShapeDtypeStruct(dt_raw.shape, f32),
            jax.ShapeDtypeStruct((1, 128), f32),
        ),
        compiler_params=small(),
        cost_estimate=cost(4 * tokens * inner * 128, 2 << 20),
    )(carried, b_in, wide, half, rows, part, states, dt_raw)


def in_kernel(place_ref, got_ref, own_ref, near_ref, other_ref, half_ref, rest_ref, *out_refs):
    quarter, inner = own_ref.shape
    feats = quarter // 4
    rows = out_refs[0].shape[0] - feats
    y, core, zh = place_ref[0], place_ref[1], place_ref[2]
    sources = [y, lax.rem(y + 3 + 2 * core, 4), lax.rem(y + 5 - 2 * core, 4), lax.rem(y + 2, 4)]
    x_grad = jnp.concatenate([got_ref[source, :inner] for source in sources], axis=0)
    targets = [zh, lax.rem(zh + 1 + 2 * core, 4), lax.rem(zh + 2, 4), lax.rem(zh + 3 + 2 * core, 4)]
    for z, out_ref in zip(targets, out_refs):
        at = pl.ds(pl.multiple_of(inner + z * rows, rows), rows)
        bc = got_ref[0, at].astype(f32)
        for other in range(1, 4):
            bc = bc + got_ref[other, at].astype(f32)
        out_ref[feats:] = bc.astype(bf16)
        mine = pl.ds(pl.multiple_of(z * feats, feats), feats)
        part = pl.ds(pl.multiple_of(lax.rem(z, 2) * feats, feats), feats)
        far = jnp.where(core == z // 2, half_ref[part], rest_ref[part])
        w = jnp.concatenate([own_ref[mine], near_ref[mine], other_ref[mine], far], axis=1)
        out_ref[:feats] = jnp.dot(w, x_grad, preferred_element_type=f32).astype(bf16)


def in_products(place, got, pieces):
    quarter, inner = pieces[0].shape
    _, height, tokens = got.shape
    feats, rows = quarter // 4, (height - inner) // 4
    return pl.pallas_call(
        in_kernel,
        in_specs=[pl.BlockSpec(memory_space=pltpu.SMEM)] + [pl.BlockSpec(memory_space=pltpu.VMEM)] * 6,
        out_shape=[jax.ShapeDtypeStruct((feats + rows, tokens), bf16)] * 4,
        compiler_params=small(),
        cost_estimate=cost(8 * quarter * inner * tokens, 4 << 20),
    )(place, got, *pieces)


def sum_kernel(own_ref, chain_ref, direct_ref, in_ref, bc_ref):
    feats = in_ref.shape[0]
    total = own_ref[...].astype(f32) + chain_ref[...].astype(f32) + direct_ref[...].astype(f32)
    total = total.astype(bf16)
    in_ref[...] = total[:feats]
    bc_ref[...] = total[feats:]


def final_sums(own, chain, direct, feats):
    height, tokens = own.shape
    return pl.pallas_call(
        sum_kernel,
        out_shape=(
            jax.ShapeDtypeStruct((feats, tokens), bf16),
            jax.ShapeDtypeStruct((height - feats, tokens), bf16),
        ),
        compiler_params=small(),
        cost_estimate=cost(4 * height * tokens, 1 << 20),
    )(own, chain, direct)


def ring_step(value, axis, way):
    pairs = [(c, i, (i + (way if c == 0 else -way)) % 4) for c in range(2) for i in range(4)]
    return lax.ppermute(value, ("core", axis), [(4 * c + i, 4 * c + j) for c, i, j in pairs])


def shifted(row, axis):
    return [lax.ppermute(row, axis, [(i, (i + s) % 4) for i in range(4)]) for s in (1, 2, 3)]


def paired(row, rounds):
    first, second, third = rounds
    return (row + second) + (first + third)


def shards(out_grad, x_in, b_in, c_in, dt_raw, dt_bias, a_log, d_skip, states, w_out, w_in):
    tokens_here, inner_here = x_in.shape
    group_heads = dt_raw.shape[0]
    head_dim = inner_here // group_heads
    state_dim = b_in.shape[1]
    blocks = lax.axis_size(SEQ)
    y = lax.axis_index("y")
    entry_state = states[0]

    w_out_y = lax.all_to_all(regrouped(w_out), "y", 0, 0)
    near = lax.all_gather(out_grad, "zh", axis=1, tiled=True)
    products = partial_products(near, w_out_y)
    w_in_held, products = lax.optimization_barrier((w_in, products))
    quarter = w_in.shape[0] // 4
    core = lax.axis_index("core")
    own = lax.dynamic_slice_in_dim(w_in_held, y * quarter, quarter)
    near_piece = lax.dynamic_slice_in_dim(w_in_held, lax.rem(y + 1 + 2 * core, 4) * quarter, quarter)
    far_at = lax.rem(y + 2, 4) * quarter + core * (quarter // 2)
    far_half = lax.dynamic_slice_in_dim(w_in_held, far_at, quarter // 2)
    head_parts = lax.all_to_all(products, "y", 0, 0)

    decay_rate = jnp.exp(a_log)
    step_size = jax.nn.softplus(dt_raw + dt_bias[:, None])
    log_step = -decay_rate[:, None] * step_size
    positions = jnp.arange(tokens_here)
    upto = (positions[:, None] <= positions[None, :]).astype(f32)
    cumlog = jnp.dot(log_step, upto, precision=lax.Precision.HIGHEST)
    wide_scalars = jnp.broadcast_to(jnp.concatenate([decay_rate, dt_bias])[:, None], (2 * group_heads, tokens_here))
    rows = jnp.concatenate([cumlog, step_size, wide_scalars], axis=0)
    ends = jnp.pad(three_parts(jnp.exp(cumlog[:, -1])), ((0, 0), (0, 5)))
    ends = jnp.broadcast_to(ends[:, None, :, None], (group_heads, blocks // group_heads, 8, state_dim))
    skip = jnp.repeat(d_skip, head_dim)[None]
    own, far_half, head_parts = lax.optimization_barrier((own, far_half, head_parts))
    one_step = [((c, i), (c, (i + 1 + 2 * c) % 4)) for c in range(2) for i in range(4)]
    near_piece = lax.ppermute(near_piece, ("core", "y"), [(4 * a[0] + a[1], 4 * b[0] + b[1]) for a, b in one_step])
    far_half = lax.ppermute(far_half, "y", [(i, (i + 2) % 4) for i in range(4)])
    swap = [(0, 1), (1, 0)]
    held = [own, near_piece, lax.ppermute(near_piece, "core", swap), far_half, lax.ppermute(far_half, "core", swap)]
    dy, sent = local_states(head_parts, rows, c_in, ends.reshape(blocks, 8, state_dim))
    ahead = suffix_scan(lax.all_to_all(sent, SEQ, 0, 0))
    ahead, dy = lax.optimization_barrier((ahead, dy))
    wide, half, part = intra_terms(dy, x_in, b_in, c_in, entry_state, rows, skip)
    *held, carried = lax.optimization_barrier((*held, lax.all_to_all(ahead, SEQ, 0, 0)))
    sent_y, dt_grad, row = x_grads(carried, b_in, wide, half, rows, part, entry_state, dt_raw)
    got = lax.all_to_all(sent_y, "y", 0, 0)
    *rounds, got = lax.optimization_barrier((*shifted(row, "zl"), got))
    place = jnp.stack([y, core, lax.axis_index("zh")])
    mine, near_terms, far_terms, direct_terms = in_products(place, got, held)
    relayed = ring_step(far_terms, "zh", 1)
    direct = ring_step(direct_terms, "zh", -1)
    relayed, direct = lax.optimization_barrier((relayed, direct))
    onward = (near_terms.astype(f32) + relayed.astype(f32)).astype(bf16)
    *rounds, onward = lax.optimization_barrier((*rounds, onward))
    chain = ring_step(onward, "zh", 1)
    row = paired(row, rounds)
    peers = lax.axis_size(("x", "core"))
    row = lax.all_to_all(jnp.broadcast_to(row[None], (peers,) + row.shape), ("x", "core"), 0, 0).sum(axis=0)
    in_grad, bc_grad = final_sums(mine, chain, direct, w_in.shape[0] // 16)
    norm_scale = (blocks * tokens_here * head_dim) ** (-0.5)
    param_grad = row[0, : 3 * group_heads].reshape(3, group_heads) * norm_scale
    return (in_grad, bc_grad, dt_grad, param_grad)


def solution(mesh):
    fine = Mesh(mesh.devices.reshape(4, 4, 2, 4, 4), ("x", "zl", "core", "y", "zh"))
    return jax.shard_map(
        shards,
        mesh=fine,
        in_specs=(
            P(SEQ, HEAD),
            P(SEQ, HEAD),
            P(SEQ, None),
            P(SEQ, None),
            P(HEAD, SEQ),
            P(HEAD),
            P(HEAD),
            P(HEAD),
            P(SEQ, HEAD, None),
            P(HEAD, None),
            P(None, HEAD),
        ),
        out_specs=(P(HEAD, SEQ), P(HEAD, SEQ), P(HEAD, SEQ), P(None, HEAD)),
        check_vma=False,
    )
```

```python
import jax
import jax.numpy as jnp
from jax import lax
from jax.experimental import pallas as pl
from jax.experimental.pallas import tpu as pltpu
from jax.sharding import Mesh, PartitionSpec as P

SEQ = ("x", "zl", "core")
HEAD = ("y", "zh")
f32, bf16 = jnp.float32, jnp.bfloat16


def scan_kernel(parts_ref, carried_ref):
    blocks = parts_ref.shape[0]
    held = jnp.zeros(carried_ref.shape[1:], f32)
    for k in range(blocks - 1, -1, -1):
        carried_ref[k] = held
        wide = parts_ref[k].astype(f32)
        total = wide[8:9] + wide[9:10] + wide[10:11]
        held = total * held + wide[:8]


def suffix_scan(parts):
    blocks, _, width = parts.shape
    return pl.pallas_call(
        scan_kernel,
        out_shape=jax.ShapeDtypeStruct((blocks, 8, width), f32),
        compiler_params=small(),
        cost_estimate=cost(blocks * 3072, blocks * 8192),
    )(parts)


def three_parts(values):
    first = values.astype(bf16).astype(f32)
    second = (values - first).astype(bf16).astype(f32)
    return jnp.stack([first, second, values - first - second], axis=-1)


def cost(flops, moved):
    return pl.CostEstimate(flops=flops, bytes_accessed=moved, transcendentals=0)


def small(mib=16):
    return pltpu.CompilerParams(vmem_limit_bytes=mib << 20)


def dot_last(a, b):
    return lax.dot_general(a, b, (((1,), (1,)), ((), ())), preferred_element_type=f32)


def regroup_kernel(w_ref, out_ref, stage_ref, in_sems, out_sems):
    _, pieces, rows, part = stage_ref.shape
    steps = [(g, r) for g in range(4) for r in range(pieces)]

    def copy_in(g, r):
        source = w_ref.at[pl.ds(r * rows, rows), pl.ds(g * part, part)]
        return pltpu.make_async_copy(source, stage_ref.at[g, r], in_sems.at[g, r])

    def copy_out(g, r):
        return pltpu.make_async_copy(stage_ref.at[g, r], out_ref.at[g, pl.ds(r * rows, rows)], out_sems.at[g, r])

    for step in steps:
        copy_in(*step).start()
    for step in steps:
        copy_in(*step).wait()
        copy_out(*step).start()
    for step in steps:
        copy_out(*step).wait()


def regrouped(w):
    rows, width = w.shape
    pieces = 4
    return pl.pallas_call(
        regroup_kernel,
        in_specs=[pl.BlockSpec(memory_space=pl.ANY)],
        out_specs=pl.BlockSpec(memory_space=pl.ANY),
        out_shape=jax.ShapeDtypeStruct((4, rows, width // 4), w.dtype),
        scratch_shapes=[
            pltpu.VMEM((4, pieces, rows // pieces, width // 4), w.dtype),
            pltpu.SemaphoreType.DMA((4, pieces)),
            pltpu.SemaphoreType.DMA((4, pieces)),
        ],
        cost_estimate=cost(0, 4 * rows * width),
    )(w)


def partial_kernel(order_ref, *refs):
    *block_refs, w_ref, out_ref, near_ref = refs
    groups, inner, depth = w_ref.shape
    width = block_refs[0].shape[1]
    for k, block_ref in enumerate(block_refs):
        near_ref[:, pl.ds(pl.multiple_of(order_ref[k] * width, width), width)] = block_ref[...]
    out = dot_last(w_ref[...].reshape(groups * inner, depth), near_ref[...]).astype(bf16)
    out_ref[...] = out.reshape(out_ref.shape)


def partial_products(order, near, w_mine):
    groups, inner, depth = w_mine.shape
    tokens = near[0].shape[0]
    return pl.pallas_call(
        partial_kernel,
        in_specs=[pl.BlockSpec(memory_space=pltpu.SMEM)] + [pl.BlockSpec(memory_space=pltpu.VMEM)] * 5,
        out_shape=pltpu.HBM((groups, inner, tokens), bf16),
        scratch_shapes=[pltpu.VMEM((tokens, depth), bf16)],
        compiler_params=small(),
        cost_estimate=cost(2 * groups * tokens * inner * depth, 4 << 20),
    )(order, *near, w_mine)


def over_channels(rows, height):
    heads, tokens = rows.shape
    return jnp.concatenate(
        [jnp.broadcast_to(rows[h:h + 1], (height // heads, tokens)) for h in range(heads)], axis=0
    )


def state_kernel(parts_ref, rows_ref, c_ref, ends_ref, dy_ref, sent_ref):
    total = parts_ref[0].astype(f32)
    for y in range(1, parts_ref.shape[0]):
        total = total + parts_ref[y].astype(f32)
    dy = total.astype(bf16)
    dy_ref[...] = dy
    start = over_channels(jnp.exp(rows_ref[:4]), dy.shape[0])
    decayed = (dy.astype(f32) * start).astype(bf16)
    state = jnp.dot(decayed, c_ref[...], preferred_element_type=f32)
    blocks, rows, width = ends_ref.shape
    state = state.reshape(blocks, rows, width)
    sent_ref[...] = jnp.concatenate([state, ends_ref[...]], axis=1).astype(bf16)


def local_states(parts, rows, c_in, ends):
    _, inner, tokens = parts.shape
    blocks, height, width = ends.shape
    return pl.pallas_call(
        state_kernel,
        out_shape=(pltpu.HBM((inner, tokens), bf16), pltpu.HBM((blocks, 2 * height, width), bf16)),
        compiler_params=small(),
        cost_estimate=cost(2 * tokens * inner * width, 2 << 20),
    )(parts, rows, c_in, ends)


def widened(columns, width):
    tokens, heads = columns.shape
    return jnp.concatenate(
        [jnp.broadcast_to(columns[:, h:h + 1], (tokens, width // heads)) for h in range(heads)], axis=1
    )


def head_sums(values, heads):
    width = values.shape[1] // heads
    return [jnp.sum(values[:, h * width:(h + 1) * width], axis=1, keepdims=True) for h in range(heads)]


def as_rows(columns):
    tokens = columns[0].shape[0]
    lanes = lax.broadcasted_iota(jnp.int32, (tokens, 128), 1)
    spread = jnp.zeros((tokens, 128), f32)
    for k, column in enumerate(columns):
        spread = jnp.where(lanes == k, column, spread)
    return spread.T[:8]


def intra_kernel(dy_ref, x_ref, b_ref, c_ref, states_ref, rows_ref, skip_ref, wide_ref, half_ref, part_ref):
    width, tokens = dy_ref.shape
    head_dim = width // 4
    cum = rows_ref[:4]
    columns = rows_ref[:8].T
    step = widened(columns[:, 4:], width)
    start = widened(jnp.exp(columns[:, :4]), width)
    b, c, states = b_ref[...], c_ref[...], states_ref[...]
    scores = dot_last(c, b)
    entered = dot_last(c, states)
    dy_wide = dy_ref[...].astype(f32).T
    dy = dy_wide.astype(bf16)
    x = x_ref[...].astype(f32)
    scaled = (x * step).astype(bf16)
    causal = lax.broadcasted_iota(jnp.int32, (tokens, tokens), 0) >= lax.broadcasted_iota(jnp.int32, (tokens, tokens), 1)
    total = jnp.zeros((tokens, tokens), f32)
    along, down, backs = [], [], []
    for h in range(4):
        mine = slice(h * head_dim, (h + 1) * head_dim)
        dy_h = dy[:, mine]
        gaps = jnp.minimum(columns[:, h:h + 1] - cum[h:h + 1], 0.0)
        mask = jnp.where(causal, jnp.exp(gaps), 0.0)
        weighed = (scores * mask).astype(bf16)
        backs.append(lax.dot_general(weighed, dy_h, (((0,), (0,)), ((), ())), preferred_element_type=f32))
        masked = dot_last(dy_h, scaled[:, mine]) * mask
        total = total + masked
        pairs = masked * scores
        along.append(jnp.sum(pairs, axis=1, keepdims=True))
        down.append(jnp.sum(pairs, axis=0, keepdims=True))
    total = total.astype(bf16)
    db = lax.dot_general(total, c, (((0,), (0,)), ((), ())), preferred_element_type=f32)
    dc = jnp.dot(total, b, preferred_element_type=f32)
    dc = dc + jnp.dot((dy_wide * start).astype(bf16), states, preferred_element_type=f32)
    back = jnp.concatenate(backs, axis=1)
    wide_ref[:width] = (step * back + skip_ref[...] * dy_wide).T
    wide_ref[width:] = db.T
    half_ref[:width] = x.T.astype(bf16)
    half_ref[width:] = dc.T.astype(bf16)
    entered = head_sums(start * dy_wide * entered, 4)
    rows = as_rows([a + e for a, e in zip(along, entered)] + head_sums(x * back, 4))
    part_ref[:8] = rows - jnp.concatenate(down + [jnp.zeros((4, tokens), f32)], axis=0)
    part_ref[8:] = jnp.broadcast_to(jnp.sum(dy_wide * x, axis=0, keepdims=True), (8, width))


def intra_terms(dy, x_in, b_in, c_in, states, rows, skip):
    width, tokens = dy.shape
    height = width + b_in.shape[1]
    return pl.pallas_call(
        intra_kernel,
        out_shape=(jax.ShapeDtypeStruct((height, tokens), f32), jax.ShapeDtypeStruct((height, tokens), bf16), jax.ShapeDtypeStruct((16, tokens), f32)),
        compiler_params=small(),
        cost_estimate=cost(14 * tokens * tokens * width, 2 << 20),
    )(dy, x_in, b_in, c_in, states, rows, skip)


def dt_rows(back, carried, half_ref, rows_ref, part_ref, states_ref, raw_ref, dt_ref, param_ref):
    width, tokens = back.shape
    head_dim = width // 4
    cum, step = rows_ref[:4], rows_ref[4:8]
    last = cum[:, tokens - 1:]
    rate, bias = rows_ref[8:12], rows_ref[12:]
    dots = jnp.sum((half_ref[:width].astype(f32) * back).reshape(4, head_dim, tokens), axis=1)
    end_decay = jnp.exp(last - cum)
    end_terms = step * end_decay * dots
    carried = carried.reshape(4, head_dim, -1)
    held = jnp.sum(carried * states_ref[...].astype(f32).reshape(4, head_dim, -1), axis=1)
    tail = jnp.sum(end_terms, axis=1, keepdims=True) + jnp.exp(last) * jnp.sum(held, axis=1, keepdims=True)
    below = lax.broadcasted_iota(jnp.int32, (tokens, tokens), 0) >= lax.broadcasted_iota(jnp.int32, (tokens, tokens), 1)
    step_grad = tail + jnp.dot(
        part_ref[:4] - end_terms, below.astype(f32), precision=lax.Precision.HIGHEST, preferred_element_type=f32
    )
    dt_sum = part_ref[4:8] + end_decay * dots - rate * step_grad
    dt = dt_sum * jax.nn.sigmoid(raw_ref[...] + bias)
    dt_ref[...] = dt
    lanes = lax.broadcasted_iota(jnp.int32, (4, width), 1)
    heads = lax.broadcasted_iota(jnp.int32, (4, width), 0)
    skip = jnp.sum(jnp.where(lanes // head_dim == heads, part_ref[8:9], 0.0), axis=1, keepdims=True)
    decays = jnp.sum(step_grad * (-rate * step), axis=1, keepdims=True)
    biases = jnp.sum(dt, axis=1, keepdims=True)
    lanes, heads = lanes[:, :128], heads[:, :128]
    placed = jnp.where(lanes == heads, decays, 0.0)
    placed = jnp.where(lanes == heads + 4, skip, placed)
    placed = jnp.where(lanes == heads + 8, biases, placed)
    param_ref[...] = jnp.sum(placed, axis=0, keepdims=True)


def x_grad_kernel(
    carried_ref, b_ref, wide_ref, half_ref, rows_ref, part_ref, states_ref, raw_ref, sent_ref, dt_ref, param_ref
):
    blocks, height, state_dim = carried_ref.shape
    width = blocks * height
    tokens = b_ref.shape[0]
    carried_wide = carried_ref[...].reshape(width, state_dim)
    carried = carried_wide.astype(bf16)
    back = dot_last(carried, b_ref[...])
    cum = rows_ref[:4]
    weight = over_channels(rows_ref[4:8] * jnp.exp(cum[:, tokens - 1:] - cum), width)
    x_grad = (wide_ref[:width] + weight * back).astype(bf16)
    x_end = (half_ref[:width].astype(f32) * weight).astype(bf16)
    entry = lax.dot_general(carried, x_end, (((0,), (0,)), ((), ())), preferred_element_type=f32)
    db = (wide_ref[width:] + entry).astype(bf16)
    rows = state_dim // 2
    for y in range(4):
        sent_ref[y, :width] = x_grad
        if y < 2:
            sent_ref[y, width:] = db[y * rows:(y + 1) * rows]
        else:
            sent_ref[y, width:] = half_ref[width + (y - 2) * rows:width + (y - 1) * rows]
    dt_rows(back, carried_wide, half_ref, rows_ref, part_ref, states_ref, raw_ref, dt_ref, param_ref)


def x_grads(carried, b_in, wide, half, rows, part, states, dt_raw):
    tokens, state_dim = b_in.shape
    inner = wide.shape[0] - state_dim
    return pl.pallas_call(
        x_grad_kernel,
        out_shape=(
            pltpu.HBM((4, inner + state_dim // 2, tokens), bf16),
            jax.ShapeDtypeStruct(dt_raw.shape, f32),
            jax.ShapeDtypeStruct((1, 128), f32),
        ),
        compiler_params=small(),
        cost_estimate=cost(4 * tokens * inner * 128, 2 << 20),
    )(carried, b_in, wide, half, rows, part, states, dt_raw)


def in_kernel(place_ref, got_ref, own_ref, near_ref, other_ref, half_ref, rest_ref, *out_refs):
    quarter, inner = own_ref.shape
    feats = quarter // 4
    rows = out_refs[0].shape[0] - feats
    y, core, zh = place_ref[0], place_ref[1], place_ref[2]
    sources = [y, lax.rem(y + 3 + 2 * core, 4), lax.rem(y + 5 - 2 * core, 4), lax.rem(y + 2, 4)]
    x_grad = jnp.concatenate([got_ref[source, :inner] for source in sources], axis=0)
    targets = [zh, lax.rem(zh + 1 + 2 * core, 4), lax.rem(zh + 2, 4), lax.rem(zh + 3 + 2 * core, 4)]
    for z, out_ref in zip(targets, out_refs):
        at = pl.ds(pl.multiple_of(inner + z * rows, rows), rows)
        bc = got_ref[0, at].astype(f32)
        for other in range(1, 4):
            bc = bc + got_ref[other, at].astype(f32)
        out_ref[feats:] = bc.astype(bf16)
        mine = pl.ds(pl.multiple_of(z * feats, feats), feats)
        part = pl.ds(pl.multiple_of(lax.rem(z, 2) * feats, feats), feats)
        far = jnp.where(core == z // 2, half_ref[part], rest_ref[part])
        w = jnp.concatenate([own_ref[mine], near_ref[mine], other_ref[mine], far], axis=1)
        out_ref[:feats] = jnp.dot(w, x_grad, preferred_element_type=f32).astype(bf16)


def in_products(place, got, pieces):
    quarter, inner = pieces[0].shape
    _, height, tokens = got.shape
    feats, rows = quarter // 4, (height - inner) // 4
    return pl.pallas_call(
        in_kernel,
        in_specs=[pl.BlockSpec(memory_space=pltpu.SMEM)] + [pl.BlockSpec(memory_space=pltpu.VMEM)] * 6,
        out_shape=[jax.ShapeDtypeStruct((feats + rows, tokens), bf16)] * 4,
        compiler_params=small(),
        cost_estimate=cost(8 * quarter * inner * tokens, 4 << 20),
    )(place, got, *pieces)


def sum_kernel(own_ref, chain_ref, direct_ref, in_ref, bc_ref):
    feats = in_ref.shape[0]
    total = own_ref[...].astype(f32) + chain_ref[...].astype(f32) + direct_ref[...].astype(f32)
    total = total.astype(bf16)
    in_ref[...] = total[:feats]
    bc_ref[...] = total[feats:]


def final_sums(own, chain, direct, feats):
    height, tokens = own.shape
    return pl.pallas_call(
        sum_kernel,
        out_shape=(
            jax.ShapeDtypeStruct((feats, tokens), bf16),
            jax.ShapeDtypeStruct((height - feats, tokens), bf16),
        ),
        compiler_params=small(),
        cost_estimate=cost(4 * height * tokens, 1 << 20),
    )(own, chain, direct)


def ring_step(value, axis, way):
    pairs = [(c, i, (i + (way if c == 0 else -way)) % 4) for c in range(2) for i in range(4)]
    return lax.ppermute(value, ("core", axis), [(4 * c + i, 4 * c + j) for c, i, j in pairs])


def shifted(row, axis):
    return [lax.ppermute(row, axis, [(i, (i + s) % 4) for i in range(4)]) for s in (1, 2, 3)]


def paired(row, rounds):
    first, second, third = rounds
    return (row + second) + (first + third)


def shards(out_grad, x_in, b_in, c_in, dt_raw, dt_bias, a_log, d_skip, states, w_out, w_in):
    tokens_here, inner_here = x_in.shape
    group_heads = dt_raw.shape[0]
    head_dim = inner_here // group_heads
    state_dim = b_in.shape[1]
    blocks = lax.axis_size(SEQ)
    y = lax.axis_index("y")
    entry_state = states[0]

    core, zh = lax.axis_index("core"), lax.axis_index("zh")
    w_out_parts, own_grad = lax.optimization_barrier((regrouped(w_out), out_grad))
    w_out_y = lax.all_to_all(w_out_parts, "y", 0, 0)
    behind = ring_step(own_grad, "zh", 1)
    ahead_grad = ring_step(own_grad, "zh", -1)
    across_grad = ring_step(behind, "zh", 1)
    order = jnp.stack([zh, lax.rem(zh + 3 + 2 * core, 4), lax.rem(zh + 1 + 2 * core, 4), lax.rem(zh + 2, 4)])
    products = partial_products(order, (own_grad, behind, ahead_grad, across_grad), w_out_y)
    w_in_held, products = lax.optimization_barrier((w_in, products))
    quarter = w_in.shape[0] // 4
    own = lax.dynamic_slice_in_dim(w_in_held, y * quarter, quarter)
    near_piece = lax.dynamic_slice_in_dim(w_in_held, lax.rem(y + 1 + 2 * core, 4) * quarter, quarter)
    far_at = lax.rem(y + 2, 4) * quarter + core * (quarter // 2)
    far_half = lax.dynamic_slice_in_dim(w_in_held, far_at, quarter // 2)
    head_parts = lax.all_to_all(products, "y", 0, 0)

    decay_rate = jnp.exp(a_log)
    step_size = jax.nn.softplus(dt_raw + dt_bias[:, None])
    log_step = -decay_rate[:, None] * step_size
    positions = jnp.arange(tokens_here)
    upto = (positions[:, None] <= positions[None, :]).astype(f32)
    cumlog = jnp.dot(log_step, upto, precision=lax.Precision.HIGHEST)
    wide_scalars = jnp.broadcast_to(jnp.concatenate([decay_rate, dt_bias])[:, None], (2 * group_heads, tokens_here))
    rows = jnp.concatenate([cumlog, step_size, wide_scalars], axis=0)
    ends = jnp.pad(three_parts(jnp.exp(cumlog[:, -1])), ((0, 0), (0, 5)))
    ends = jnp.broadcast_to(ends[:, None, :, None], (group_heads, blocks // group_heads, 8, state_dim))
    skip = jnp.repeat(d_skip, head_dim)[None]
    own, far_half, head_parts = lax.optimization_barrier((own, far_half, head_parts))
    one_step = [((c, i), (c, (i + 1 + 2 * c) % 4)) for c in range(2) for i in range(4)]
    near_piece = lax.ppermute(near_piece, ("core", "y"), [(4 * a[0] + a[1], 4 * b[0] + b[1]) for a, b in one_step])
    far_half = lax.ppermute(far_half, "y", [(i, (i + 2) % 4) for i in range(4)])
    swap = [(0, 1), (1, 0)]
    held = [own, near_piece, lax.ppermute(near_piece, "core", swap), far_half, lax.ppermute(far_half, "core", swap)]
    dy, sent = local_states(head_parts, rows, c_in, ends.reshape(blocks, 8, state_dim))
    ahead = suffix_scan(lax.all_to_all(sent, SEQ, 0, 0))
    ahead, dy = lax.optimization_barrier((ahead, dy))
    wide, half, part = intra_terms(dy, x_in, b_in, c_in, entry_state, rows, skip)
    *held, carried = lax.optimization_barrier((*held, lax.all_to_all(ahead, SEQ, 0, 0)))
    sent_y, dt_grad, row = x_grads(carried, b_in, wide, half, rows, part, entry_state, dt_raw)
    got = lax.all_to_all(sent_y, "y", 0, 0)
    *rounds, got = lax.optimization_barrier((*shifted(row, "zl"), got))
    place = jnp.stack([y, core, zh])
    mine, near_terms, far_terms, direct_terms = in_products(place, got, held)
    relayed = ring_step(far_terms, "zh", 1)
    direct = ring_step(direct_terms, "zh", -1)
    onward = (near_terms.astype(f32) + relayed.astype(f32)).astype(bf16)
    *rounds, onward = lax.optimization_barrier((*rounds, onward))
    chain = ring_step(onward, "zh", 1)
    row = paired(row, rounds)
    row, direct = lax.optimization_barrier((row, direct))
    peers = lax.axis_size(("x", "core"))
    row = lax.all_to_all(jnp.broadcast_to(row[None], (peers,) + row.shape), ("x", "core"), 0, 0).sum(axis=0)
    in_grad, bc_grad = final_sums(mine, chain, direct, w_in.shape[0] // 16)
    norm_scale = (blocks * tokens_here * head_dim) ** (-0.5)
    param_grad = row[0, : 3 * group_heads].reshape(3, group_heads) * norm_scale
    return (in_grad, bc_grad, dt_grad, param_grad)


def solution(mesh):
    fine = Mesh(mesh.devices.reshape(4, 4, 2, 4, 4), ("x", "zl", "core", "y", "zh"))
    return jax.shard_map(
        shards,
        mesh=fine,
        in_specs=(
            P(SEQ, HEAD),
            P(SEQ, HEAD),
            P(SEQ, None),
            P(SEQ, None),
            P(HEAD, SEQ),
            P(HEAD),
            P(HEAD),
            P(HEAD),
            P(SEQ, HEAD, None),
            P(HEAD, None),
            P(None, HEAD),
        ),
        out_specs=(P(HEAD, SEQ), P(HEAD, SEQ), P(HEAD, SEQ), P(None, HEAD)),
        check_vma=False,
    )
```

```python
import jax
import jax.numpy as jnp
from jax import lax
from jax.experimental import pallas as pl
from jax.experimental.pallas import tpu as pltpu
from jax.sharding import Mesh, PartitionSpec as P

SEQ = ("x", "zl", "core")
HEAD = ("y", "zh")
f32, bf16 = jnp.float32, jnp.bfloat16


def scan_kernel(parts_ref, carried_ref):
    blocks = parts_ref.shape[0]
    held = jnp.zeros(carried_ref.shape[1:], f32)
    for k in range(blocks - 1, -1, -1):
        carried_ref[k] = held
        wide = parts_ref[k].astype(f32)
        total = wide[8:9] + wide[9:10] + wide[10:11]
        held = total * held + wide[:8]


def suffix_scan(parts):
    blocks, _, width = parts.shape
    return pl.pallas_call(
        scan_kernel,
        out_shape=jax.ShapeDtypeStruct((blocks, 8, width), f32),
        compiler_params=small(),
        cost_estimate=cost(blocks * 3072, blocks * 8192),
    )(parts)


def three_parts(values):
    first = values.astype(bf16).astype(f32)
    second = (values - first).astype(bf16).astype(f32)
    return jnp.stack([first, second, values - first - second], axis=-1)


def cost(flops, moved):
    return pl.CostEstimate(flops=flops, bytes_accessed=moved, transcendentals=0)


def small(mib=16):
    return pltpu.CompilerParams(vmem_limit_bytes=mib << 20)


def dot_last(a, b):
    return lax.dot_general(a, b, (((1,), (1,)), ((), ())), preferred_element_type=f32)


def regroup_kernel(w_ref, out_ref, stage_ref, in_sems, out_sems):
    _, pieces, rows, part = stage_ref.shape
    steps = [(g, r) for g in range(4) for r in range(pieces)]

    def copy_in(g, r):
        source = w_ref.at[pl.ds(r * rows, rows), pl.ds(g * part, part)]
        return pltpu.make_async_copy(source, stage_ref.at[g, r], in_sems.at[g, r])

    def copy_out(g, r):
        return pltpu.make_async_copy(stage_ref.at[g, r], out_ref.at[g, pl.ds(r * rows, rows)], out_sems.at[g, r])

    for step in steps:
        copy_in(*step).start()
    for step in steps:
        copy_in(*step).wait()
        copy_out(*step).start()
    for step in steps:
        copy_out(*step).wait()


def regrouped(w):
    rows, width = w.shape
    pieces = 4
    return pl.pallas_call(
        regroup_kernel,
        in_specs=[pl.BlockSpec(memory_space=pl.ANY)],
        out_specs=pl.BlockSpec(memory_space=pl.ANY),
        out_shape=jax.ShapeDtypeStruct((4, rows, width // 4), w.dtype),
        scratch_shapes=[
            pltpu.VMEM((4, pieces, rows // pieces, width // 4), w.dtype),
            pltpu.SemaphoreType.DMA((4, pieces)),
            pltpu.SemaphoreType.DMA((4, pieces)),
        ],
        cost_estimate=cost(0, 4 * rows * width),
    )(w)


def partial_kernel(near_ref, w_ref, out_ref):
    groups, inner, depth = w_ref.shape
    out = dot_last(w_ref[...].reshape(groups * inner, depth), near_ref[...]).astype(bf16)
    out_ref[...] = out.reshape(out_ref.shape)


def partial_products(near, w_mine):
    groups, inner, depth = w_mine.shape
    tokens = near.shape[0]
    return pl.pallas_call(
        partial_kernel,
        out_shape=pltpu.HBM((groups, inner, tokens), bf16),
        compiler_params=small(),
        cost_estimate=cost(2 * groups * tokens * inner * depth, 4 << 20),
    )(near, w_mine)


def over_channels(rows, height):
    heads, tokens = rows.shape
    return jnp.concatenate(
        [jnp.broadcast_to(rows[h:h + 1], (height // heads, tokens)) for h in range(heads)], axis=0
    )


def state_kernel(parts_ref, rows_ref, c_ref, ends_ref, dy_ref, sent_ref):
    total = parts_ref[0].astype(f32)
    for y in range(1, parts_ref.shape[0]):
        total = total + parts_ref[y].astype(f32)
    dy = total.astype(bf16)
    dy_ref[...] = dy
    start = over_channels(jnp.exp(rows_ref[:4]), dy.shape[0])
    decayed = (dy.astype(f32) * start).astype(bf16)
    state = jnp.dot(decayed, c_ref[...], preferred_element_type=f32)
    blocks, rows, width = ends_ref.shape
    state = state.reshape(blocks, rows, width)
    sent_ref[...] = jnp.concatenate([state, ends_ref[...]], axis=1).astype(bf16)


def local_states(parts, rows, c_in, ends):
    _, inner, tokens = parts.shape
    blocks, height, width = ends.shape
    return pl.pallas_call(
        state_kernel,
        out_shape=(pltpu.HBM((inner, tokens), bf16), pltpu.HBM((blocks, 2 * height, width), bf16)),
        compiler_params=small(),
        cost_estimate=cost(2 * tokens * inner * width, 2 << 20),
    )(parts, rows, c_in, ends)


def widened(columns, width):
    tokens, heads = columns.shape
    return jnp.concatenate(
        [jnp.broadcast_to(columns[:, h:h + 1], (tokens, width // heads)) for h in range(heads)], axis=1
    )


def head_sums(values, heads):
    width = values.shape[1] // heads
    return [jnp.sum(values[:, h * width:(h + 1) * width], axis=1, keepdims=True) for h in range(heads)]


def as_rows(columns):
    tokens = columns[0].shape[0]
    lanes = lax.broadcasted_iota(jnp.int32, (tokens, 128), 1)
    spread = jnp.zeros((tokens, 128), f32)
    for k, column in enumerate(columns):
        spread = jnp.where(lanes == k, column, spread)
    return spread.T[:8]


def intra_kernel(dy_ref, x_ref, b_ref, c_ref, states_ref, rows_ref, skip_ref, wide_ref, half_ref, part_ref):
    width, tokens = dy_ref.shape
    head_dim = width // 4
    cum = rows_ref[:4]
    columns = rows_ref[:8].T
    step = widened(columns[:, 4:], width)
    start = widened(jnp.exp(columns[:, :4]), width)
    b, c, states = b_ref[...], c_ref[...], states_ref[...]
    scores = dot_last(c, b)
    entered = dot_last(c, states)
    dy_wide = dy_ref[...].astype(f32).T
    dy = dy_wide.astype(bf16)
    x = x_ref[...].astype(f32)
    scaled = (x * step).astype(bf16)
    causal = lax.broadcasted_iota(jnp.int32, (tokens, tokens), 0) >= lax.broadcasted_iota(jnp.int32, (tokens, tokens), 1)
    total = jnp.zeros((tokens, tokens), f32)
    along, down, backs = [], [], []
    for h in range(4):
        mine = slice(h * head_dim, (h + 1) * head_dim)
        dy_h = dy[:, mine]
        gaps = jnp.minimum(columns[:, h:h + 1] - cum[h:h + 1], 0.0)
        mask = jnp.where(causal, jnp.exp(gaps), 0.0)
        weighed = (scores * mask).astype(bf16)
        backs.append(lax.dot_general(weighed, dy_h, (((0,), (0,)), ((), ())), preferred_element_type=f32))
        masked = dot_last(dy_h, scaled[:, mine]) * mask
        total = total + masked
        pairs = masked * scores
        along.append(jnp.sum(pairs, axis=1, keepdims=True))
        down.append(jnp.sum(pairs, axis=0, keepdims=True))
    total = total.astype(bf16)
    db = lax.dot_general(total, c, (((0,), (0,)), ((), ())), preferred_element_type=f32)
    dc = jnp.dot(total, b, preferred_element_type=f32)
    dc = dc + jnp.dot((dy_wide * start).astype(bf16), states, preferred_element_type=f32)
    back = jnp.concatenate(backs, axis=1)
    wide_ref[:width] = (step * back + skip_ref[...] * dy_wide).T
    wide_ref[width:] = db.T
    half_ref[:width] = x.T.astype(bf16)
    half_ref[width:] = dc.T.astype(bf16)
    entered = head_sums(start * dy_wide * entered, 4)
    rows = as_rows([a + e for a, e in zip(along, entered)] + head_sums(x * back, 4))
    part_ref[:8] = rows - jnp.concatenate(down + [jnp.zeros((4, tokens), f32)], axis=0)
    part_ref[8:] = jnp.broadcast_to(jnp.sum(dy_wide * x, axis=0, keepdims=True), (8, width))


def intra_terms(dy, x_in, b_in, c_in, states, rows, skip):
    width, tokens = dy.shape
    height = width + b_in.shape[1]
    return pl.pallas_call(
        intra_kernel,
        out_shape=(jax.ShapeDtypeStruct((height, tokens), f32), jax.ShapeDtypeStruct((height, tokens), bf16), jax.ShapeDtypeStruct((16, tokens), f32)),
        compiler_params=small(),
        cost_estimate=cost(14 * tokens * tokens * width, 2 << 20),
    )(dy, x_in, b_in, c_in, states, rows, skip)


def dt_rows(back, carried, half_ref, rows_ref, part_ref, states_ref, raw_ref, dt_ref, param_ref):
    width, tokens = back.shape
    head_dim = width // 4
    cum, step = rows_ref[:4], rows_ref[4:8]
    last = cum[:, tokens - 1:]
    rate, bias = rows_ref[8:12], rows_ref[12:]
    dots = jnp.sum((half_ref[:width].astype(f32) * back).reshape(4, head_dim, tokens), axis=1)
    end_decay = jnp.exp(last - cum)
    end_terms = step * end_decay * dots
    carried = carried.reshape(4, head_dim, -1)
    held = jnp.sum(carried * states_ref[...].astype(f32).reshape(4, head_dim, -1), axis=1)
    tail = jnp.sum(end_terms, axis=1, keepdims=True) + jnp.exp(last) * jnp.sum(held, axis=1, keepdims=True)
    below = lax.broadcasted_iota(jnp.int32, (tokens, tokens), 0) >= lax.broadcasted_iota(jnp.int32, (tokens, tokens), 1)
    step_grad = tail + jnp.dot(
        part_ref[:4] - end_terms, below.astype(f32), precision=lax.Precision.HIGHEST, preferred_element_type=f32
    )
    dt_sum = part_ref[4:8] + end_decay * dots - rate * step_grad
    dt = dt_sum * jax.nn.sigmoid(raw_ref[...] + bias)
    dt_ref[...] = dt
    lanes = lax.broadcasted_iota(jnp.int32, (4, width), 1)
    heads = lax.broadcasted_iota(jnp.int32, (4, width), 0)
    skip = jnp.sum(jnp.where(lanes // head_dim == heads, part_ref[8:9], 0.0), axis=1, keepdims=True)
    decays = jnp.sum(step_grad * (-rate * step), axis=1, keepdims=True)
    biases = jnp.sum(dt, axis=1, keepdims=True)
    lanes, heads = lanes[:, :128], heads[:, :128]
    placed = jnp.where(lanes == heads, decays, 0.0)
    placed = jnp.where(lanes == heads + 4, skip, placed)
    placed = jnp.where(lanes == heads + 8, biases, placed)
    param_ref[...] = jnp.sum(placed, axis=0, keepdims=True)


def x_grad_kernel(
    carried_ref, b_ref, wide_ref, half_ref, rows_ref, part_ref, states_ref, raw_ref, sent_ref, dt_ref, param_ref
):
    blocks, height, state_dim = carried_ref.shape
    width = blocks * height
    tokens = b_ref.shape[0]
    carried_wide = carried_ref[...].reshape(width, state_dim)
    carried = carried_wide.astype(bf16)
    back = dot_last(carried, b_ref[...])
    cum = rows_ref[:4]
    weight = over_channels(rows_ref[4:8] * jnp.exp(cum[:, tokens - 1:] - cum), width)
    x_grad = (wide_ref[:width] + weight * back).astype(bf16)
    x_end = (half_ref[:width].astype(f32) * weight).astype(bf16)
    entry = lax.dot_general(carried, x_end, (((0,), (0,)), ((), ())), preferred_element_type=f32)
    db = (wide_ref[width:] + entry).astype(bf16)
    rows = state_dim // 2
    for y in range(4):
        sent_ref[y, :width] = x_grad
        if y < 2:
            sent_ref[y, width:] = db[y * rows:(y + 1) * rows]
        else:
            sent_ref[y, width:] = half_ref[width + (y - 2) * rows:width + (y - 1) * rows]
    dt_rows(back, carried_wide, half_ref, rows_ref, part_ref, states_ref, raw_ref, dt_ref, param_ref)


def x_grads(carried, b_in, wide, half, rows, part, states, dt_raw):
    tokens, state_dim = b_in.shape
    inner = wide.shape[0] - state_dim
    return pl.pallas_call(
        x_grad_kernel,
        out_shape=(
            pltpu.HBM((4, inner + state_dim // 2, tokens), bf16),
            jax.ShapeDtypeStruct(dt_raw.shape, f32),
            jax.ShapeDtypeStruct((1, 128), f32),
        ),
        compiler_params=small(),
        cost_estimate=cost(4 * tokens * inner * 128, 2 << 20),
    )(carried, b_in, wide, half, rows, part, states, dt_raw)


def in_kernel(place_ref, got_ref, own_ref, near_ref, other_ref, half_ref, rest_ref, *out_refs):
    quarter, inner = own_ref.shape
    feats = quarter // 4
    rows = out_refs[0].shape[0] - feats
    y, core, zh = place_ref[0], place_ref[1], place_ref[2]
    sources = [y, lax.rem(y + 3 + 2 * core, 4), lax.rem(y + 5 - 2 * core, 4), lax.rem(y + 2, 4)]
    x_grad = jnp.concatenate([got_ref[source, :inner] for source in sources], axis=0)
    targets = [zh, lax.rem(zh + 1 + 2 * core, 4), lax.rem(zh + 2, 4), lax.rem(zh + 3 + 2 * core, 4)]
    for z, out_ref in zip(targets, out_refs):
        at = pl.ds(pl.multiple_of(inner + z * rows, rows), rows)
        bc = got_ref[0, at].astype(f32)
        for other in range(1, 4):
            bc = bc + got_ref[other, at].astype(f32)
        out_ref[feats:] = bc.astype(bf16)
        mine = pl.ds(pl.multiple_of(z * feats, feats), feats)
        part = pl.ds(pl.multiple_of(lax.rem(z, 2) * feats, feats), feats)
        far = jnp.where(core == z // 2, half_ref[part], rest_ref[part])
        w = jnp.concatenate([own_ref[mine], near_ref[mine], other_ref[mine], far], axis=1)
        out_ref[:feats] = jnp.dot(w, x_grad, preferred_element_type=f32).astype(bf16)


def in_products(place, got, pieces):
    quarter, inner = pieces[0].shape
    _, height, tokens = got.shape
    feats, rows = quarter // 4, (height - inner) // 4
    return pl.pallas_call(
        in_kernel,
        in_specs=[pl.BlockSpec(memory_space=pltpu.SMEM)] + [pl.BlockSpec(memory_space=pltpu.VMEM)] * 6,
        out_shape=[jax.ShapeDtypeStruct((feats + rows, tokens), bf16)] * 4,
        compiler_params=small(),
        cost_estimate=cost(8 * quarter * inner * tokens, 4 << 20),
    )(place, got, *pieces)


def sum_kernel(own_ref, chain_ref, direct_ref, in_ref, bc_ref):
    feats = in_ref.shape[0]
    total = own_ref[...].astype(f32) + chain_ref[...].astype(f32) + direct_ref[...].astype(f32)
    total = total.astype(bf16)
    in_ref[...] = total[:feats]
    bc_ref[...] = total[feats:]


def final_sums(own, chain, direct, feats):
    height, tokens = own.shape
    return pl.pallas_call(
        sum_kernel,
        out_shape=(
            jax.ShapeDtypeStruct((feats, tokens), bf16),
            jax.ShapeDtypeStruct((height - feats, tokens), bf16),
        ),
        compiler_params=small(),
        cost_estimate=cost(4 * height * tokens, 1 << 20),
    )(own, chain, direct)


def ring_step(value, axis, way):
    pairs = [(c, i, (i + (way if c == 0 else -way)) % 4) for c in range(2) for i in range(4)]
    return lax.ppermute(value, ("core", axis), [(4 * c + i, 4 * c + j) for c, i, j in pairs])


def shifted(row, axis):
    return [lax.ppermute(row, axis, [(i, (i + s) % 4) for i in range(4)]) for s in (1, 2, 3)]


def paired(row, rounds):
    first, second, third = rounds
    return (row + second) + (first + third)


def shards(out_grad, x_in, b_in, c_in, dt_raw, dt_bias, a_log, d_skip, states, w_out, w_in):
    tokens_here, inner_here = x_in.shape
    group_heads = dt_raw.shape[0]
    head_dim = inner_here // group_heads
    state_dim = b_in.shape[1]
    blocks = lax.axis_size(SEQ)
    y = lax.axis_index("y")
    entry_state = states[0]

    w_out_y = lax.all_to_all(regrouped(w_out), "y", 0, 0)
    near = lax.all_gather(out_grad, "zh", axis=1, tiled=True)
    products = partial_products(near, w_out_y)
    w_in_held, products = lax.optimization_barrier((w_in, products))
    quarter = w_in.shape[0] // 4
    core = lax.axis_index("core")
    own = lax.dynamic_slice_in_dim(w_in_held, y * quarter, quarter)
    near_piece = lax.dynamic_slice_in_dim(w_in_held, lax.rem(y + 1 + 2 * core, 4) * quarter, quarter)
    far_at = lax.rem(y + 2, 4) * quarter + core * (quarter // 2)
    far_half = lax.dynamic_slice_in_dim(w_in_held, far_at, quarter // 2)
    head_parts = lax.all_to_all(products, "y", 0, 0)

    decay_rate = jnp.exp(a_log)
    step_size = jax.nn.softplus(dt_raw + dt_bias[:, None])
    log_step = -decay_rate[:, None] * step_size
    positions = jnp.arange(tokens_here)
    upto = (positions[:, None] <= positions[None, :]).astype(f32)
    cumlog = jnp.dot(log_step, upto, precision=lax.Precision.HIGHEST)
    wide_scalars = jnp.broadcast_to(jnp.concatenate([decay_rate, dt_bias])[:, None], (2 * group_heads, tokens_here))
    rows = jnp.concatenate([cumlog, step_size, wide_scalars], axis=0)
    ends = jnp.pad(three_parts(jnp.exp(cumlog[:, -1])), ((0, 0), (0, 5)))
    ends = jnp.broadcast_to(ends[:, None, :, None], (group_heads, blocks // group_heads, 8, state_dim))
    skip = jnp.repeat(d_skip, head_dim)[None]
    own, far_half, head_parts = lax.optimization_barrier((own, far_half, head_parts))
    one_step = [((c, i), (c, (i + 1 + 2 * c) % 4)) for c in range(2) for i in range(4)]
    near_piece = lax.ppermute(near_piece, ("core", "y"), [(4 * a[0] + a[1], 4 * b[0] + b[1]) for a, b in one_step])
    far_half = lax.ppermute(far_half, "y", [(i, (i + 2) % 4) for i in range(4)])
    swap = [(0, 1), (1, 0)]
    held = [own, near_piece, lax.ppermute(near_piece, "core", swap), far_half, lax.ppermute(far_half, "core", swap)]
    dy, sent = local_states(head_parts, rows, c_in, ends.reshape(blocks, 8, state_dim))
    ahead = suffix_scan(lax.all_to_all(sent, SEQ, 0, 0))
    ahead, dy = lax.optimization_barrier((ahead, dy))
    wide, half, part = intra_terms(dy, x_in, b_in, c_in, entry_state, rows, skip)
    *held, carried = lax.optimization_barrier((*held, lax.all_to_all(ahead, SEQ, 0, 0)))
    sent_y, dt_grad, row = x_grads(carried, b_in, wide, half, rows, part, entry_state, dt_raw)
    got = lax.all_to_all(sent_y, "y", 0, 0)
    *rounds, got = lax.optimization_barrier((*shifted(row, "zl"), got))
    place = jnp.stack([y, core, lax.axis_index("zh")])
    mine, near_terms, far_terms, direct_terms = in_products(place, got, held)
    relayed = ring_step(far_terms, "zh", 1)
    relayed, direct_terms = lax.optimization_barrier((relayed, direct_terms))
    onward = (near_terms.astype(f32) + relayed.astype(f32)).astype(bf16)
    *rounds, onward = lax.optimization_barrier((*rounds, onward))
    chain = ring_step(onward, "zh", 1)
    direct = ring_step(direct_terms, "zh", -1)
    row = paired(row, rounds)
    peers = lax.axis_size(("x", "core"))
    row = lax.all_to_all(jnp.broadcast_to(row[None], (peers,) + row.shape), ("x", "core"), 0, 0).sum(axis=0)
    in_grad, bc_grad = final_sums(mine, chain, direct, w_in.shape[0] // 16)
    norm_scale = (blocks * tokens_here * head_dim) ** (-0.5)
    param_grad = row[0, : 3 * group_heads].reshape(3, group_heads) * norm_scale
    return (in_grad, bc_grad, dt_grad, param_grad)


def solution(mesh):
    fine = Mesh(mesh.devices.reshape(4, 4, 2, 4, 4), ("x", "zl", "core", "y", "zh"))
    return jax.shard_map(
        shards,
        mesh=fine,
        in_specs=(
            P(SEQ, HEAD),
            P(SEQ, HEAD),
            P(SEQ, None),
            P(SEQ, None),
            P(HEAD, SEQ),
            P(HEAD),
            P(HEAD),
            P(HEAD),
            P(SEQ, HEAD, None),
            P(HEAD, None),
            P(None, HEAD),
        ),
        out_specs=(P(HEAD, SEQ), P(HEAD, SEQ), P(HEAD, SEQ), P(None, HEAD)),
        check_vma=False,
    )
```

```python
import jax
import jax.numpy as jnp
from jax import lax
from jax.experimental import pallas as pl
from jax.experimental.pallas import tpu as pltpu
from jax.sharding import Mesh, PartitionSpec as P

SEQ = ("x", "zl", "core")
HEAD = ("y", "zh")
f32, bf16 = jnp.float32, jnp.bfloat16


def scan_kernel(parts_ref, carried_ref):
    blocks = parts_ref.shape[0]
    held = jnp.zeros(carried_ref.shape[1:], f32)
    for k in range(blocks - 1, -1, -1):
        carried_ref[k] = held
        wide = parts_ref[k].astype(f32)
        total = wide[8:9] + wide[9:10] + wide[10:11]
        held = total * held + wide[:8]


def suffix_scan(parts):
    blocks, _, width = parts.shape
    return pl.pallas_call(
        scan_kernel,
        out_shape=jax.ShapeDtypeStruct((blocks, 8, width), f32),
        compiler_params=small(),
        cost_estimate=cost(blocks * 3072, blocks * 8192),
    )(parts)


def three_parts(values):
    first = values.astype(bf16).astype(f32)
    second = (values - first).astype(bf16).astype(f32)
    return jnp.stack([first, second, values - first - second], axis=-1)


def cost(flops, moved):
    return pl.CostEstimate(flops=flops, bytes_accessed=moved, transcendentals=0)


def small(mib=16):
    return pltpu.CompilerParams(vmem_limit_bytes=mib << 20)


def dot_last(a, b):
    return lax.dot_general(a, b, (((1,), (1,)), ((), ())), preferred_element_type=f32)


def regroup_kernel(w_ref, out_ref, stage_ref, in_sems, out_sems):
    _, pieces, rows, part = stage_ref.shape
    steps = [(g, r) for g in range(4) for r in range(pieces)]

    def copy_in(g, r):
        source = w_ref.at[pl.ds(r * rows, rows), pl.ds(g * part, part)]
        return pltpu.make_async_copy(source, stage_ref.at[g, r], in_sems.at[g, r])

    def copy_out(g, r):
        return pltpu.make_async_copy(stage_ref.at[g, r], out_ref.at[g, pl.ds(r * rows, rows)], out_sems.at[g, r])

    for step in steps:
        copy_in(*step).start()
    for step in steps:
        copy_in(*step).wait()
        copy_out(*step).start()
    for step in steps:
        copy_out(*step).wait()


def regrouped(w):
    rows, width = w.shape
    pieces = 4
    return pl.pallas_call(
        regroup_kernel,
        in_specs=[pl.BlockSpec(memory_space=pl.ANY)],
        out_specs=pl.BlockSpec(memory_space=pl.ANY),
        out_shape=jax.ShapeDtypeStruct((4, rows, width // 4), w.dtype),
        scratch_shapes=[
            pltpu.VMEM((4, pieces, rows // pieces, width // 4), w.dtype),
            pltpu.SemaphoreType.DMA((4, pieces)),
            pltpu.SemaphoreType.DMA((4, pieces)),
        ],
        cost_estimate=cost(0, 4 * rows * width),
    )(w)


def partial_kernel(near_ref, w_ref, out_ref):
    groups, inner, depth = w_ref.shape
    out = dot_last(w_ref[...].reshape(groups * inner, depth), near_ref[...]).astype(bf16)
    out_ref[...] = out.reshape(out_ref.shape)


def partial_products(near, w_mine):
    groups, inner, depth = w_mine.shape
    tokens = near.shape[0]
    return pl.pallas_call(
        partial_kernel,
        out_shape=pltpu.HBM((groups, inner, tokens), bf16),
        compiler_params=small(),
        cost_estimate=cost(2 * groups * tokens * inner * depth, 4 << 20),
    )(near, w_mine)


def over_channels(rows, height):
    heads, tokens = rows.shape
    return jnp.concatenate(
        [jnp.broadcast_to(rows[h:h + 1], (height // heads, tokens)) for h in range(heads)], axis=0
    )


def state_kernel(parts_ref, rows_ref, c_ref, ends_ref, dy_ref, sent_ref):
    total = parts_ref[0].astype(f32)
    for y in range(1, parts_ref.shape[0]):
        total = total + parts_ref[y].astype(f32)
    dy = total.astype(bf16)
    dy_ref[...] = dy
    start = over_channels(jnp.exp(rows_ref[:4]), dy.shape[0])
    decayed = (dy.astype(f32) * start).astype(bf16)
    state = jnp.dot(decayed, c_ref[...], preferred_element_type=f32)
    blocks, rows, width = ends_ref.shape
    state = state.reshape(blocks, rows, width)
    sent_ref[...] = jnp.concatenate([state, ends_ref[...]], axis=1).astype(bf16)


def local_states(parts, rows, c_in, ends):
    _, inner, tokens = parts.shape
    blocks, height, width = ends.shape
    return pl.pallas_call(
        state_kernel,
        out_shape=(pltpu.HBM((inner, tokens), bf16), pltpu.HBM((blocks, 2 * height, width), bf16)),
        compiler_params=small(),
        cost_estimate=cost(2 * tokens * inner * width, 2 << 20),
    )(parts, rows, c_in, ends)


def widened(columns, width):
    tokens, heads = columns.shape
    return jnp.concatenate(
        [jnp.broadcast_to(columns[:, h:h + 1], (tokens, width // heads)) for h in range(heads)], axis=1
    )


def head_sums(values, heads):
    width = values.shape[1] // heads
    return [jnp.sum(values[:, h * width:(h + 1) * width], axis=1, keepdims=True) for h in range(heads)]


def as_rows(columns):
    tokens = columns[0].shape[0]
    lanes = lax.broadcasted_iota(jnp.int32, (tokens, 128), 1)
    spread = jnp.zeros((tokens, 128), f32)
    for k, column in enumerate(columns):
        spread = jnp.where(lanes == k, column, spread)
    return spread.T[:8]


def intra_kernel(dy_ref, x_ref, b_ref, c_ref, states_ref, rows_ref, skip_ref, wide_ref, half_ref, part_ref):
    width, tokens = dy_ref.shape
    head_dim = width // 4
    cum = rows_ref[:4]
    columns = rows_ref[:8].T
    step = widened(columns[:, 4:], width)
    start = widened(jnp.exp(columns[:, :4]), width)
    b, c, states = b_ref[...], c_ref[...], states_ref[...]
    scores = dot_last(c, b)
    entered = dot_last(c, states)
    dy_wide = dy_ref[...].astype(f32).T
    dy = dy_wide.astype(bf16)
    x = x_ref[...].astype(f32)
    scaled = (x * step).astype(bf16)
    causal = lax.broadcasted_iota(jnp.int32, (tokens, tokens), 0) >= lax.broadcasted_iota(jnp.int32, (tokens, tokens), 1)
    total = jnp.zeros((tokens, tokens), f32)
    along, down, backs = [], [], []
    for h in range(4):
        mine = slice(h * head_dim, (h + 1) * head_dim)
        dy_h = dy[:, mine]
        gaps = jnp.minimum(columns[:, h:h + 1] - cum[h:h + 1], 0.0)
        mask = jnp.where(causal, jnp.exp(gaps), 0.0)
        weighed = (scores * mask).astype(bf16)
        backs.append(lax.dot_general(weighed, dy_h, (((0,), (0,)), ((), ())), preferred_element_type=f32))
        masked = dot_last(dy_h, scaled[:, mine]) * mask
        total = total + masked
        pairs = masked * scores
        along.append(jnp.sum(pairs, axis=1, keepdims=True))
        down.append(jnp.sum(pairs, axis=0, keepdims=True))
    total = total.astype(bf16)
    db = lax.dot_general(total, c, (((0,), (0,)), ((), ())), preferred_element_type=f32)
    dc = jnp.dot(total, b, preferred_element_type=f32)
    dc = dc + jnp.dot((dy_wide * start).astype(bf16), states, preferred_element_type=f32)
    back = jnp.concatenate(backs, axis=1)
    wide_ref[:width] = (step * back + skip_ref[...] * dy_wide).T
    wide_ref[width:] = db.T
    half_ref[:width] = x.T.astype(bf16)
    half_ref[width:] = dc.T.astype(bf16)
    entered = head_sums(start * dy_wide * entered, 4)
    rows = as_rows([a + e for a, e in zip(along, entered)] + head_sums(x * back, 4))
    part_ref[:8] = rows - jnp.concatenate(down + [jnp.zeros((4, tokens), f32)], axis=0)
    part_ref[8:] = jnp.broadcast_to(jnp.sum(dy_wide * x, axis=0, keepdims=True), (8, width))


def intra_terms(dy, x_in, b_in, c_in, states, rows, skip):
    width, tokens = dy.shape
    height = width + b_in.shape[1]
    return pl.pallas_call(
        intra_kernel,
        out_shape=(jax.ShapeDtypeStruct((height, tokens), f32), jax.ShapeDtypeStruct((height, tokens), bf16), jax.ShapeDtypeStruct((16, tokens), f32)),
        compiler_params=small(),
        cost_estimate=cost(14 * tokens * tokens * width, 2 << 20),
    )(dy, x_in, b_in, c_in, states, rows, skip)


def dt_rows(back, carried, half_ref, rows_ref, part_ref, states_ref, raw_ref, dt_ref, param_ref):
    width, tokens = back.shape
    head_dim = width // 4
    cum, step = rows_ref[:4], rows_ref[4:8]
    last = cum[:, tokens - 1:]
    rate, bias = rows_ref[8:12], rows_ref[12:]
    dots = jnp.sum((half_ref[:width].astype(f32) * back).reshape(4, head_dim, tokens), axis=1)
    end_decay = jnp.exp(last - cum)
    end_terms = step * end_decay * dots
    carried = carried.reshape(4, head_dim, -1)
    held = jnp.sum(carried * states_ref[...].astype(f32).reshape(4, head_dim, -1), axis=1)
    tail = jnp.sum(end_terms, axis=1, keepdims=True) + jnp.exp(last) * jnp.sum(held, axis=1, keepdims=True)
    below = lax.broadcasted_iota(jnp.int32, (tokens, tokens), 0) >= lax.broadcasted_iota(jnp.int32, (tokens, tokens), 1)
    step_grad = tail + jnp.dot(
        part_ref[:4] - end_terms, below.astype(f32), precision=lax.Precision.HIGHEST, preferred_element_type=f32
    )
    dt_sum = part_ref[4:8] + end_decay * dots - rate * step_grad
    dt = dt_sum * jax.nn.sigmoid(raw_ref[...] + bias)
    dt_ref[...] = dt
    lanes = lax.broadcasted_iota(jnp.int32, (4, width), 1)
    heads = lax.broadcasted_iota(jnp.int32, (4, width), 0)
    skip = jnp.sum(jnp.where(lanes // head_dim == heads, part_ref[8:9], 0.0), axis=1, keepdims=True)
    decays = jnp.sum(step_grad * (-rate * step), axis=1, keepdims=True)
    biases = jnp.sum(dt, axis=1, keepdims=True)
    lanes, heads = lanes[:, :128], heads[:, :128]
    placed = jnp.where(lanes == heads, decays, 0.0)
    placed = jnp.where(lanes == heads + 4, skip, placed)
    placed = jnp.where(lanes == heads + 8, biases, placed)
    param_ref[...] = jnp.sum(placed, axis=0, keepdims=True)


def x_grad_kernel(
    carried_ref, b_ref, wide_ref, half_ref, rows_ref, part_ref, states_ref, raw_ref, sent_ref, dt_ref, param_ref
):
    blocks, height, state_dim = carried_ref.shape
    width = blocks * height
    tokens = b_ref.shape[0]
    carried_wide = carried_ref[...].reshape(width, state_dim)
    carried = carried_wide.astype(bf16)
    back = dot_last(carried, b_ref[...])
    cum = rows_ref[:4]
    weight = over_channels(rows_ref[4:8] * jnp.exp(cum[:, tokens - 1:] - cum), width)
    x_grad = (wide_ref[:width] + weight * back).astype(bf16)
    x_end = (half_ref[:width].astype(f32) * weight).astype(bf16)
    entry = lax.dot_general(carried, x_end, (((0,), (0,)), ((), ())), preferred_element_type=f32)
    db = (wide_ref[width:] + entry).astype(bf16)
    rows = state_dim // 2
    for y in range(4):
        sent_ref[y, :width] = x_grad
        if y < 2:
            sent_ref[y, width:] = db[y * rows:(y + 1) * rows]
        else:
            sent_ref[y, width:] = half_ref[width + (y - 2) * rows:width + (y - 1) * rows]
    dt_rows(back, carried_wide, half_ref, rows_ref, part_ref, states_ref, raw_ref, dt_ref, param_ref)


def x_grads(carried, b_in, wide, half, rows, part, states, dt_raw):
    tokens, state_dim = b_in.shape
    inner = wide.shape[0] - state_dim
    return pl.pallas_call(
        x_grad_kernel,
        out_shape=(
            pltpu.HBM((4, inner + state_dim // 2, tokens), bf16),
            jax.ShapeDtypeStruct(dt_raw.shape, f32),
            jax.ShapeDtypeStruct((1, 128), f32),
        ),
        compiler_params=small(),
        cost_estimate=cost(4 * tokens * inner * 128, 2 << 20),
    )(carried, b_in, wide, half, rows, part, states, dt_raw)


def in_kernel(place_ref, got_ref, own_ref, near_ref, other_ref, half_ref, rest_ref, *out_refs):
    quarter, inner = own_ref.shape
    feats = quarter // 4
    rows = out_refs[0].shape[0] - feats
    y, core, zh = place_ref[0], place_ref[1], place_ref[2]
    sources = [y, lax.rem(y + 3 + 2 * core, 4), lax.rem(y + 5 - 2 * core, 4), lax.rem(y + 2, 4)]
    x_grad = jnp.concatenate([got_ref[source, :inner] for source in sources], axis=0)
    targets = [zh, lax.rem(zh + 1 + 2 * core, 4), lax.rem(zh + 2, 4), lax.rem(zh + 3 + 2 * core, 4)]
    for z, out_ref in zip(targets, out_refs):
        at = pl.ds(pl.multiple_of(inner + z * rows, rows), rows)
        bc = got_ref[0, at].astype(f32)
        for other in range(1, 4):
            bc = bc + got_ref[other, at].astype(f32)
        out_ref[feats:] = bc.astype(bf16)
        mine = pl.ds(pl.multiple_of(z * feats, feats), feats)
        part = pl.ds(pl.multiple_of(lax.rem(z, 2) * feats, feats), feats)
        far = jnp.where(core == z // 2, half_ref[part], rest_ref[part])
        w = jnp.concatenate([own_ref[mine], near_ref[mine], other_ref[mine], far], axis=1)
        out_ref[:feats] = jnp.dot(w, x_grad, preferred_element_type=f32).astype(bf16)


def in_products(place, got, pieces):
    quarter, inner = pieces[0].shape
    _, height, tokens = got.shape
    feats, rows = quarter // 4, (height - inner) // 4
    return pl.pallas_call(
        in_kernel,
        in_specs=[pl.BlockSpec(memory_space=pltpu.SMEM)] + [pl.BlockSpec(memory_space=pltpu.VMEM)] * 6,
        out_shape=[jax.ShapeDtypeStruct((feats + rows, tokens), bf16)] * 4,
        compiler_params=small(),
        cost_estimate=cost(8 * quarter * inner * tokens, 4 << 20),
    )(place, got, *pieces)


def sum_kernel(own_ref, chain_ref, direct_ref, in_ref, bc_ref):
    feats = in_ref.shape[0]
    total = own_ref[...].astype(f32) + chain_ref[...].astype(f32) + direct_ref[...].astype(f32)
    total = total.astype(bf16)
    in_ref[...] = total[:feats]
    bc_ref[...] = total[feats:]


def final_sums(own, chain, direct, feats):
    height, tokens = own.shape
    return pl.pallas_call(
        sum_kernel,
        out_shape=(
            jax.ShapeDtypeStruct((feats, tokens), bf16),
            jax.ShapeDtypeStruct((height - feats, tokens), bf16),
        ),
        compiler_params=small(),
        cost_estimate=cost(4 * height * tokens, 1 << 20),
    )(own, chain, direct)


def ring_step(value, axis, way):
    pairs = [(c, i, (i + (way if c == 0 else -way)) % 4) for c in range(2) for i in range(4)]
    return lax.ppermute(value, ("core", axis), [(4 * c + i, 4 * c + j) for c, i, j in pairs])


def shifted(row, axis):
    return [lax.ppermute(row, axis, [(i, (i + s) % 4) for i in range(4)]) for s in (1, 2, 3)]


def paired(row, rounds):
    first, second, third = rounds
    return (row + second) + (first + third)


def shards(out_grad, x_in, b_in, c_in, dt_raw, dt_bias, a_log, d_skip, states, w_out, w_in):
    tokens_here, inner_here = x_in.shape
    group_heads = dt_raw.shape[0]
    head_dim = inner_here // group_heads
    state_dim = b_in.shape[1]
    blocks = lax.axis_size(SEQ)
    y = lax.axis_index("y")
    entry_state = states[0]

    w_out_y = lax.all_to_all(regrouped(w_out), "y", 0, 0)
    near = lax.all_gather(out_grad, "zh", axis=1, tiled=True)
    products = partial_products(near, w_out_y)
    w_in_held, products = lax.optimization_barrier((w_in, products))
    quarter = w_in.shape[0] // 4
    core = lax.axis_index("core")
    own = lax.dynamic_slice_in_dim(w_in_held, y * quarter, quarter)
    near_piece = lax.dynamic_slice_in_dim(w_in_held, lax.rem(y + 1 + 2 * core, 4) * quarter, quarter)
    far_at = lax.rem(y + 2, 4) * quarter + core * (quarter // 2)
    far_half = lax.dynamic_slice_in_dim(w_in_held, far_at, quarter // 2)
    head_parts = lax.all_to_all(products, "y", 0, 0)

    decay_rate = jnp.exp(a_log)
    step_size = jax.nn.softplus(dt_raw + dt_bias[:, None])
    log_step = -decay_rate[:, None] * step_size
    positions = jnp.arange(tokens_here)
    upto = (positions[:, None] <= positions[None, :]).astype(f32)
    cumlog = jnp.dot(log_step, upto, precision=lax.Precision.HIGHEST)
    wide_scalars = jnp.broadcast_to(jnp.concatenate([decay_rate, dt_bias])[:, None], (2 * group_heads, tokens_here))
    rows = jnp.concatenate([cumlog, step_size, wide_scalars], axis=0)
    ends = jnp.pad(three_parts(jnp.exp(cumlog[:, -1])), ((0, 0), (0, 5)))
    ends = jnp.broadcast_to(ends[:, None, :, None], (group_heads, blocks // group_heads, 8, state_dim))
    skip = jnp.repeat(d_skip, head_dim)[None]
    own, far_half, head_parts = lax.optimization_barrier((own, far_half, head_parts))
    one_step = [((c, i), (c, (i + 1 + 2 * c) % 4)) for c in range(2) for i in range(4)]
    near_piece = lax.ppermute(near_piece, ("core", "y"), [(4 * a[0] + a[1], 4 * b[0] + b[1]) for a, b in one_step])
    far_half = lax.ppermute(far_half, "y", [(i, (i + 2) % 4) for i in range(4)])
    swap = [(0, 1), (1, 0)]
    held = [own, near_piece, lax.ppermute(near_piece, "core", swap), far_half, lax.ppermute(far_half, "core", swap)]
    dy, sent = local_states(head_parts, rows, c_in, ends.reshape(blocks, 8, state_dim))
    ahead = suffix_scan(lax.all_to_all(sent, SEQ, 0, 0))
    ahead, dy = lax.optimization_barrier((ahead, dy))
    wide, half, part = intra_terms(dy, x_in, b_in, c_in, entry_state, rows, skip)
    *held, carried = lax.optimization_barrier((*held, lax.all_to_all(ahead, SEQ, 0, 0)))
    sent_y, dt_grad, row = x_grads(carried, b_in, wide, half, rows, part, entry_state, dt_raw)
    got = lax.all_to_all(sent_y, "y", 0, 0)
    *rounds, got = lax.optimization_barrier((*shifted(row, "zl"), got))
    place = jnp.stack([y, core, lax.axis_index("zh")])
    mine, near_terms, far_terms, direct_terms = in_products(place, got, held)
    relayed = ring_step(far_terms, "zh", 1)
    row = paired(row, rounds)
    peers = lax.axis_size(("x", "core"))
    spread = lax.all_to_all(jnp.broadcast_to(row[None], (peers,) + row.shape), ("x", "core"), 0, 0)
    relayed, direct_terms, spread = lax.optimization_barrier((relayed, direct_terms, spread))
    onward = (near_terms.astype(f32) + relayed.astype(f32)).astype(bf16)
    chain = ring_step(onward, "zh", 1)
    direct = ring_step(direct_terms, "zh", -1)
    row = spread.sum(axis=0)
    in_grad, bc_grad = final_sums(mine, chain, direct, w_in.shape[0] // 16)
    norm_scale = (blocks * tokens_here * head_dim) ** (-0.5)
    param_grad = row[0, : 3 * group_heads].reshape(3, group_heads) * norm_scale
    return (in_grad, bc_grad, dt_grad, param_grad)


def solution(mesh):
    fine = Mesh(mesh.devices.reshape(4, 4, 2, 4, 4), ("x", "zl", "core", "y", "zh"))
    return jax.shard_map(
        shards,
        mesh=fine,
        in_specs=(
            P(SEQ, HEAD),
            P(SEQ, HEAD),
            P(SEQ, None),
            P(SEQ, None),
            P(HEAD, SEQ),
            P(HEAD),
            P(HEAD),
            P(HEAD),
            P(SEQ, HEAD, None),
            P(HEAD, None),
            P(None, HEAD),
        ),
        out_specs=(P(HEAD, SEQ), P(HEAD, SEQ), P(HEAD, SEQ), P(None, HEAD)),
        check_vma=False,
    )
```
